256 devices in a mesh: seq: 8 (over y_lo, x), head: 32 (over z, y_hi, core).
Axes of the slice: x: 4, y: 4 (y_hi: 2, y_lo: 2; y = y_hi * 2 + y_lo), z: 8, core: 2. Of those that a mesh axis runs over, the one named last changes fastest.
Arguments:
- queries: bfloat16 [32, 128, 576], P(None, 'head')
- prompt_latent: bfloat16 [4, 32768, 576], P(None, ('seq', 'head'))
- pool_latent: bfloat16 [512, 64, 576], P(('seq', 'head')), may hold values from -6 to 6
- value_up: bfloat16 [128, 512, 128], P('head'), may hold values from -0.70703125 to 0.70703125
- parents: int32 [32], replicated, may hold values from 0 to 31, as said below
- page_lists: int32 [32, 64], replicated, may hold values from 0 to 511, as said below
- lengths: int32 [32], replicated, may hold values from 2049 to 4096, as said below
Outputs:
- attended: bfloat16 [32, 128, 128], P(None, 'head')
The draws below stay inside these ranges and needn't reach their ends.
Inputs may be any that keep to these rules, and one draw needn't show every extreme that they name: parents[b] is a beam of the same request: 8 * (b // 8) <= parents[b] < 8 * (b // 8 + 1). `page_lists`: each row holds 64 distinct page numbers; the first 32 of them are the same for all beams of one request. `lengths`: the first beam of each request has 4096 suffix positions.
All inputs are finite; a program needn't handle non-finite values.
Results may differ from the reference program's by a relative error of at most 0.01.
Values may be sent and summed in bfloat16 or wider, within the bound.
A program may use at most 128 MiB of HBM per device.

```python
import jax
import jax.numpy as jnp
from jax import lax

HEADS = 128
LAT = 512
ROPE = 64
VDIM = 128
REQS = 4
BEAM = 8
PAGE = 64
MAXP = 64
BEAMS = 32
PROMPT = 32768
POOL = 512


def prompt_values(key, spread):
    width = LAT + ROPE
    base = jnp.clip(jax.random.normal(jax.random.fold_in(key, 11), (REQS, PROMPT, width), jnp.float32), -6.0, 6.0)
    noise = jnp.clip(jax.random.normal(jax.random.fold_in(key, 12), (REQS, width), jnp.float32), -6.0, 6.0)
    token_scale = jnp.exp(jax.random.uniform(jax.random.fold_in(key, 13), (REQS, PROMPT, 1), jnp.float32, -spread, spread))
    positions = jnp.arange(PROMPT)[None, :, None]
    token_scale = jnp.where(positions >= PROMPT - 2, 1.0, token_scale)
    values = base * token_scale
    twin = base[:, PROMPT - 1, :] + 0.5 * noise
    return values.at[:, PROMPT - 2, :].set(twin)


def draw_prompt_latent(key, part):
    values = prompt_values(key, 0.0)
    return values.astype(jnp.bfloat16)


def draw_queries(key, part):
    key = jax.random.fold_in(key, 5)
    width = LAT + ROPE
    drawn = 1.2 * jnp.clip(jax.random.normal(jax.random.fold_in(key, 1), (BEAMS, HEADS, width), jnp.float32), -6.0, 6.0)
    return drawn.astype(jnp.bfloat16)


def draw_parents(key, part):
    key = jax.random.fold_in(key, 21)
    offsets = jax.random.randint(key, (BEAMS,), 0, BEAM)
    return (jnp.arange(BEAMS) // BEAM * BEAM + offsets).astype(jnp.int32)


def draw_page_lists(key, part):
    key = jax.random.fold_in(key, 31)
    half = MAXP // 2
    request_keys = jax.random.split(key, REQS)
    orders = jax.vmap(lambda one_key: jax.random.permutation(one_key, POOL))(request_keys)
    beams = jnp.arange(BEAMS)
    request = beams // BEAM
    within = beams % BEAM
    shared_slots = jnp.broadcast_to(jnp.arange(half)[None, :], (BEAMS, half))
    own_slots = half + (within[:, None] * half + jnp.arange(half)[None, :]) % (POOL - half)
    slots = jnp.concatenate([shared_slots, own_slots], axis=1)
    return jnp.take_along_axis(orders[request], slots, axis=1).astype(jnp.int32)


def draw_lengths(key, part):
    key = jax.random.fold_in(key, 41)
    most = MAXP * PAGE
    values = jax.random.randint(key, (BEAMS,), most // 2 + 1, most + 1)
    return jnp.where(jnp.arange(BEAMS) % BEAM == 0, most, values).astype(jnp.int32)


def shard_levels(key, dims, shards, smallest, top_value):
    factor_of = 1.0
    for dim, blocks in shards:
        draws = jax.random.uniform(jax.random.fold_in(jax.random.fold_in(key, 6), dim), (blocks,), jnp.float32, smallest / len(shards), top_value / len(shards))
        factor_of = factor_of * jnp.repeat(jnp.exp(draws), dims[dim] // blocks).reshape((-1,) + (1,) * (len(dims) - 1 - dim))
    return factor_of


def bell_draw(rng, extent, scale, bound, pieces=(), kind=jnp.bfloat16):
    array = scale * jax.random.normal(rng, extent, jnp.float32)
    if pieces:
        array = array * shard_levels(rng, extent, pieces, -0.22, 0.18)
    return jnp.clip(array, -bound, bound).astype(kind)


def setup_inputs(seed: int = 0) -> dict:
    seeds = jax.random.split(jax.random.key(seed), 8)
    queries = draw_queries(jax.random.fold_in(seeds[7], 71), 0)
    prompt_latent = draw_prompt_latent(jax.random.fold_in(seeds[7], 71), 0)
    pool_latent = bell_draw(seeds[2], (POOL, PAGE, LAT + ROPE), 1.0, 6.0, ((0, 256),))
    value_up = bell_draw(seeds[3], (HEADS, LAT, VDIM), (4.0 / LAT ** 0.5), 0.70703125, ((0, 32),))
    parents = draw_parents(jax.random.fold_in(seeds[7], 71), 0)
    page_lists = draw_page_lists(jax.random.fold_in(seeds[7], 71), 0)
    lengths = draw_lengths(jax.random.fold_in(seeds[7], 71), 0)
    return dict(queries=queries, prompt_latent=prompt_latent, pool_latent=pool_latent, value_up=value_up, parents=parents, page_lists=page_lists, lengths=lengths)


masked_floor = -1e30


def live_lengths(chosen_pages, chosen_lengths, page_ids):
    slots = jnp.arange(chosen_pages.shape[1], dtype=jnp.int32)
    room = jnp.clip(chosen_lengths[:, None] - slots[None, :] * PAGE, 0, PAGE)
    match = chosen_pages[:, :, None] == page_ids[None, None, :]
    return jnp.sum(jnp.where(match, room[:, :, None], 0), axis=1).astype(jnp.int32)


def token_mask(live):
    positions = jnp.arange(PAGE, dtype=jnp.int32)
    return (positions[None, None, :] < live[:, :, None]).reshape(live.shape[0], -1)


def reference(queries, prompt_latent, pool_latent, value_up, parents, page_lists, lengths):
    beams = jnp.arange(BEAMS, dtype=jnp.int32)
    picked = parents[:, None] == beams[None, :]
    chosen_pages = jnp.sum(jnp.where(picked[:, :, None], page_lists[None, :, :], 0), axis=1).astype(jnp.int32)
    chosen_lengths = jnp.sum(jnp.where(picked, lengths[None, :], 0), axis=1).astype(jnp.int32)
    live = live_lengths(chosen_pages, chosen_lengths, jnp.arange(POOL, dtype=jnp.int32))
    suffix_valid = token_mask(live)
    prompt_wide = prompt_latent.astype(jnp.float32)
    pool_wide = pool_latent.reshape(POOL * PAGE, LAT + ROPE).astype(jnp.float32)
    value_wide = value_up.astype(jnp.float32)
    scale_factor = (VDIM + ROPE) ** -0.5

    def one_beam(items):
        beam, query, pool_valid = items
        request = (beam // BEAM).astype(jnp.int32)
        prompt_rows = lax.dynamic_index_in_dim(prompt_wide, request, 0, keepdims=False)
        keys = jnp.concatenate([prompt_rows, pool_wide], axis=0)
        valid = jnp.concatenate([jnp.ones((PROMPT,), dtype=bool), pool_valid])
        scores = jnp.dot(query.astype(jnp.float32), keys.T, preferred_element_type=jnp.float32) * scale_factor
        masked = jnp.where(valid[None, :], scores, masked_floor)
        peak = jnp.max(masked, axis=1, keepdims=True)
        weights = jnp.where(valid[None, :], jnp.exp(masked - peak), 0.0)
        sums = jnp.sum(weights, axis=1, keepdims=True)
        rounded = lax.optimization_barrier(weights.astype(jnp.bfloat16)).astype(jnp.float32)
        latent_out = jnp.dot(rounded, keys[:, :LAT], preferred_element_type=jnp.float32) / sums
        latent_out = lax.optimization_barrier(latent_out.astype(jnp.bfloat16)).astype(jnp.float32)
        attended = jnp.einsum("hl,hlv->hv", latent_out, value_wide)
        return attended.astype(jnp.bfloat16)

    return lax.map(one_beam, (beams, queries, suffix_valid))
```

```python
import jax
import jax.numpy as jnp
from jax import lax
from jax.experimental import pallas as pl
from jax.experimental.pallas import tpu as pltpu
from jax.sharding import PartitionSpec as P

LAT = 512
ROPE = 64
WIDTH = LAT + ROPE
VDIM = 128
BEAM = 8
PAGE = 64
MAXP = 64
NZ = 8
PACK = LAT + 128
KEYS = 128
LOG2E = 1.4426950408889634
RATE = (VDIM + ROPE) ** -0.5 * LOG2E
MESH = pl.DeviceIdType.MESH
F32 = jnp.float32
BF16 = jnp.bfloat16


def place(x, y, z, c):
    return ((y % 2) * 4 + x, z * 4 + (y // 2) * 2 + c)


def split3(value):
    first = value.astype(BF16).astype(F32)
    rest = value - first
    second = rest.astype(BF16).astype(F32)
    return first, second, rest - second


def pack_stats(peak, total):
    rows = peak.shape[0]
    lane = lax.broadcasted_iota(jnp.int32, (rows, 128), 1)
    out = jnp.zeros((rows, 128), F32)
    for i, term in enumerate((*split3(peak), *split3(total))):
        out = jnp.where(lane == i, term, out)
    return out.astype(BF16)


def unpack_stats(stats):
    stats = stats.astype(F32)
    peak = stats[:, 0:1] + stats[:, 1:2] + stats[:, 2:3]
    total = stats[:, 3:4] + stats[:, 4:5] + stats[:, 5:6]
    return peak, total


def merge(parts):
    stats = [unpack_stats(part[:, LAT:]) for part in parts]
    peak = stats[0][0]
    for other, _ in stats[1:]:
        peak = jnp.maximum(peak, other)
    total = jnp.zeros_like(peak)
    latent = jnp.zeros((peak.shape[0], LAT), F32)
    for part, (part_peak, part_total) in zip(parts, stats):
        keep = jnp.exp2((part_peak - peak) * RATE)
        total = total + part_total * keep
        latent = latent + part[:, :LAT].astype(F32) * keep
    return peak, total, latent


def kernel(
    parents, lengths, page_lists, queries, prompt, pool, value_up,
    out,
    q_buf, k_prompt, k_pool, v_buf, lists, room, cap, scores, probs,
    part, rs1, rs2_src, rs2, out_src,
    local_sem, key_send, key_recv, core_send, core_recv, swap_send, swap_recv, q_send, q_recv,
    rs1_send, rs1_recv, rs2_send, rs2_recv, out_send, out_recv,
):
    seq = lax.axis_index("seq")
    head = lax.axis_index("head")
    x = seq % 4
    y_lo = seq // 4
    c = head % 2
    y_hi = (head // 2) % 2
    z = head // 4
    y = y_hi * 2 + y_lo
    x_hi = x // 2
    x_lo = x % 2
    step = 1 - 2 * c
    request = x_lo * 2 + y_lo

    def shifted(dx, dy, sign=1):
        return place((x + sign * dx + 4) % 4, (y + sign * dy + 4) % 4, z, c)

    other_core = place(x, y, z, 1 - c)
    mirror = place(x, 3 - y, z, c)
    key_moves = ((1, 0), (0, 1), (1, 1))
    scatter_moves = ((2, 0), (0, 2), (2, 2))
    out_moves = [(dx, dy) for dy in range(2) for dx in range(4) if (dx, dy) != (0, 0)]

    def out_place(dx, dy):
        return place((x + dx) % 4, y_hi * 2 + (y_lo + dy) % 2, z, c)

    def out_source(dx, dy):
        return place((x - dx + 4) % 4, y_hi * 2 + (y_lo + dy) % 2, z, c)

    barrier = pltpu.get_barrier_semaphore()
    senders = [shifted(dx * step, dy * step, -1) for dx, dy in key_moves]
    senders += [other_core, mirror]
    senders += [place(x, y, (z + dz) % NZ, c) for dz in range(1, NZ)]
    senders += [shifted(dx, dy) for dx, dy in scatter_moves]
    senders += [out_source(dx, dy) for dx, dy in out_moves]
    for sender in senders:
        pl.semaphore_signal(barrier, inc=1, device_id=sender, device_id_type=MESH)

    own_q = pltpu.make_async_copy(queries.at[request], q_buf.at[y_hi, :, z], local_sem.at[0])
    own_prompt = pltpu.make_async_copy(prompt.at[request], k_prompt.at[c, 0], local_sem.at[1])
    own_pool = pltpu.make_async_copy(pool, k_pool.at[c, 0], local_sem.at[2])
    own_v = pltpu.make_async_copy(value_up, v_buf, local_sem.at[3])
    for copy in (own_q, own_prompt, own_pool, own_v):
        copy.start()

    slot = lax.broadcasted_iota(jnp.int32, (4, MAXP), 1)
    for b in range(BEAM):
        parent = parents[request * BEAM + b]
        lists[4 * b : 4 * b + 4, :] = jnp.broadcast_to(page_lists[pl.ds(parent, 1), :], (4, MAXP))
        room[4 * b : 4 * b + 4, :] = jnp.clip(lengths[parent] - slot * PAGE, 0, PAGE)
    chosen = lists[...]
    space = room[...]
    lane = lax.broadcasted_iota(jnp.int32, (4 * BEAM, KEYS), 1)
    for cc in range(2):
        sign = 1 - 2 * cc
        for kind, (dx, dy) in enumerate(((0, 0),) + key_moves):
            sy = (y - sign * dy + 4) % 4
            s_seq, s_head = place((x - sign * dx + 4) % 4, sy, z, cc)
            page = (s_seq * 32 + s_head) * 2
            live = [
                jnp.sum(jnp.where(chosen == page + i, space, 0), axis=1, keepdims=True) for i in range(2)
            ]
            seen = lane < jnp.where(lane < PAGE, live[0], live[1] + PAGE)
            cap[:, (cc * 4 + kind) * KEYS : (cc * 4 + kind + 1) * KEYS] = jnp.where(seen, jnp.inf, -jnp.inf)

    pl.semaphore_wait(barrier, len(senders))

    copies = []

    def send(src, dst, send_sem, recv_sem, target):
        copy = pltpu.make_async_remote_copy(
            src_ref=src, dst_ref=dst, send_sem=send_sem, recv_sem=recv_sem, device_id=target, device_id_type=MESH
        )
        copy.start()
        copies.append(copy)
        return copy

    mirror_request = x_lo * 2 + 1 - y_lo
    swap = send(queries.at[mirror_request], q_buf.at[y_hi, :, z], swap_send, swap_recv, mirror)
    q_copies = {}
    z_order = (4, 3, 5, 2, 6, 1, 7)
    for dz in z_order:
        q_copies[0, dz] = send(
            queries.at[request], q_buf.at[y_hi, :, z], q_send.at[0, dz], q_recv.at[0, dz],
            place(x, y, (z + dz) % NZ, c),
        )
    key_copies = []
    for i, (dx, dy) in enumerate(key_moves):
        target_request = (x_lo + dx) % 2 * 2 + (y_lo + dy) % 2
        target = shifted(dx * step, dy * step)
        key_copies.append((
            send(prompt.at[target_request], k_prompt.at[c, i + 1], key_send.at[i, 0], key_recv.at[i, 0], target),
            send(pool, k_pool.at[c, i + 1], key_send.at[i, 1], key_recv.at[i, 1], target),
        ))
    core_copies = []

    def to_core(kind, prompt_src, pool_src):
        core_copies.append(send(
            prompt_src, k_prompt.at[c, kind], core_send.at[kind, 0], core_recv.at[kind, 0], other_core))
        core_copies.append(send(
            pool_src, k_pool.at[c, kind], core_send.at[kind, 1], core_recv.at[kind, 1], other_core))

    to_core(0, prompt.at[request], pool)

    swap.wait_recv()
    for dz in z_order:
        q_copies[1, dz] = send(
            q_buf.at[1 - y_hi, :, z], q_buf.at[1 - y_hi, :, z], q_send.at[1, dz], q_recv.at[1, dz],
            place(x, y, (z + dz) % NZ, c),
        )
    for i, (prompt_copy, pool_copy) in enumerate(key_copies):
        prompt_copy.wait_recv()
        pool_copy.wait_recv()
        to_core(i + 1, k_prompt.at[c, i + 1], k_pool.at[c, i + 1])
    own_q.wait()
    own_prompt.wait()
    own_pool.wait()
    for copy in core_copies:
        copy.wait_recv()

    rs1_copies = []

    def attend(group):
        rows = q_buf[group].reshape(2 * KEYS, WIDTH)
        scores[:, : 8 * KEYS] = lax.dot_general(
            rows, k_prompt[...].reshape(8 * KEYS, WIDTH), (((1,), (1,)), ((), ())), preferred_element_type=F32)
        raw = lax.dot_general(
            rows, k_pool[...].reshape(8 * KEYS, WIDTH), (((1,), (1,)), ((), ())), preferred_element_type=F32)
        limit = cap[...].reshape(2, 1, 16, 8 * KEYS)
        raw = jnp.minimum(raw.reshape(2, NZ, 16, 8 * KEYS), limit).reshape(2 * KEYS, 8 * KEYS)
        scores[:, 8 * KEYS :] = raw
        peak = jnp.max(scores[...], axis=1, keepdims=True)
        weights = jnp.exp2((scores[...] - peak) * RATE)
        total = jnp.sum(weights, axis=1, keepdims=True)
        probs[...] = weights.astype(BF16)
        latent = jnp.dot(
            probs[:, : 8 * KEYS], k_prompt[...].reshape(8 * KEYS, WIDTH)[:, :LAT], preferred_element_type=F32)
        latent += jnp.dot(
            probs[:, 8 * KEYS :], k_pool[...].reshape(8 * KEYS, WIDTH)[:, :LAT], preferred_element_type=F32)
        part[group, :, :, :LAT] = latent.astype(BF16).reshape(2, KEYS, LAT)
        part[group, :, :, LAT:] = pack_stats(peak, total).reshape(2, KEYS, 128)

    def scatter(i, group, half):
        dx, dy = scatter_moves[i]
        rs1_copies.append(send(
            part.at[group, half], rs1.at[i], rs1_send.at[i], rs1_recv.at[i], shifted(dx, dy)))

    for dz in z_order:
        q_copies[0, dz].wait_recv()
    attend(y_hi)
    scatter(0, y_hi, 1 - x_hi)
    for dz in z_order:
        q_copies[1, dz].wait_recv()
    attend(1 - y_hi)
    scatter(2, 1 - y_hi, 1 - x_hi)
    scatter(1, 1 - y_hi, x_hi)

    for copy in rs1_copies:
        copy.wait_recv()
    peak, total, latent = merge([part[y_hi, x_hi], rs1[0], rs1[1], rs1[2]])
    rs2_src[:, :, :LAT] = latent.astype(BF16).reshape(NZ, 16, LAT)
    rs2_src[:, :, LAT:] = pack_stats(peak, total).reshape(NZ, 16, 128)
    rs2_copies = []
    for dz in z_order:
        target_z = (z + dz) % NZ
        rs2_copies.append(send(
            rs2_src.at[target_z], rs2.at[dz], rs2_send.at[dz], rs2_recv.at[dz], place(x, y, target_z, c)))
    rs2[0] = rs2_src[z]
    own_v.wait()
    for copy in rs2_copies:
        copy.wait_recv()
    peak, total, latent = merge([rs2[i] for i in range(NZ)])
    latent = (latent / total).astype(BF16)
    row = lax.broadcasted_iota(jnp.int32, (16, VDIM), 0) % 4
    attended = jnp.zeros((16, VDIM), F32)
    for h in range(4):
        product = jnp.dot(latent, v_buf[h], preferred_element_type=F32)
        attended = jnp.where(row == h, product, attended)
    out_src[...] = attended.astype(BF16)
    place_out = request * 2 + x_hi
    out_copies = []
    for i, (dx, dy) in enumerate(out_moves):
        out_copies.append(send(
            out_src, out.at[place_out], out_send.at[i], out_recv.at[i], out_place(dx, dy)))
    out[place_out] = out_src[...]
    for copy in out_copies:
        copy.wait_recv()
    for copy in copies:
        copy.wait_send()


def body(queries, prompt_latent, pool_latent, value_up, parents, page_lists, lengths):
    vmem = pl.BlockSpec(memory_space=pltpu.VMEM)
    smem = pl.BlockSpec(memory_space=pltpu.SMEM)
    hbm = pl.BlockSpec(memory_space=pl.ANY)
    dma = pltpu.SemaphoreType.DMA
    result = pl.pallas_call(
        kernel,
        out_shape=jax.ShapeDtypeStruct((8, 16, VDIM), BF16),
        in_specs=[smem, smem, vmem, hbm, hbm, hbm, hbm],
        out_specs=vmem,
        scratch_shapes=[
            pltpu.VMEM((2, 2, NZ, 16, WIDTH), BF16),
            pltpu.VMEM((2, 4, KEYS, WIDTH), BF16),
            pltpu.VMEM((2, 4, 2, PAGE, WIDTH), BF16),
            pltpu.VMEM((4, LAT, VDIM), BF16),
            pltpu.VMEM((4 * BEAM, MAXP), jnp.int32),
            pltpu.VMEM((4 * BEAM, MAXP), jnp.int32),
            pltpu.VMEM((4 * BEAM, 8 * KEYS), F32),
            pltpu.VMEM((2 * KEYS, 16 * KEYS), F32),
            pltpu.VMEM((2 * KEYS, 16 * KEYS), BF16),
            pltpu.VMEM((2, 2, KEYS, PACK), BF16),
            pltpu.VMEM((3, KEYS, PACK), BF16),
            pltpu.VMEM((NZ, 16, PACK), BF16),
            pltpu.VMEM((NZ, 16, PACK), BF16),
            pltpu.VMEM((16, VDIM), BF16),
            dma((4,)), dma((3, 2)), dma((3, 2)), dma((4, 2)), dma((4, 2)), dma, dma, dma((2, NZ)), dma((2, NZ)),
            dma((3,)), dma((3,)), dma((NZ,)), dma((NZ,)), dma((7,)), dma((7,)),
        ],
        compiler_params=pltpu.CompilerParams(
            collective_id=0, has_side_effects=True, vmem_limit_bytes=48 * 2**20
        ),
    )(
        parents, lengths, page_lists, queries.reshape(4, 2, 16, WIDTH), prompt_latent, pool_latent, value_up
    )
    return result.reshape(32, 4, VDIM)


def solution(mesh):
    return jax.shard_map(
        body,
        mesh=mesh,
        in_specs=(
            P(None, "head", None),
            P(None, ("seq", "head"), None),
            P(("seq", "head"), None, None),
            P("head", None, None),
            P(),
            P(),
            P(),
        ),
        out_specs=P(None, "head", None),
        check_vma=False,
    )
```

```python
import jax
import jax.numpy as jnp
from jax import lax
from jax.experimental import pallas as pl
from jax.experimental.pallas import tpu as pltpu
from jax.sharding import PartitionSpec as P

LAT = 512
ROPE = 64
WIDTH = LAT + ROPE
VDIM = 128
BEAM = 8
PAGE = 64
MAXP = 64
NZ = 8
PACK = LAT + 128
KEYS = 128
LOG2E = 1.4426950408889634
RATE = (VDIM + ROPE) ** -0.5 * LOG2E
MESH = pl.DeviceIdType.MESH
F32 = jnp.float32
BF16 = jnp.bfloat16


def place(x, y, z, c):
    return ((y % 2) * 4 + x, z * 4 + (y // 2) * 2 + c)


def split3(value):
    first = value.astype(BF16).astype(F32)
    rest = value - first
    second = rest.astype(BF16).astype(F32)
    return first, second, rest - second


def pack_stats(peak, total):
    rows = peak.shape[0]
    lane = lax.broadcasted_iota(jnp.int32, (rows, 128), 1)
    out = jnp.zeros((rows, 128), F32)
    for i, term in enumerate((*split3(peak), *split3(total))):
        out = jnp.where(lane == i, term, out)
    return out.astype(BF16)


def unpack_stats(stats):
    stats = stats.astype(F32)
    peak = stats[:, 0:1] + stats[:, 1:2] + stats[:, 2:3]
    total = stats[:, 3:4] + stats[:, 4:5] + stats[:, 5:6]
    return peak, total


def merge(parts, stats):
    peak = stats[0][0]
    for other, _ in stats[1:]:
        peak = jnp.maximum(peak, other)
    total = jnp.zeros_like(peak)
    latent = jnp.zeros((peak.shape[0], LAT), F32)
    for part, (part_peak, part_total) in zip(parts, stats):
        keep = jnp.exp2((part_peak - peak) * RATE)
        total = total + part_total * keep
        latent = latent + part[:, :LAT].astype(F32) * keep
    return peak, total, latent


def kernel(
    parents, lengths, page_lists, queries, prompt, pool, value_up,
    out,
    q_in, q_wide, q_mirror, q_buf, pool_in, keys, v_buf, lists, room, cap, scores, probs,
    part, stat, rs1, rs1_stat, rs2_src, rs2, out_src,
    local_sem, key_send, key_recv, core_send, core_recv, swap_send, swap_recv, q_send, q_recv,
    rs1_send, rs1_recv, rs2_send, rs2_recv, out_send, out_recv,
):
    seq = lax.axis_index("seq")
    head = lax.axis_index("head")
    x = seq % 4
    y_lo = seq // 4
    c = head % 2
    y_hi = (head // 2) % 2
    z = head // 4
    y = y_hi * 2 + y_lo
    x_hi = x // 2
    x_lo = x % 2
    step = 1 - 2 * c
    request = x_lo * 2 + y_lo

    def shifted(dx, dy, sign=1):
        return place((x + sign * dx + 4) % 4, (y + sign * dy + 4) % 4, z, c)

    other_core = place(x, y, z, 1 - c)
    mirror = place(x, 3 - y, z, c)
    key_moves = ((1, 0), (0, 1), (1, 1))
    scatter_moves = ((2, 0), (0, 2), (2, 2))
    out_moves = [(dx, dy) for dy in range(2) for dx in range(4) if (dx, dy) != (0, 0)]

    def out_place(dx, dy):
        return place((x + dx) % 4, y_hi * 2 + (y_lo + dy) % 2, z, c)

    def out_source(dx, dy):
        return place((x - dx + 4) % 4, y_hi * 2 + (y_lo + dy) % 2, z, c)

    barrier = pltpu.get_barrier_semaphore()
    senders = [shifted(dx * step, dy * step, -1) for dx, dy in key_moves]
    senders += [other_core, mirror]
    senders += [place(x, y, (z + dz) % NZ, c) for dz in range(1, NZ)]
    senders += [shifted(dx, dy) for dx, dy in scatter_moves]
    senders += [out_source(dx, dy) for dx, dy in out_moves]
    for sender in senders:
        pl.semaphore_signal(barrier, inc=1, device_id=sender, device_id_type=MESH)

    mirror_request = x_lo * 2 + 1 - y_lo
    own_q = pltpu.make_async_copy(queries.at[pl.ds(request * BEAM, BEAM)], q_in.at[0], local_sem.at[0])
    mirror_q = pltpu.make_async_copy(queries.at[pl.ds(mirror_request * BEAM, BEAM)], q_in.at[1], local_sem.at[1])
    own_pool = pltpu.make_async_copy(pool, pool_in, local_sem.at[2])
    own_prompt = pltpu.make_async_copy(prompt.at[request], keys.at[c, 0, 0], local_sem.at[3])
    own_v = pltpu.make_async_copy(value_up, v_buf, local_sem.at[4])
    own_q.start()
    mirror_q.start()
    own_pool.start()
    own_prompt.start()
    own_v.start()

    def packed(i):
        for b in range(BEAM):
            block = q_in[i, b].astype(F32)
            half, start = b // 4, b % 4 * 4
            q_wide[i, start : start + 4, half * LAT : (half + 1) * LAT] = block[:, :LAT]
            if half:
                rotary = jnp.concatenate([q_in[i, b - 4].astype(F32)[:, LAT:], block[:, LAT:]], axis=1)
                q_wide[i, start : start + 4, 2 * LAT :] = rotary
        return q_wide[i].astype(BF16)

    mirror_q.wait()
    q_mirror[...] = packed(1)
    own_q.wait()
    q_buf[y_hi, z] = packed(0)
    own_pool.wait()
    flat_pool = pool_in[...].reshape(KEYS, WIDTH)
    keys[c, 0, 1, :LAT] = flat_pool[:, :LAT].T
    keys[c, 0, 1, LAT:] = flat_pool[:, LAT:].T

    pl.semaphore_wait(barrier, len(senders))

    copies = []

    def send(src, dst, send_sem, recv_sem, target):
        copy = pltpu.make_async_remote_copy(
            src_ref=src, dst_ref=dst, send_sem=send_sem, recv_sem=recv_sem, device_id=target, device_id_type=MESH
        )
        copy.start()
        copies.append(copy)
        return copy

    swap = send(q_mirror, q_buf.at[y_hi, z], swap_send, swap_recv, mirror)
    q_copies = {}
    far = (4, 3, 5)
    near = (2, 6, 1, 7)
    for dz in far + near:
        q_copies[0, dz] = send(
            q_buf.at[y_hi, z], q_buf.at[y_hi, z], q_send.at[0, dz], q_recv.at[0, dz],
            place(x, y, (z + dz) % NZ, c),
        )
    key_copies = []
    for i, (dx, dy) in enumerate(key_moves):
        target_request = (x_lo + dx) % 2 * 2 + (y_lo + dy) % 2
        target = shifted(dx * step, dy * step)
        key_copies.append((
            send(prompt.at[target_request], keys.at[c, i + 1, 0], key_send.at[i, 0], key_recv.at[i, 0], target),
            send(keys.at[c, 0, 1], keys.at[c, i + 1, 1], key_send.at[i, 1], key_recv.at[i, 1], target),
        ))
    own_prompt.wait()
    core_copies = [
        send(keys.at[c, 0], keys.at[c, 0], core_send.at[0], core_recv.at[0], other_core)]

    slot = lax.broadcasted_iota(jnp.int32, (4, MAXP), 1)
    for b in range(BEAM):
        parent = parents[request * BEAM + b]
        lists[4 * b : 4 * b + 4, :] = jnp.broadcast_to(page_lists[pl.ds(parent, 1), :], (4, MAXP))
        room[4 * b : 4 * b + 4, :] = jnp.clip(lengths[parent] - slot * PAGE, 0, PAGE)
    chosen = lists[...]
    space = room[...]
    lane = lax.broadcasted_iota(jnp.int32, (4 * BEAM, KEYS), 1)
    for cc in range(2):
        sign = 1 - 2 * cc
        for kind, (dx, dy) in enumerate(((0, 0),) + key_moves):
            sy = (y - sign * dy + 4) % 4
            s_seq, s_head = place((x - sign * dx + 4) % 4, sy, z, cc)
            page = (s_seq * 32 + s_head) * 2
            live = [
                jnp.sum(jnp.where(chosen == page + i, space, 0), axis=1, keepdims=True) for i in range(2)
            ]
            seen = lane < jnp.where(lane < PAGE, live[0], live[1] + PAGE)
            cap[:, (cc * 4 + kind) * KEYS : (cc * 4 + kind + 1) * KEYS] = jnp.where(seen, jnp.inf, -jnp.inf)

    swap.wait_recv()
    for dz in near:
        q_copies[1, dz] = send(
            q_buf.at[1 - y_hi, z], q_buf.at[1 - y_hi, z], q_send.at[1, dz], q_recv.at[1, dz],
            place(x, y, (z + dz) % NZ, c),
        )
    for dz in far:
        q_copies[0, dz].wait_recv()
        source = (z - dz + NZ) % NZ
        q_copies[1, dz] = send(
            q_buf.at[y_hi, source], q_buf.at[y_hi, source], q_send.at[1, dz], q_recv.at[1, dz], shifted(0, 2))
    for i, (prompt_copy, pool_copy) in enumerate(key_copies):
        prompt_copy.wait_recv()
        pool_copy.wait_recv()
        core_copies.append(send(
            keys.at[c, i + 1], keys.at[c, i + 1], core_send.at[i + 1], core_recv.at[i + 1], other_core))
    for copy in core_copies:
        copy.wait_recv()

    key_blocks = [(cc, kind, pooled) for pooled in range(2) for cc in range(2) for kind in range(4)]

    rs1_copies = []

    def attend(group):
        block = q_buf[group].reshape(KEYS, 2 * LAT + 128)
        rotary = block[:, 2 * LAT :]
        lane = lax.broadcasted_iota(jnp.int32, (KEYS, 128), 1)
        rows = jnp.concatenate([
            jnp.concatenate([block[:, :LAT], jnp.where(lane < ROPE, rotary, 0)], axis=1),
            jnp.concatenate([block[:, LAT : 2 * LAT], jnp.where(lane < ROPE, 0, rotary)], axis=1),
        ], axis=0)
        for pair in range(8):
            columns = jnp.concatenate([keys[k] for k in key_blocks[2 * pair : 2 * pair + 2]], axis=1)
            columns = jnp.concatenate([columns, columns[LAT:]], axis=0)
            raw = jnp.dot(rows, columns, preferred_element_type=F32)
            if pair >= 4:
                limit = cap[:, (2 * pair - 8) * KEYS : (2 * pair - 6) * KEYS].reshape(2, 1, 16, 2 * KEYS)
                raw = jnp.minimum(raw.reshape(2, NZ, 16, 2 * KEYS), limit).reshape(2 * KEYS, 2 * KEYS)
            scores[:, 2 * pair * KEYS : 2 * (pair + 1) * KEYS] = raw
        peak = jnp.max(scores[...], axis=1, keepdims=True)
        weights = jnp.exp2((scores[...] - peak) * RATE)
        total = jnp.sum(weights, axis=1, keepdims=True)
        probs[...] = weights.astype(BF16)
        values = jnp.concatenate([keys[cc, kind, pooled, :LAT] for cc, kind, pooled in key_blocks], axis=1)
        latent = lax.dot_general(
            probs[...], values, (((1,), (1,)), ((), ())), preferred_element_type=F32)
        part[group] = latent.astype(BF16).reshape(2, KEYS, LAT)
        for half in range(2):
            half_rows = slice(half * KEYS, (half + 1) * KEYS)
            stat[group, half] = jnp.where(lane == 0, peak[half_rows], total[half_rows]).T[:8]

    def scatter(i, group, half):
        dx, dy = scatter_moves[i]
        rs1_copies.append(send(
            part.at[group, half], rs1.at[i], rs1_send.at[i, 0], rs1_recv.at[i, 0], shifted(dx, dy)))
        rs1_copies.append(send(
            stat.at[group, half], rs1_stat.at[i], rs1_send.at[i, 1], rs1_recv.at[i, 1], shifted(dx, dy)))

    for dz in near:
        q_copies[0, dz].wait_recv()
    attend(y_hi)
    scatter(0, y_hi, 1 - x_hi)
    for dz in near + far:
        q_copies[1, dz].wait_recv()
    attend(1 - y_hi)
    scatter(2, 1 - y_hi, 1 - x_hi)
    scatter(1, 1 - y_hi, x_hi)

    for copy in rs1_copies:
        copy.wait_recv()
    columns = jnp.concatenate([
        stat[y_hi, x_hi], rs1_stat[0], rs1_stat[1], rs1_stat[2], jnp.zeros((KEYS - 32, KEYS), F32)], axis=0).T
    peak, total, latent = merge(
        [part[y_hi, x_hi], rs1[0], rs1[1], rs1[2]],
        [(columns[:, 8 * i : 8 * i + 1], columns[:, 8 * i + 1 : 8 * i + 2]) for i in range(4)])
    rs2_src[:, :, :LAT] = latent.astype(BF16).reshape(NZ, 16, LAT)
    rs2_src[:, :, LAT:] = pack_stats(peak, total).reshape(NZ, 16, 128)
    rs2_copies = []
    for dz in far + near:
        target_z = (z + dz) % NZ
        rs2_copies.append(send(
            rs2_src.at[target_z], rs2.at[dz], rs2_send.at[dz], rs2_recv.at[dz], place(x, y, target_z, c)))
    rs2[0] = rs2_src[z]
    own_v.wait()
    for copy in rs2_copies:
        copy.wait_recv()
    blocks = [rs2[i] for i in range(NZ)]
    peak, total, latent = merge(blocks, [unpack_stats(block[:, LAT:]) for block in blocks])
    latent = (latent / total).astype(BF16)
    row = lax.broadcasted_iota(jnp.int32, (16, VDIM), 0) % 4
    attended = jnp.zeros((16, VDIM), F32)
    for h in range(4):
        product = jnp.dot(latent, v_buf[h], preferred_element_type=F32)
        attended = jnp.where(row == h, product, attended)
    out_src[...] = attended.astype(BF16)
    place_out = request * 2 + x_hi
    out_copies = []
    for i, (dx, dy) in enumerate(out_moves):
        out_copies.append(send(
            out_src, out.at[place_out], out_send.at[i], out_recv.at[i], out_place(dx, dy)))
    out[place_out] = out_src[...]
    for copy in out_copies:
        copy.wait_recv()
    for copy in copies:
        copy.wait_send()


def body(queries, prompt_latent, pool_latent, value_up, parents, page_lists, lengths):
    vmem = pl.BlockSpec(memory_space=pltpu.VMEM)
    smem = pl.BlockSpec(memory_space=pltpu.SMEM)
    hbm = pl.BlockSpec(memory_space=pl.ANY)
    dma = pltpu.SemaphoreType.DMA
    result = pl.pallas_call(
        kernel,
        out_shape=jax.ShapeDtypeStruct((8, 16, VDIM), BF16),
        in_specs=[smem, smem, vmem, hbm, hbm, hbm, hbm],
        out_specs=vmem,
        scratch_shapes=[
            pltpu.VMEM((2, BEAM, 4, WIDTH), BF16),
            pltpu.VMEM((2, 16, 2 * LAT + 128), F32),
            pltpu.VMEM((16, 2 * LAT + 128), BF16),
            pltpu.VMEM((2, NZ, 16, 2 * LAT + 128), BF16),
            pltpu.VMEM((2, PAGE, WIDTH), BF16),
            pltpu.VMEM((2, 4, 2, WIDTH, KEYS), BF16),
            pltpu.VMEM((4, LAT, VDIM), BF16),
            pltpu.VMEM((4 * BEAM, MAXP), jnp.int32),
            pltpu.VMEM((4 * BEAM, MAXP), jnp.int32),
            pltpu.VMEM((4 * BEAM, 8 * KEYS), F32),
            pltpu.VMEM((2 * KEYS, 16 * KEYS), F32),
            pltpu.VMEM((2 * KEYS, 16 * KEYS), BF16),
            pltpu.VMEM((2, 2, KEYS, LAT), BF16),
            pltpu.VMEM((2, 2, 8, KEYS), F32),
            pltpu.VMEM((3, KEYS, LAT), BF16),
            pltpu.VMEM((3, 8, KEYS), F32),
            pltpu.VMEM((NZ, 16, PACK), BF16),
            pltpu.VMEM((NZ, 16, PACK), BF16),
            pltpu.VMEM((16, VDIM), BF16),
            dma((5,)), dma((3, 2)), dma((3, 2)), dma((4,)), dma((4,)), dma, dma, dma((2, NZ)), dma((2, NZ)),
            dma((3, 2)), dma((3, 2)), dma((NZ,)), dma((NZ,)), dma((7,)), dma((7,)),
        ],
        compiler_params=pltpu.CompilerParams(
            collective_id=0, has_side_effects=True, vmem_limit_bytes=60 * 2**20
        ),
    )(
        parents, lengths, page_lists, queries, prompt_latent.swapaxes(1, 2), pool_latent, value_up
    )
    return result.reshape(32, 4, VDIM)


def solution(mesh):
    return jax.shard_map(
        body,
        mesh=mesh,
        in_specs=(
            P(None, "head", None),
            P(None, ("seq", "head"), None),
            P(("seq", "head"), None, None),
            P("head", None, None),
            P(),
            P(),
            P(),
        ),
        out_specs=P(None, "head", None),
        check_vma=False,
    )
```

```python
import jax
import jax.numpy as jnp
from jax import lax
from jax.experimental import pallas as pl
from jax.experimental.pallas import tpu as pltpu
from jax.sharding import PartitionSpec as P

LAT = 512
ROPE = 64
WIDTH = LAT + ROPE
VDIM = 128
BEAM = 8
PAGE = 64
MAXP = 64
NZ = 8
RELATIVE = (4, 3, 5, 2, 6, 1, 7, 0)
SLOT = {dz: k for k, dz in enumerate(RELATIVE)}
KEYS = 128
LOG2E = 1.4426950408889634
RATE = (VDIM + ROPE) ** -0.5 * LOG2E
MESH = pl.DeviceIdType.MESH
F32 = jnp.float32
BF16 = jnp.bfloat16


def place(x, y, z, c):
    return ((y % 2) * 4 + x, z * 4 + (y // 2) * 2 + c)


def merge(parts, stats):
    peak = stats[0][0]
    for other, _ in stats[1:]:
        peak = jnp.maximum(peak, other)
    total = jnp.zeros_like(peak)
    latent = jnp.zeros((peak.shape[0], LAT), F32)
    for part, (part_peak, part_total) in zip(parts, stats):
        keep = jnp.exp2((part_peak - peak) * RATE)
        total = total + part_total * keep
        latent = latent + part[:, :LAT].astype(F32) * keep
    return peak, total, latent


def kernel(
    parents_hbm, lengths_hbm, lists_hbm, queries, prompt, pool, value_up,
    out,
    parents, lengths, page_lists,
    q_in, q_wide, q_mirror, q_buf, pool_in, keys, v_buf, lists, room, cap, scores, probs,
    part, stat, rs1, rs1_stat, rs2_src, rs2_stat_src, rs2, rs2_stat, out_src,
    local_sem, key_send, key_recv, core_send, core_recv, swap_send, swap_recv, q_send, q_recv,
    rs1_send, rs1_recv, rs2_send, rs2_recv, out_send, out_recv,
):
    seq = lax.axis_index("seq")
    head = lax.axis_index("head")
    x = seq % 4
    y_lo = seq // 4
    c = head % 2
    y_hi = (head // 2) % 2
    z = head // 4
    y = y_hi * 2 + y_lo
    x_hi = x // 2
    x_lo = x % 2
    step = 1 - 2 * c
    request = x_lo * 2 + y_lo

    def shifted(dx, dy, sign=1):
        return place((x + sign * dx + 4) % 4, (y + sign * dy + 4) % 4, z, c)

    other_core = place(x, y, z, 1 - c)
    mirror = place(x, 3 - y, z, c)
    key_moves = ((1, 0), (0, 1), (1, 1))
    scatter_moves = ((0, 2), (2, 2), (2, 0))
    out_moves = [(dx, dy) for dy in range(2) for dx in range(4) if (dx, dy) != (0, 0)]

    def out_place(dx, dy):
        return place((x + dx) % 4, y_hi * 2 + (y_lo + dy) % 2, z, c)

    barrier = pltpu.get_barrier_semaphore()
    senders = [place(x, y, (z + dz) % NZ, c) for dz in RELATIVE[:-1]]
    senders += [shifted(dx * step, dy * step, -1) for dx, dy in key_moves]
    senders += [shifted(dx, dy) for dx, dy in scatter_moves]
    senders += [mirror, other_core]
    for sender in senders:
        pl.semaphore_signal(barrier, inc=1, device_id=sender, device_id_type=MESH)

    mirror_request = x_lo * 2 + 1 - y_lo
    own_q = pltpu.make_async_copy(queries.at[pl.ds(request * BEAM, BEAM)], q_in.at[0], local_sem.at[0])
    mirror_q = pltpu.make_async_copy(queries.at[pl.ds(mirror_request * BEAM, BEAM)], q_in.at[1], local_sem.at[1])
    own_pool = pltpu.make_async_copy(pool, pool_in, local_sem.at[2])
    own_prompt = pltpu.make_async_copy(prompt.at[request], keys.at[c, 0, 0], local_sem.at[3])
    own_v = pltpu.make_async_copy(value_up, v_buf, local_sem.at[4])
    get_parents = pltpu.make_async_copy(parents_hbm, parents, local_sem.at[5])
    get_lengths = pltpu.make_async_copy(lengths_hbm, lengths, local_sem.at[6])
    get_lists = pltpu.make_async_copy(lists_hbm, page_lists, local_sem.at[7])
    own_q.start()
    mirror_q.start()
    own_pool.start()
    own_prompt.start()
    get_parents.start()
    get_lengths.start()
    get_lists.start()
    own_v.start()

    def packed(i):
        for b in range(BEAM):
            block = q_in[i, b].astype(F32)
            half, start = b // 4, b % 4 * 4
            q_wide[i, start : start + 4, half * LAT : (half + 1) * LAT] = block[:, :LAT]
            if half:
                rotary = jnp.concatenate([q_in[i, b - 4].astype(F32)[:, LAT:], block[:, LAT:]], axis=1)
                q_wide[i, start : start + 4, 2 * LAT :] = rotary
        return q_wide[i].astype(BF16)

    mirror_q.wait()
    q_mirror[...] = packed(1)
    own_q.wait()
    q_buf[y_hi, SLOT[0]] = packed(0)
    own_pool.wait()
    flat_pool = pool_in[...].reshape(KEYS, WIDTH)
    keys[c, 0, 1, :LAT] = flat_pool[:, :LAT].T
    keys[c, 0, 1, LAT:] = flat_pool[:, LAT:].T

    pl.semaphore_wait(barrier, len(senders))

    copies = []

    def send(src, dst, send_sem, recv_sem, target):
        copy = pltpu.make_async_remote_copy(
            src_ref=src, dst_ref=dst, send_sem=send_sem, recv_sem=recv_sem, device_id=target, device_id_type=MESH
        )
        copy.start()
        copies.append(copy)
        return copy

    swap = send(q_mirror, q_buf.at[y_hi, SLOT[0]], swap_send, swap_recv, mirror)
    q_copies = {}

    def along_z(group, dz):
        slot = SLOT[(NZ - dz) % NZ]
        q_copies[group, slot] = send(
            q_buf.at[(y_hi + group) % 2, SLOT[0]], q_buf.at[(y_hi + group) % 2, slot],
            q_send.at[group, slot], q_recv.at[group, slot], place(x, y, (z + dz) % NZ, c),
        )

    for dz in RELATIVE[:-1]:
        along_z(0, dz)
    key_copies = {}
    for pooled in range(2):
        for i, (dx, dy) in enumerate(key_moves):
            target_request = (x_lo + dx) % 2 * 2 + (y_lo + dy) % 2
            key_copies[pooled, i + 1] = send(
                keys.at[c, 0, 1] if pooled else prompt.at[target_request], keys.at[c, i + 1, pooled],
                key_send.at[i, pooled], key_recv.at[i, pooled], shifted(dx * step, dy * step))
    core_copies = []

    def to_core(kind, pooled):
        core_copies.append(send(
            keys.at[c, kind, pooled], keys.at[c, kind, pooled],
            core_send.at[kind, pooled], core_recv.at[kind, pooled], other_core))

    own_prompt.wait()
    to_core(0, 0)
    to_core(0, 1)

    get_parents.wait()
    get_lengths.wait()
    get_lists.wait()
    slot = lax.broadcasted_iota(jnp.int32, (4, MAXP), 1)
    for b in range(BEAM):
        parent = parents[request * BEAM + b]
        lists[4 * b : 4 * b + 4, :] = jnp.broadcast_to(page_lists[pl.ds(parent, 1), :], (4, MAXP))
        room[4 * b : 4 * b + 4, :] = jnp.clip(lengths[parent] - slot * PAGE, 0, PAGE)
    chosen = lists[...]
    space = room[...]
    lane = lax.broadcasted_iota(jnp.int32, (4 * BEAM, KEYS), 1)
    for cc in range(2):
        sign = 1 - 2 * cc
        for kind, (dx, dy) in enumerate(((0, 0),) + key_moves):
            sy = (y - sign * dy + 4) % 4
            s_seq, s_head = place((x - sign * dx + 4) % 4, sy, z, cc)
            page = (s_seq * 32 + s_head) * 2
            live = [
                jnp.sum(jnp.where(chosen == page + i, space, 0), axis=1, keepdims=True) for i in range(2)
            ]
            seen = lane < jnp.where(lane < PAGE, live[0], live[1] + PAGE)
            cap[:, (cc * 4 + kind) * KEYS : (cc * 4 + kind + 1) * KEYS] = jnp.where(seen, jnp.inf, -jnp.inf)

    swap.wait_recv()
    for dz in RELATIVE[1:-1]:
        along_z(1, dz)
    for kind in range(1, 4):
        key_copies[0, kind].wait_recv()
        to_core(kind, 0)
    q_copies[0, 0].wait_recv()
    q_copies[1, 0] = send(
        q_buf.at[y_hi, 0], q_buf.at[y_hi, 0], q_send.at[1, 0], q_recv.at[1, 0], shifted(0, 2))
    for kind in range(1, 4):
        key_copies[1, kind].wait_recv()
        to_core(kind, 1)
    for copy in core_copies:
        copy.wait_recv()

    key_blocks = [(cc, kind, pooled) for pooled in range(2) for cc in range(2) for kind in range(4)]

    rs1_copies = {}

    def attend(group):
        block = q_buf[group].reshape(KEYS, 2 * LAT + 128)
        rotary = block[:, 2 * LAT :]
        lane = lax.broadcasted_iota(jnp.int32, (KEYS, 128), 1)
        rows = jnp.concatenate([
            jnp.concatenate([block[:, :LAT], jnp.where(lane < ROPE, rotary, 0)], axis=1),
            jnp.concatenate([block[:, LAT : 2 * LAT], jnp.where(lane < ROPE, 0, rotary)], axis=1),
        ], axis=0)
        for pair in range(8):
            columns = jnp.concatenate([keys[k] for k in key_blocks[2 * pair : 2 * pair + 2]], axis=1)
            columns = jnp.concatenate([columns, columns[LAT:]], axis=0)
            raw = jnp.dot(rows, columns, preferred_element_type=F32)
            if pair >= 4:
                limit = cap[:, (2 * pair - 8) * KEYS : (2 * pair - 6) * KEYS].reshape(2, 1, 16, 2 * KEYS)
                raw = jnp.minimum(raw.reshape(2, NZ, 16, 2 * KEYS), limit).reshape(2 * KEYS, 2 * KEYS)
            scores[:, 2 * pair * KEYS : 2 * (pair + 1) * KEYS] = raw
        peak = jnp.max(scores[...], axis=1, keepdims=True)
        weights = jnp.exp2((scores[...] - peak) * RATE)
        total = jnp.sum(weights, axis=1, keepdims=True)
        probs[...] = weights.astype(BF16)
        values = jnp.concatenate([keys[cc, kind, pooled, :LAT] for cc, kind, pooled in key_blocks], axis=1)
        latent = lax.dot_general(
            probs[...], values, (((1,), (1,)), ((), ())), preferred_element_type=F32)
        part[group] = latent.astype(BF16).reshape(2, KEYS, LAT)
        for half in range(2):
            half_rows = slice(half * KEYS, (half + 1) * KEYS)
            stat[group, half] = jnp.where(lane == 0, peak[half_rows], total[half_rows]).T[:8]

    chunks = (slice(0, 64), slice(64, 128))

    def scatter(i, group, half, chunk):
        rows = pl.ds(64 * chunk, 64)
        rs1_copies[i, chunk] = send(
            part.at[group, half, rows], rs1.at[i, rows],
            rs1_send.at[i, chunk], rs1_recv.at[i, chunk], shifted(*scatter_moves[i]))

    def scatter_stat(i, group, half):
        rs1_copies[i, 2] = send(
            stat.at[group, half], rs1_stat.at[i], rs1_send.at[i, 2], rs1_recv.at[i, 2], shifted(*scatter_moves[i]))

    for slot in range(1, NZ - 1):
        q_copies[0, slot].wait_recv()
    attend(y_hi)
    scatter_stat(1, y_hi, 1 - x_hi)
    scatter_stat(0, y_hi, x_hi)
    for chunk in range(2):
        scatter(1, y_hi, 1 - x_hi, chunk)
        scatter(0, y_hi, x_hi, chunk)
    for slot in range(NZ - 1):
        q_copies[1, slot].wait_recv()
    attend(1 - y_hi)
    scatter_stat(2, 1 - y_hi, 1 - x_hi)
    for chunk in range(2):
        scatter(2, 1 - y_hi, 1 - x_hi, chunk)

    rs2_copies = []
    for i in range(3):
        rs1_copies[i, 2].wait_recv()
    columns = jnp.concatenate([
        stat[1 - y_hi, x_hi], rs1_stat[0], rs1_stat[1], rs1_stat[2], jnp.zeros((KEYS - 32, KEYS), F32)], axis=0).T
    lane = lax.broadcasted_iota(jnp.int32, (64, KEYS), 1)
    row = lax.broadcasted_iota(jnp.int32, (64, KEYS), 0) % 16
    for chunk, rows in enumerate(chunks):
        for i in range(3):
            rs1_copies[i, chunk].wait_recv()
        peak, total, latent = merge(
            [part[1 - y_hi, x_hi, rows], rs1[0, rows], rs1[1, rows], rs1[2, rows]],
            [(columns[rows, 8 * i : 8 * i + 1], columns[rows, 8 * i + 1 : 8 * i + 2]) for i in range(4)])
        rs2_src[4 * chunk : 4 * chunk + 4] = latent.astype(BF16).reshape(4, 16, LAT)
        spread = jnp.where(lane == row, peak, 0.0) + jnp.where(lane == row + 16, total, 0.0)
        rs2_stat_src[4 * chunk : 4 * chunk + 4] = jnp.sum(spread.reshape(4, 16, KEYS), axis=1, keepdims=True)
        for slot in range(4 * chunk, 4 * chunk + 4):
            target = place(x, 3 - y, (z + RELATIVE[slot]) % NZ, c)
            rs2_copies.append(send(
                rs2_src.at[slot], rs2.at[slot], rs2_send.at[slot, 0], rs2_recv.at[slot, 0], target))
            rs2_copies.append(send(
                rs2_stat_src.at[slot], rs2_stat.at[slot], rs2_send.at[slot, 1], rs2_recv.at[slot, 1], target))
    own_v.wait()
    for copy in rs2_copies:
        copy.wait_recv()
    lane = lax.broadcasted_iota(jnp.int32, (16, KEYS), 1)
    row = lax.broadcasted_iota(jnp.int32, (16, KEYS), 0)
    stats = []
    for slot in range(NZ):
        line = rs2_stat[slot]
        stats.append((
            jnp.sum(jnp.where(lane == row, line, 0.0), axis=1, keepdims=True),
            jnp.sum(jnp.where(lane == row + 16, line, 0.0), axis=1, keepdims=True)))
    peak, total, latent = merge([rs2[slot] for slot in range(NZ)], stats)
    latent = (latent / total).astype(BF16)
    attended = jnp.zeros((16, VDIM), F32)
    for h in range(4):
        product = jnp.dot(latent, v_buf[h], preferred_element_type=F32)
        attended = jnp.where(row % 4 == h, product, attended)
    out_src[...] = attended.astype(BF16)
    place_out = mirror_request * 2 + x_hi
    out_copies = []
    for i, (dx, dy) in enumerate(out_moves):
        out_copies.append(send(
            out_src, out.at[place_out], out_send.at[i], out_recv.at[i], out_place(dx, dy)))
    out[place_out] = out_src[...]
    for copy in out_copies:
        copy.wait_recv()
    for copy in copies:
        copy.wait_send()


def body(queries, prompt_latent, pool_latent, value_up, parents, page_lists, lengths):
    vmem = pl.BlockSpec(memory_space=pltpu.VMEM)
    hbm = pl.BlockSpec(memory_space=pltpu.HBM)
    dma = pltpu.SemaphoreType.DMA
    result = pl.pallas_call(
        kernel,
        out_shape=jax.ShapeDtypeStruct((8, 16, VDIM), BF16),
        in_specs=[hbm] * 7,
        out_specs=vmem,
        scratch_shapes=[
            pltpu.SMEM((32,), jnp.int32),
            pltpu.SMEM((32,), jnp.int32),
            pltpu.VMEM((32, MAXP), jnp.int32),
            pltpu.VMEM((2, BEAM, 4, WIDTH), BF16),
            pltpu.VMEM((2, 16, 2 * LAT + 128), F32),
            pltpu.VMEM((16, 2 * LAT + 128), BF16),
            pltpu.VMEM((2, NZ, 16, 2 * LAT + 128), BF16),
            pltpu.VMEM((2, PAGE, WIDTH), BF16),
            pltpu.VMEM((2, 4, 2, WIDTH, KEYS), BF16),
            pltpu.VMEM((4, LAT, VDIM), BF16),
            pltpu.VMEM((4 * BEAM, MAXP), jnp.int32),
            pltpu.VMEM((4 * BEAM, MAXP), jnp.int32),
            pltpu.VMEM((4 * BEAM, 8 * KEYS), F32),
            pltpu.VMEM((2 * KEYS, 16 * KEYS), F32),
            pltpu.VMEM((2 * KEYS, 16 * KEYS), BF16),
            pltpu.VMEM((2, 2, KEYS, LAT), BF16),
            pltpu.VMEM((2, 2, 8, KEYS), F32),
            pltpu.VMEM((3, KEYS, LAT), BF16),
            pltpu.VMEM((3, 8, KEYS), F32),
            pltpu.VMEM((NZ, 16, LAT), BF16),
            pltpu.VMEM((NZ, 1, KEYS), F32),
            pltpu.VMEM((NZ, 16, LAT), BF16),
            pltpu.VMEM((NZ, 1, KEYS), F32),
            pltpu.VMEM((16, VDIM), BF16),
            dma((8,)), dma((3, 2)), dma((3, 2)), dma((4, 2)), dma((4, 2)), dma, dma, dma((2, NZ)), dma((2, NZ)),
            dma((3, 3)), dma((3, 3)), dma((NZ, 2)), dma((NZ, 2)), dma((7,)), dma((7,)),
        ],
        compiler_params=pltpu.CompilerParams(
            collective_id=0, has_side_effects=True, vmem_limit_bytes=60 * 2**20
        ),
    )(
        parents, lengths, page_lists, queries, prompt_latent.swapaxes(1, 2), pool_latent, value_up
    )
    return result.reshape(32, 4, VDIM)


def solution(mesh):
    return jax.shard_map(
        body,
        mesh=mesh,
        in_specs=(
            P(None, "head", None),
            P(None, ("seq", "head"), None),
            P(("seq", "head"), None, None),
            P("head", None, None),
            P(),
            P(),
            P(),
        ),
        out_specs=P(None, "head", None),
        check_vma=False,
    )
```

```python
import jax
import jax.numpy as jnp
from jax import lax
from jax.experimental import pallas as pl
from jax.experimental.pallas import tpu as pltpu
from jax.sharding import PartitionSpec as P

LAT = 512
ROPE = 64
WIDTH = LAT + ROPE
VDIM = 128
BEAM = 8
PAGE = 64
MAXP = 64
NZ = 8
RELATIVE = (4, 3, 5, 2, 6, 1, 7, 0)
SLOT = {dz: k for k, dz in enumerate(RELATIVE)}
KEYS = 128
LOG2E = 1.4426950408889634
RATE = (VDIM + ROPE) ** -0.5 * LOG2E
MESH = pl.DeviceIdType.MESH
F32 = jnp.float32
BF16 = jnp.bfloat16


def place(x, y, z, c):
    return ((y % 2) * 4 + x, z * 4 + (y // 2) * 2 + c)


def merge(parts, stats):
    peak = stats[0][0]
    for other, _ in stats[1:]:
        peak = jnp.maximum(peak, other)
    total = jnp.zeros_like(peak)
    latent = jnp.zeros((peak.shape[0], LAT), F32)
    for part, (part_peak, part_total) in zip(parts, stats):
        keep = jnp.exp2((part_peak - peak) * RATE)
        total = total + part_total * keep
        latent = latent + part[:, :LAT].astype(F32) * keep
    return peak, total, latent


def lines(peak, total):
    rows = peak.shape[0]
    lane = lax.broadcasted_iota(jnp.int32, (rows, KEYS), 1)
    row = lax.broadcasted_iota(jnp.int32, (rows, KEYS), 0) % 16
    spread = jnp.where(lane == row, peak, 0.0) + jnp.where(lane == row + 16, total, 0.0)
    return jnp.sum(spread.reshape(rows // 16, 16, KEYS), axis=1, keepdims=True)


def from_line(line):
    lane = lax.broadcasted_iota(jnp.int32, (16, KEYS), 1)
    row = lax.broadcasted_iota(jnp.int32, (16, KEYS), 0)
    return (
        jnp.sum(jnp.where(lane == row, line, 0.0), axis=1, keepdims=True),
        jnp.sum(jnp.where(lane == row + 16, line, 0.0), axis=1, keepdims=True))


def kernel(
    parents_hbm, lengths_hbm, lists_hbm, queries, prompt, pool, value_up,
    out,
    parents, lengths, page_lists,
    q_in, q_wide, q_mirror, q_buf, pool_in, keys, v_buf, lists, room, cap, scores, probs,
    part, stat, rs1, rs1_stat, zs, zs_stat_src, zs_stat, rs2_src, rs2_stat_src, rs2, rs2_stat, out_src,
    local_sem, key_send, key_recv, core_send, core_recv, swap_send, swap_recv, q_send, q_recv,
    rs1_send, rs1_recv, zs_send, zs_recv, rs2_send, rs2_recv, out_send, out_recv,
):
    seq = lax.axis_index("seq")
    head = lax.axis_index("head")
    x = seq % 4
    y_lo = seq // 4
    c = head % 2
    y_hi = (head // 2) % 2
    z = head // 4
    y = y_hi * 2 + y_lo
    x_hi = x // 2
    x_lo = x % 2
    step = 1 - 2 * c
    request = x_lo * 2 + y_lo

    def shifted(dx, dy, sign=1):
        return place((x + sign * dx + 4) % 4, (y + sign * dy + 4) % 4, z, c)

    other_core = place(x, y, z, 1 - c)
    mirror = place(x, 3 - y, z, c)
    key_moves = ((1, 0), (0, 1), (1, 1))
    scatter_moves = ((0, 2), (2, 0))
    out_moves = [(dx, dy) for dy in range(2) for dx in range(4) if (dx, dy) != (0, 0)]

    def out_place(dx, dy):
        return place((x + dx) % 4, y_hi * 2 + (y_lo + dy) % 2, z, c)

    barrier = pltpu.get_barrier_semaphore()
    senders = [place(x, y, (z + dz) % NZ, c) for dz in RELATIVE[:-1]]
    senders += [shifted(dx * step, dy * step, -1) for dx, dy in key_moves]
    senders += [shifted(dx, dy) for dx, dy in scatter_moves]
    senders += [mirror, other_core]
    for sender in senders:
        pl.semaphore_signal(barrier, inc=1, device_id=sender, device_id_type=MESH)

    mirror_request = x_lo * 2 + 1 - y_lo
    own_q = pltpu.make_async_copy(queries.at[pl.ds(request * BEAM, BEAM)], q_in.at[0], local_sem.at[0])
    mirror_q = pltpu.make_async_copy(queries.at[pl.ds(mirror_request * BEAM, BEAM)], q_in.at[1], local_sem.at[1])
    own_pool = pltpu.make_async_copy(pool, pool_in, local_sem.at[2])
    own_prompt = pltpu.make_async_copy(prompt.at[request], keys.at[c, 0, 0], local_sem.at[3])
    own_v = pltpu.make_async_copy(value_up, v_buf, local_sem.at[4])
    get_parents = pltpu.make_async_copy(parents_hbm, parents, local_sem.at[5])
    get_lengths = pltpu.make_async_copy(lengths_hbm, lengths, local_sem.at[6])
    get_lists = pltpu.make_async_copy(lists_hbm, page_lists, local_sem.at[7])
    own_q.start()
    mirror_q.start()
    own_pool.start()
    own_prompt.start()
    get_parents.start()
    get_lengths.start()
    get_lists.start()
    own_v.start()

    def packed(i):
        for b in range(BEAM):
            block = q_in[i, b].astype(F32)
            half, start = b // 4, b % 4 * 4
            q_wide[i, start : start + 4, half * LAT : (half + 1) * LAT] = block[:, :LAT]
            if half:
                rotary = jnp.concatenate([q_in[i, b - 4].astype(F32)[:, LAT:], block[:, LAT:]], axis=1)
                q_wide[i, start : start + 4, 2 * LAT :] = rotary
        return q_wide[i].astype(BF16)

    mirror_q.wait()
    q_mirror[...] = packed(1)
    own_q.wait()
    q_buf[y_hi, SLOT[0]] = packed(0)
    own_pool.wait()
    flat_pool = pool_in[...].reshape(KEYS, WIDTH)
    keys[c, 0, 1, :LAT] = flat_pool[:, :LAT].T
    keys[c, 0, 1, LAT:] = flat_pool[:, LAT:].T

    pl.semaphore_wait(barrier, len(senders))

    copies = []

    def send(src, dst, send_sem, recv_sem, target):
        copy = pltpu.make_async_remote_copy(
            src_ref=src, dst_ref=dst, send_sem=send_sem, recv_sem=recv_sem, device_id=target, device_id_type=MESH
        )
        copy.start()
        copies.append(copy)
        return copy

    swap = send(q_mirror, q_buf.at[y_hi, SLOT[0]], swap_send, swap_recv, mirror)
    q_copies = {}

    def along_z(group, dz):
        slot = SLOT[(NZ - dz) % NZ]
        q_copies[group, slot] = send(
            q_buf.at[(y_hi + group) % 2, SLOT[0]], q_buf.at[(y_hi + group) % 2, slot],
            q_send.at[group, slot], q_recv.at[group, slot], place(x, y, (z + dz) % NZ, c),
        )

    pieces = ((0, slice(0, WIDTH)), (1, slice(0, WIDTH // 2)), (1, slice(WIDTH // 2, WIDTH)))
    key_copies = {}

    def key_piece(kind, piece):
        pooled, rows = pieces[piece]
        dx, dy = key_moves[kind - 1]
        target_request = (x_lo + dx) % 2 * 2 + (y_lo + dy) % 2
        key_copies[kind, piece] = send(
            keys.at[c, 0, 1, rows] if pooled else prompt.at[target_request], keys.at[c, kind, pooled, rows],
            key_send.at[kind - 1, piece], key_recv.at[kind - 1, piece], shifted(dx * step, dy * step))

    core_copies = []

    def to_core(kind, piece):
        pooled, rows = pieces[piece]
        core_copies.append(send(
            keys.at[c, kind, pooled, rows], keys.at[c, kind, pooled, rows],
            core_send.at[kind, piece], core_recv.at[kind, piece], other_core))

    for kind in range(1, 4):
        key_piece(kind, 0)
    for dz in RELATIVE[:-1]:
        along_z(0, dz)
    for piece in (1, 2):
        for kind in range(1, 4):
            key_piece(kind, piece)
    own_prompt.wait()
    for piece in range(3):
        to_core(0, piece)

    get_parents.wait()
    get_lengths.wait()
    get_lists.wait()
    slot = lax.broadcasted_iota(jnp.int32, (4, MAXP), 1)
    for b in range(BEAM):
        parent = parents[request * BEAM + b]
        lists[4 * b : 4 * b + 4, :] = jnp.broadcast_to(page_lists[pl.ds(parent, 1), :], (4, MAXP))
        room[4 * b : 4 * b + 4, :] = jnp.clip(lengths[parent] - slot * PAGE, 0, PAGE)
    chosen = lists[...]
    space = room[...]
    lane = lax.broadcasted_iota(jnp.int32, (4 * BEAM, KEYS), 1)
    for cc in range(2):
        sign = 1 - 2 * cc
        for kind, (dx, dy) in enumerate(((0, 0),) + key_moves):
            sy = (y - sign * dy + 4) % 4
            s_seq, s_head = place((x - sign * dx + 4) % 4, sy, z, cc)
            page = (s_seq * 32 + s_head) * 2
            live = [
                jnp.sum(jnp.where(chosen == page + i, space, 0), axis=1, keepdims=True) for i in range(2)
            ]
            seen = lane < jnp.where(lane < PAGE, live[0], live[1] + PAGE)
            cap[:, (cc * 4 + kind) * KEYS : (cc * 4 + kind + 1) * KEYS] = jnp.where(seen, jnp.inf, -jnp.inf)

    swap.wait_recv()
    for dz in RELATIVE[1:-1]:
        along_z(1, dz)
    for kind in range(1, 4):
        key_copies[kind, 0].wait_recv()
        to_core(kind, 0)
    q_copies[0, 0].wait_recv()
    q_copies[1, 0] = send(
        q_buf.at[y_hi, 0], q_buf.at[y_hi, 0], q_send.at[1, 0], q_recv.at[1, 0], shifted(0, 2))
    for piece in (1, 2):
        for kind in range(1, 4):
            key_copies[kind, piece].wait_recv()
            to_core(kind, piece)
    for copy in core_copies:
        copy.wait_recv()

    key_blocks = [(cc, kind, pooled) for pooled in range(2) for cc in range(2) for kind in range(4)]

    rs1_copies = {}

    def attend(group, z_first):
        block = q_buf[group].reshape(KEYS, 2 * LAT + 128)
        rotary = block[:, 2 * LAT :]
        lane = lax.broadcasted_iota(jnp.int32, (KEYS, 128), 1)
        rows = jnp.concatenate([
            jnp.concatenate([block[:, :LAT], jnp.where(lane < ROPE, rotary, 0)], axis=1),
            jnp.concatenate([block[:, LAT : 2 * LAT], jnp.where(lane < ROPE, 0, rotary)], axis=1),
        ], axis=0)
        for pair in range(8):
            columns = jnp.concatenate([keys[k] for k in key_blocks[2 * pair : 2 * pair + 2]], axis=1)
            columns = jnp.concatenate([columns, columns[LAT:]], axis=0)
            raw = jnp.dot(rows, columns, preferred_element_type=F32)
            if pair >= 4:
                limit = cap[:, (2 * pair - 8) * KEYS : (2 * pair - 6) * KEYS].reshape(2, 1, 16, 2 * KEYS)
                raw = jnp.minimum(raw.reshape(2, NZ, 16, 2 * KEYS), limit).reshape(2 * KEYS, 2 * KEYS)
            scores[:, 2 * pair * KEYS : 2 * (pair + 1) * KEYS] = raw
        peak = jnp.max(scores[...], axis=1, keepdims=True)
        weights = jnp.exp2((scores[...] - peak) * RATE)
        total = jnp.sum(weights, axis=1, keepdims=True)
        probs[...] = weights.astype(BF16)
        values = jnp.concatenate([keys[cc, kind, pooled, :LAT] for cc, kind, pooled in key_blocks], axis=1)
        latent = lax.dot_general(
            probs[...], values, (((1,), (1,)), ((), ())), preferred_element_type=F32)
        part[group] = latent.astype(BF16).reshape(2, KEYS, LAT)
        for half in range(2):
            half_rows = slice(half * KEYS, (half + 1) * KEYS)
            stat[group, half] = jnp.where(lane == 0, peak[half_rows], total[half_rows]).T[:8]
            if z_first:
                zs_stat_src[half] = lines(peak[half_rows], total[half_rows])

    chunks = (slice(0, 64), slice(64, 128))

    def scatter(i, group, half, chunk):
        rows = pl.ds(64 * chunk, 64)
        rs1_copies[i, chunk] = send(
            part.at[group, half, rows], rs1.at[i, rows],
            rs1_send.at[i, chunk], rs1_recv.at[i, chunk], shifted(*scatter_moves[i]))

    def scatter_stat(i, group, half):
        rs1_copies[i, 2] = send(
            stat.at[group, half], rs1_stat.at[i], rs1_send.at[i, 2], rs1_recv.at[i, 2], shifted(*scatter_moves[i]))

    zs_copies = []
    for slot in range(1, NZ - 1):
        q_copies[0, slot].wait_recv()
    attend(y_hi, True)
    scatter_stat(0, y_hi, x_hi)
    scatter(0, y_hi, x_hi, 0)
    for slot in range(NZ - 1):
        target = place(x, y, (z + RELATIVE[slot]) % NZ, c)
        zs_copies.append(send(
            part.at[y_hi, 1 - x_hi, pl.ds(16 * slot, 16)], zs.at[slot], zs_send.at[slot, 0], zs_recv.at[slot, 0], target))
        zs_copies.append(send(
            zs_stat_src.at[1 - x_hi, slot], zs_stat.at[slot], zs_send.at[slot, 1], zs_recv.at[slot, 1], target))
    scatter(0, y_hi, x_hi, 1)
    for slot in range(NZ - 1):
        q_copies[1, slot].wait_recv()
    attend(1 - y_hi, False)
    scatter_stat(1, 1 - y_hi, 1 - x_hi)
    for chunk in range(2):
        scatter(1, 1 - y_hi, 1 - x_hi, chunk)

    rs2_copies = []

    def home(slot, target):
        rs2_copies.append(send(
            rs2_src.at[slot], rs2.at[slot], rs2_send.at[slot, 0], rs2_recv.at[slot, 0], target))
        rs2_copies.append(send(
            rs2_stat_src.at[slot], rs2_stat.at[slot], rs2_send.at[slot, 1], rs2_recv.at[slot, 1], target))

    for i in range(2):
        rs1_copies[i, 2].wait_recv()
    columns = jnp.concatenate([
        stat[1 - y_hi, x_hi], rs1_stat[0], rs1_stat[1], jnp.zeros((KEYS - 24, KEYS), F32)], axis=0).T
    for chunk, rows in enumerate(chunks):
        for i in range(2):
            rs1_copies[i, chunk].wait_recv()
        peak, total, latent = merge(
            [part[1 - y_hi, x_hi, rows], rs1[0, rows], rs1[1, rows]],
            [(columns[rows, 8 * i : 8 * i + 1], columns[rows, 8 * i + 1 : 8 * i + 2]) for i in range(3)])
        rs2_src[4 * chunk : 4 * chunk + 4] = latent.astype(BF16).reshape(4, 16, LAT)
        rs2_stat_src[4 * chunk : 4 * chunk + 4] = lines(peak, total)
        for slot in range(4 * chunk, 4 * chunk + 4):
            home(slot, place(x, 3 - y, (z + RELATIVE[slot]) % NZ, c))
    for copy in zs_copies:
        copy.wait_recv()
    peak, total, latent = merge(
        [part[y_hi, 1 - x_hi, 16 * SLOT[0] :]] + [zs[slot] for slot in range(NZ - 1)],
        [from_line(zs_stat_src[1 - x_hi, SLOT[0]])] + [from_line(zs_stat[slot]) for slot in range(NZ - 1)])
    rs2_src[NZ] = latent.astype(BF16)
    rs2_stat_src[NZ : NZ + 1] = lines(peak, total)
    home(NZ, place((x + 2) % 4, y_hi * 2 + 1 - y_lo, z, c))
    own_v.wait()
    for copy in rs2_copies:
        copy.wait_recv()
    peak, total, latent = merge([rs2[slot] for slot in range(NZ + 1)], [from_line(rs2_stat[slot]) for slot in range(NZ + 1)])
    latent = (latent / total).astype(BF16)
    attended = jnp.zeros((16, VDIM), F32)
    row = lax.broadcasted_iota(jnp.int32, (16, VDIM), 0)
    for h in range(4):
        product = jnp.dot(latent, v_buf[h], preferred_element_type=F32)
        attended = jnp.where(row % 4 == h, product, attended)
    out_src[...] = attended.astype(BF16)
    place_out = mirror_request * 2 + x_hi
    out_copies = []
    for i, (dx, dy) in enumerate(out_moves):
        out_copies.append(send(
            out_src, out.at[place_out], out_send.at[i], out_recv.at[i], out_place(dx, dy)))
    out[place_out] = out_src[...]
    for copy in out_copies:
        copy.wait_recv()
    for copy in copies:
        copy.wait_send()


def body(queries, prompt_latent, pool_latent, value_up, parents, page_lists, lengths):
    vmem = pl.BlockSpec(memory_space=pltpu.VMEM)
    hbm = pl.BlockSpec(memory_space=pltpu.HBM)
    operands = (parents, lengths, page_lists, queries, prompt_latent.swapaxes(1, 2), pool_latent, value_up)
    dma = pltpu.SemaphoreType.DMA
    result = pl.pallas_call(
        kernel,
        out_shape=pltpu.VMEM((8, 16, VDIM), BF16),
        in_specs=[hbm] * 7,
        out_specs=vmem,
        scratch_shapes=[
            pltpu.SMEM((32,), jnp.int32),
            pltpu.SMEM((32,), jnp.int32),
            pltpu.VMEM((32, MAXP), jnp.int32),
            pltpu.VMEM((2, BEAM, 4, WIDTH), BF16),
            pltpu.VMEM((2, 16, 2 * LAT + 128), F32),
            pltpu.VMEM((16, 2 * LAT + 128), BF16),
            pltpu.VMEM((2, NZ, 16, 2 * LAT + 128), BF16),
            pltpu.VMEM((2, PAGE, WIDTH), BF16),
            pltpu.VMEM((2, 4, 2, WIDTH, KEYS), BF16),
            pltpu.VMEM((4, LAT, VDIM), BF16),
            pltpu.VMEM((4 * BEAM, MAXP), jnp.int32),
            pltpu.VMEM((4 * BEAM, MAXP), jnp.int32),
            pltpu.VMEM((4 * BEAM, 8 * KEYS), F32),
            pltpu.VMEM((2 * KEYS, 16 * KEYS), F32),
            pltpu.VMEM((2 * KEYS, 16 * KEYS), BF16),
            pltpu.VMEM((2, 2, KEYS, LAT), BF16),
            pltpu.VMEM((2, 2, 8, KEYS), F32),
            pltpu.VMEM((2, KEYS, LAT), BF16),
            pltpu.VMEM((2, 8, KEYS), F32),
            pltpu.VMEM((NZ - 1, 16, LAT), BF16),
            pltpu.VMEM((2, NZ, 1, KEYS), F32),
            pltpu.VMEM((NZ - 1, 1, KEYS), F32),
            pltpu.VMEM((NZ + 1, 16, LAT), BF16),
            pltpu.VMEM((NZ + 1, 1, KEYS), F32),
            pltpu.VMEM((NZ + 1, 16, LAT), BF16),
            pltpu.VMEM((NZ + 1, 1, KEYS), F32),
            pltpu.VMEM((16, VDIM), BF16),
            dma((8,)), dma((3, 3)), dma((3, 3)), dma((4, 3)), dma((4, 3)), dma, dma, dma((2, NZ)), dma((2, NZ)),
            dma((2, 3)), dma((2, 3)), dma((NZ - 1, 2)), dma((NZ - 1, 2)), dma((NZ + 1, 2)), dma((NZ + 1, 2)), dma((7,)), dma((7,)),
        ],
        compiler_params=pltpu.CompilerParams(
            collective_id=0, has_side_effects=True, vmem_limit_bytes=48 * 2**20
        ),
    )(
        *[pltpu.with_memory_space_constraint(operand, pltpu.HBM) for operand in operands]
    )
    return result.reshape(32, 4, VDIM)


def solution(mesh):
    return jax.shard_map(
        body,
        mesh=mesh,
        in_specs=(
            P(None, "head", None),
            P(None, ("seq", "head"), None),
            P(("seq", "head"), None, None),
            P("head", None, None),
            P(),
            P(),
            P(),
        ),
        out_specs=P(None, "head", None),
        check_vma=False,
    )
```

```python
import jax
import jax.numpy as jnp
from jax import lax
from jax.experimental import pallas as pl
from jax.experimental.pallas import tpu as pltpu
from jax.sharding import PartitionSpec as P

LAT = 512
ROPE = 64
WIDTH = LAT + ROPE
VDIM = 128
BEAM = 8
PAGE = 64
MAXP = 64
NZ = 8
RELATIVE = (4, 3, 5, 2, 6, 1, 7, 0)
CHUNKS = 2
CHUNK = 128 // CHUNKS
SLOT = {dz: k for k, dz in enumerate(RELATIVE)}
KEYS = 128
LOG2E = 1.4426950408889634
RATE = (VDIM + ROPE) ** -0.5 * LOG2E
LOWEST = -3.0e38
MESH = pl.DeviceIdType.MESH
F32 = jnp.float32
BF16 = jnp.bfloat16


def place(x, y, z, c):
    return ((y % 2) * 4 + x, z * 4 + (y // 2) * 2 + c)


def merge(parts, stats):
    peak = stats[0][0]
    for other, _ in stats[1:]:
        peak = jnp.maximum(peak, other)
    total = jnp.zeros_like(peak)
    latent = jnp.zeros((peak.shape[0], LAT), F32)
    for part, (part_peak, part_total) in zip(parts, stats):
        keep = jnp.exp2((part_peak - peak) * RATE)
        total = total + part_total * keep
        latent = latent + part[:, :LAT].astype(F32) * keep
    return peak, total, latent


def lines(peak, total):
    rows = peak.shape[0]
    lane = lax.broadcasted_iota(jnp.int32, (rows, KEYS), 1)
    row = lax.broadcasted_iota(jnp.int32, (rows, KEYS), 0) % 16
    spread = jnp.where(lane == row, peak, 0.0) + jnp.where(lane == row + 16, total, 0.0)
    return jnp.sum(spread.reshape(rows // 16, 16, KEYS), axis=1, keepdims=True)


def from_line(line):
    lane = lax.broadcasted_iota(jnp.int32, (16, KEYS), 1)
    row = lax.broadcasted_iota(jnp.int32, (16, KEYS), 0)
    return (
        jnp.sum(jnp.where(lane == row, line, 0.0), axis=1, keepdims=True),
        jnp.sum(jnp.where(lane == row + 16, line, 0.0), axis=1, keepdims=True))


def kernel(
    parents_hbm, lengths_hbm, lists_hbm, queries, prompt, pool, value_up,
    out,
    parents, lengths, page_lists,
    q_in, q_wide, q_mirror, q_buf, pool_in, keys, v_buf, lists, room, cap, scores, probs,
    part, stat, rs1, rs1_stat, zs, zs_stat_src, zs_stat, rs2_src, rs2_stat_src, rs2, rs2_stat, out_src,
    local_sem, key_send, key_recv, core_send, core_recv, swap_send, swap_recv, q_send, q_recv,
    rs1_send, rs1_recv, zs_send, zs_recv, rs2_send, rs2_recv, out_send, out_recv,
):
    seq = lax.axis_index("seq")
    head = lax.axis_index("head")
    x = seq % 4
    y_lo = seq // 4
    c = head % 2
    y_hi = (head // 2) % 2
    z = head // 4
    y = y_hi * 2 + y_lo
    x_hi = x // 2
    x_lo = x % 2
    step = 1 - 2 * c
    request = x_lo * 2 + y_lo

    def shifted(dx, dy, sign=1):
        return place((x + sign * dx + 4) % 4, (y + sign * dy + 4) % 4, z, c)

    other_core = place(x, y, z, 1 - c)
    mirror = place(x, 3 - y, z, c)
    key_moves = ((1, 0), (0, 1), (1, 1))
    scatter_moves = ((0, 2), (2, 0))
    out_moves = [(dx, dy) for dy in range(2) for dx in range(4) if (dx, dy) != (0, 0)]

    def out_place(dx, dy):
        return place((x + dx) % 4, y_hi * 2 + (y_lo + dy) % 2, z, c)

    barrier = pltpu.get_barrier_semaphore()
    senders = [place(x, y, (z + dz) % NZ, c) for dz in (2, 6, 1, 7)]
    senders += [shifted(dx * step, dy * step, -1) for dx, dy in key_moves]
    senders += [shifted(dx, dy) for dx, dy in scatter_moves]
    senders += [mirror, other_core]
    for sender in senders:
        pl.semaphore_signal(barrier, inc=1, device_id=sender, device_id_type=MESH)

    mirror_request = x_lo * 2 + 1 - y_lo
    own_q = pltpu.make_async_copy(queries.at[pl.ds(request * BEAM, BEAM)], q_in.at[0], local_sem.at[0])
    mirror_q = pltpu.make_async_copy(queries.at[pl.ds(mirror_request * BEAM, BEAM)], q_in.at[1], local_sem.at[1])
    own_pool = pltpu.make_async_copy(pool, pool_in, local_sem.at[2])
    own_prompt = pltpu.make_async_copy(prompt.at[request], keys.at[c, 0, 0], local_sem.at[3])
    own_v = pltpu.make_async_copy(value_up, v_buf, local_sem.at[4])
    get_parents = pltpu.make_async_copy(parents_hbm, parents, local_sem.at[5])
    get_lengths = pltpu.make_async_copy(lengths_hbm, lengths, local_sem.at[6])
    get_lists = pltpu.make_async_copy(lists_hbm, page_lists, local_sem.at[7])
    own_q.start()
    mirror_q.start()
    own_pool.start()
    own_prompt.start()
    get_parents.start()
    get_lengths.start()
    get_lists.start()
    own_v.start()

    def packed(i):
        for b in range(BEAM):
            block = q_in[i, b].astype(F32)
            half, start = b // 4, b % 4 * 4
            q_wide[i, start : start + 4, half * LAT : (half + 1) * LAT] = block[:, :LAT]
            if half:
                rotary = jnp.concatenate([q_in[i, b - 4].astype(F32)[:, LAT:], block[:, LAT:]], axis=1)
                q_wide[i, start : start + 4, 2 * LAT :] = rotary
        return q_wide[i].astype(BF16)

    mirror_q.wait()
    q_mirror[...] = packed(1)
    own_q.wait()
    q_buf[y_hi, SLOT[0]] = packed(0)
    own_pool.wait()
    flat_pool = pool_in[...].reshape(KEYS, WIDTH)
    keys[c, 0, 1, :LAT] = flat_pool[:, :LAT].T
    keys[c, 0, 1, LAT:] = flat_pool[:, LAT:].T

    pl.semaphore_wait(barrier, len(senders))

    copies = []

    def send(src, dst, send_sem, recv_sem, target):
        copy = pltpu.make_async_remote_copy(
            src_ref=src, dst_ref=dst, send_sem=send_sem, recv_sem=recv_sem, device_id=target, device_id_type=MESH
        )
        copy.start()
        copies.append(copy)
        return copy

    swap = send(q_mirror, q_buf.at[y_hi, SLOT[0]], swap_send, swap_recv, mirror)
    q_copies = {}

    def along_z(group, source, dz, slot):
        side = (y_hi + group) % 2
        q_copies[group, slot] = send(
            q_buf.at[side, source], q_buf.at[side, slot],
            q_send.at[group, slot], q_recv.at[group, slot], place(x, y, (z + dz + NZ) % NZ, c))

    def first_step(group):
        for dz in (2, 6, 1, 7):
            along_z(group, SLOT[0], dz, SLOT[NZ - dz])

    def second_step(group):
        q_copies[group, SLOT[6]].wait_recv()
        q_copies[group, SLOT[2]].wait_recv()
        along_z(group, SLOT[6] + c * (SLOT[2] - SLOT[6]), 2 * step, SLOT[4])
        along_z(group, SLOT[6], 1, SLOT[5])
        along_z(group, SLOT[2], -1, SLOT[3])

    def wait_queries(group):
        for dz in (1, 7, 3, 5, 4):
            q_copies[group, SLOT[dz]].wait_recv()

    first_step(0)
    pieces = ((0, slice(0, WIDTH)), (1, slice(0, WIDTH // 2)), (1, slice(WIDTH // 2, WIDTH)))
    key_copies = {}

    def key_piece(kind, piece):
        pooled, rows = pieces[piece]
        dx, dy = key_moves[kind - 1]
        target_request = (x_lo + dx) % 2 * 2 + (y_lo + dy) % 2
        key_copies[kind, piece] = send(
            keys.at[c, 0, 1, rows] if pooled else prompt.at[target_request], keys.at[c, kind, pooled, rows],
            key_send.at[kind - 1, piece], key_recv.at[kind - 1, piece], shifted(dx * step, dy * step))

    core_copies = {}

    def to_core(kind, piece):
        pooled, rows = pieces[piece]
        core_copies[kind, piece] = send(
            keys.at[c, kind, pooled, rows], keys.at[c, kind, pooled, rows],
            core_send.at[kind, piece], core_recv.at[kind, piece], other_core)

    def wait_core(piece):
        for kind in range(4):
            core_copies[kind, piece].wait_recv()

    for kind in range(1, 4):
        key_piece(kind, 0)
    for piece in (1, 2):
        for kind in range(1, 4):
            key_piece(kind, piece)
    own_prompt.wait()
    for piece in range(3):
        to_core(0, piece)

    get_parents.wait()
    get_lengths.wait()
    get_lists.wait()
    slot = lax.broadcasted_iota(jnp.int32, (4, MAXP), 1)
    for b in range(BEAM):
        parent = parents[request * BEAM + b]
        lists[4 * b : 4 * b + 4, :] = jnp.broadcast_to(page_lists[pl.ds(parent, 1), :], (4, MAXP))
        room[4 * b : 4 * b + 4, :] = jnp.clip(lengths[parent] - slot * PAGE, 0, PAGE)
    chosen = lists[...]
    space = room[...]
    lane = lax.broadcasted_iota(jnp.int32, (4 * BEAM, KEYS), 1)
    for cc in range(2):
        sign = 1 - 2 * cc
        for kind, (dx, dy) in enumerate(((0, 0),) + key_moves):
            sy = (y - sign * dy + 4) % 4
            s_seq, s_head = place((x - sign * dx + 4) % 4, sy, z, cc)
            page = (s_seq * 32 + s_head) * 2
            live = [
                jnp.sum(jnp.where(chosen == page + i, space, 0), axis=1, keepdims=True) for i in range(2)
            ]
            seen = lane < jnp.where(lane < PAGE, live[0], live[1] + PAGE)
            cap[:, (cc * 4 + kind) * KEYS : (cc * 4 + kind + 1) * KEYS] = jnp.where(seen, jnp.inf, -jnp.inf)

    swap.wait_recv()
    first_step(1)
    second_step(0)
    for kind in range(1, 4):
        key_copies[kind, 0].wait_recv()
        to_core(kind, 0)
    second_step(1)
    for kind in range(1, 4):
        key_copies[kind, 1].wait_recv()
        to_core(kind, 1)

    def attend(group, pooled):
        block = q_buf[group].reshape(KEYS, 2 * LAT + 128)
        rotary = block[:, 2 * LAT :]
        lane = lax.broadcasted_iota(jnp.int32, (KEYS, 128), 1)
        rows = jnp.concatenate([
            jnp.concatenate([block[:, :LAT], jnp.where(lane < ROPE, rotary, 0)], axis=1),
            jnp.concatenate([block[:, LAT : 2 * LAT], jnp.where(lane < ROPE, 0, rotary)], axis=1),
        ], axis=0)
        for pair in range(4):
            cc, kind = pair // 2, pair % 2 * 2
            columns = jnp.concatenate([keys[cc, kind, pooled], keys[cc, kind + 1, pooled]], axis=1)
            columns = jnp.concatenate([columns, columns[LAT:]], axis=0)
            raw = jnp.dot(rows, columns, preferred_element_type=F32)
            if pooled:
                limit = cap[:, 2 * pair * KEYS : 2 * (pair + 1) * KEYS].reshape(2, 1, 16, 2 * KEYS)
                raw = jnp.minimum(raw.reshape(2, NZ, 16, 2 * KEYS), limit).reshape(2 * KEYS, 2 * KEYS)
            scores[:, 2 * pair * KEYS : 2 * (pair + 1) * KEYS] = raw
        peak = jnp.max(scores[...], axis=1, keepdims=True)
        if pooled:
            peak = jnp.maximum(peak, LOWEST)
        weights = jnp.exp2((scores[...] - peak) * RATE)
        total = jnp.sum(weights, axis=1, keepdims=True)
        probs[...] = weights.astype(BF16)
        values = jnp.concatenate([keys[cc, kind, pooled, :LAT] for cc in range(2) for kind in range(4)], axis=1)
        latent = lax.dot_general(
            probs[...], values, (((1,), (1,)), ((), ())), preferred_element_type=F32)
        return peak, total, latent

    def finish(group, first, z_first):
        peak1, total1, latent1 = first
        peak2, total2, latent2 = attend(group, 1)
        peak = jnp.maximum(peak1, peak2)
        keep1 = jnp.exp2((peak1 - peak) * RATE)
        keep2 = jnp.exp2((peak2 - peak) * RATE)
        total = total1 * keep1 + total2 * keep2
        part[group] = (latent1 * keep1 + latent2 * keep2).astype(BF16).reshape(2, KEYS, LAT)
        lane = lax.broadcasted_iota(jnp.int32, (KEYS, 128), 1)
        for half in range(2):
            half_rows = slice(half * KEYS, (half + 1) * KEYS)
            stat[group, half] = jnp.where(lane == 0, peak[half_rows], total[half_rows]).T[:8]
            if z_first:
                zs_stat_src[half] = lines(peak[half_rows], total[half_rows])

    def scatter(i, group, half):
        target = shifted(*scatter_moves[i])
        rs1_copies[i, CHUNKS] = send(
            stat.at[group, half], rs1_stat.at[i], rs1_send.at[i, CHUNKS], rs1_recv.at[i, CHUNKS], target)
        for chunk in range(CHUNKS):
            rows = pl.ds(CHUNK * chunk, CHUNK)
            rs1_copies[i, chunk] = send(
                part.at[group, half, rows], rs1.at[i, rows], rs1_send.at[i, chunk], rs1_recv.at[i, chunk], target)

    rs1_copies = {}
    zs_copies = []
    wait_queries(0)
    wait_core(0)
    prompt_a = attend(y_hi, 0)
    for kind in range(1, 4):
        key_copies[kind, 2].wait_recv()
        to_core(kind, 2)
    wait_queries(1)
    prompt_b = attend(1 - y_hi, 0)
    wait_core(1)
    wait_core(2)
    finish(y_hi, prompt_a, True)
    for slot in range(NZ - 1):
        target = place(x, y, (z + RELATIVE[slot]) % NZ, c)
        zs_copies.append(send(
            part.at[y_hi, 1 - x_hi, pl.ds(16 * slot, 16)], zs.at[slot], zs_send.at[slot, 0], zs_recv.at[slot, 0], target))
        zs_copies.append(send(
            zs_stat_src.at[1 - x_hi, slot], zs_stat.at[slot], zs_send.at[slot, 1], zs_recv.at[slot, 1], target))
    scatter(0, y_hi, x_hi)
    finish(1 - y_hi, prompt_b, False)
    scatter(1, 1 - y_hi, 1 - x_hi)

    rs2_copies = []

    def home(slot, target):
        rs2_copies.append(send(
            rs2_src.at[slot], rs2.at[slot], rs2_send.at[slot, 0], rs2_recv.at[slot, 0], target))
        rs2_copies.append(send(
            rs2_stat_src.at[slot], rs2_stat.at[slot], rs2_send.at[slot, 1], rs2_recv.at[slot, 1], target))

    for i in range(2):
        rs1_copies[i, CHUNKS].wait_recv()
    columns = jnp.concatenate([
        stat[1 - y_hi, x_hi], rs1_stat[0], rs1_stat[1], jnp.zeros((KEYS - 24, KEYS), F32)], axis=0).T
    per = CHUNK // 16
    for chunk in range(CHUNKS):
        rows = slice(chunk * CHUNK, (chunk + 1) * CHUNK)
        for i in range(2):
            rs1_copies[i, chunk].wait_recv()
        peak, total, latent = merge(
            [part[1 - y_hi, x_hi, rows], rs1[0, rows], rs1[1, rows]],
            [(columns[rows, 8 * i : 8 * i + 1], columns[rows, 8 * i + 1 : 8 * i + 2]) for i in range(3)])
        rs2_src[per * chunk : per * chunk + per] = latent.astype(BF16).reshape(per, 16, LAT)
        rs2_stat_src[per * chunk : per * chunk + per] = lines(peak, total)
        for slot in range(per * chunk, per * chunk + per):
            home(slot, place(x, 3 - y, (z + RELATIVE[slot]) % NZ, c))
    for copy in zs_copies:
        copy.wait_recv()
    peak, total, latent = merge(
        [part[y_hi, 1 - x_hi, 16 * SLOT[0] :]] + [zs[slot] for slot in range(NZ - 1)],
        [from_line(zs_stat_src[1 - x_hi, SLOT[0]])] + [from_line(zs_stat[slot]) for slot in range(NZ - 1)])
    rs2_src[NZ] = latent.astype(BF16)
    rs2_stat_src[NZ : NZ + 1] = lines(peak, total)
    home(NZ, place((x + 2) % 4, y_hi * 2 + 1 - y_lo, z, c))
    own_v.wait()
    for copy in rs2_copies:
        copy.wait_recv()
    peak, total, latent = merge([rs2[slot] for slot in range(NZ + 1)], [from_line(rs2_stat[slot]) for slot in range(NZ + 1)])
    latent = (latent / total).astype(BF16)
    attended = jnp.zeros((16, VDIM), F32)
    row = lax.broadcasted_iota(jnp.int32, (16, VDIM), 0)
    for h in range(4):
        product = jnp.dot(latent, v_buf[h], preferred_element_type=F32)
        attended = jnp.where(row % 4 == h, product, attended)
    out_src[...] = attended.astype(BF16)
    place_out = mirror_request * 2 + x_hi
    out_copies = []
    for i, (dx, dy) in enumerate(out_moves):
        out_copies.append(send(
            out_src, out.at[place_out], out_send.at[i], out_recv.at[i], out_place(dx, dy)))
    out[place_out] = out_src[...]
    for copy in out_copies:
        copy.wait_recv()
    for copy in copies:
        copy.wait_send()


def body(queries, prompt_latent, pool_latent, value_up, parents, page_lists, lengths):
    vmem = pl.BlockSpec(memory_space=pltpu.VMEM)
    hbm = pl.BlockSpec(memory_space=pltpu.HBM)
    operands = (parents, lengths, page_lists, queries, prompt_latent.swapaxes(1, 2), pool_latent, value_up)
    dma = pltpu.SemaphoreType.DMA
    result = pl.pallas_call(
        kernel,
        out_shape=pltpu.VMEM((8, 16, VDIM), BF16),
        in_specs=[hbm] * 7,
        out_specs=vmem,
        scratch_shapes=[
            pltpu.SMEM((32,), jnp.int32),
            pltpu.SMEM((32,), jnp.int32),
            pltpu.VMEM((32, MAXP), jnp.int32),
            pltpu.VMEM((2, BEAM, 4, WIDTH), BF16),
            pltpu.VMEM((2, 16, 2 * LAT + 128), F32),
            pltpu.VMEM((16, 2 * LAT + 128), BF16),
            pltpu.VMEM((2, NZ, 16, 2 * LAT + 128), BF16),
            pltpu.VMEM((2, PAGE, WIDTH), BF16),
            pltpu.VMEM((2, 4, 2, WIDTH, KEYS), BF16),
            pltpu.VMEM((4, LAT, VDIM), BF16),
            pltpu.VMEM((4 * BEAM, MAXP), jnp.int32),
            pltpu.VMEM((4 * BEAM, MAXP), jnp.int32),
            pltpu.VMEM((4 * BEAM, 8 * KEYS), F32),
            pltpu.VMEM((2 * KEYS, 8 * KEYS), F32),
            pltpu.VMEM((2 * KEYS, 8 * KEYS), BF16),
            pltpu.VMEM((2, 2, KEYS, LAT), BF16),
            pltpu.VMEM((2, 2, 8, KEYS), F32),
            pltpu.VMEM((2, KEYS, LAT), BF16),
            pltpu.VMEM((2, 8, KEYS), F32),
            pltpu.VMEM((NZ - 1, 16, LAT), BF16),
            pltpu.VMEM((2, NZ, 1, KEYS), F32),
            pltpu.VMEM((NZ - 1, 1, KEYS), F32),
            pltpu.VMEM((NZ + 1, 16, LAT), BF16),
            pltpu.VMEM((NZ + 1, 1, KEYS), F32),
            pltpu.VMEM((NZ + 1, 16, LAT), BF16),
            pltpu.VMEM((NZ + 1, 1, KEYS), F32),
            pltpu.VMEM((16, VDIM), BF16),
            dma((8,)), dma((3, 3)), dma((3, 3)), dma((4, 3)), dma((4, 3)), dma, dma, dma((2, NZ)), dma((2, NZ)),
            dma((2, CHUNKS + 1)), dma((2, CHUNKS + 1)), dma((NZ - 1, 2)), dma((NZ - 1, 2)), dma((NZ + 1, 2)), dma((NZ + 1, 2)), dma((7,)), dma((7,)),
        ],
        compiler_params=pltpu.CompilerParams(
            collective_id=0, has_side_effects=True, vmem_limit_bytes=48 * 2**20
        ),
    )(
        *[pltpu.with_memory_space_constraint(operand, pltpu.HBM) for operand in operands]
    )
    return result.reshape(32, 4, VDIM)


def solution(mesh):
    return jax.shard_map(
        body,
        mesh=mesh,
        in_specs=(
            P(None, "head", None),
            P(None, ("seq", "head"), None),
            P(("seq", "head"), None, None),
            P("head", None, None),
            P(),
            P(),
            P(),
        ),
        out_specs=P(None, "head", None),
        check_vma=False,
    )
```

```python
import jax
import jax.numpy as jnp
from jax import lax
from jax.experimental import pallas as pl
from jax.experimental.pallas import tpu as pltpu
from jax.sharding import PartitionSpec as P

LAT = 512
ROPE = 64
WIDTH = LAT + ROPE
VDIM = 128
BEAM = 8
PAGE = 64
MAXP = 64
NZ = 8
RELATIVE = (4, 3, 5, 2, 6, 1, 7, 0)
BLOCK = 32
ROWS = 256
SLOT = {dz: k for k, dz in enumerate(RELATIVE)}
KEYS = 128
LOG2E = 1.4426950408889634
RATE = (VDIM + ROPE) ** -0.5 * LOG2E
LOWEST = -3.0e38
MESH = pl.DeviceIdType.MESH
F32 = jnp.float32
BF16 = jnp.bfloat16


def place(x, y, z, c):
    return ((y % 2) * 4 + x, z * 4 + (y // 2) * 2 + c)


def merge(parts, stats):
    peak = stats[0][0]
    for other, _ in stats[1:]:
        peak = jnp.maximum(peak, other)
    total = jnp.zeros_like(peak)
    latent = jnp.zeros((peak.shape[0], LAT), F32)
    for part, (part_peak, part_total) in zip(parts, stats):
        keep = jnp.exp2((part_peak - peak) * RATE)
        total = total + part_total * keep
        latent = latent + part[:, :LAT].astype(F32) * keep
    return peak, total, latent


def lines(peak, total):
    rows = peak.shape[0]
    lane = lax.broadcasted_iota(jnp.int32, (rows, KEYS), 1)
    row = lax.broadcasted_iota(jnp.int32, (rows, KEYS), 0) % BLOCK
    spread = jnp.where(lane == row, peak, 0.0) + jnp.where(lane == row + BLOCK, total, 0.0)
    return jnp.sum(spread.reshape(rows // BLOCK, BLOCK, KEYS), axis=1, keepdims=True)


def from_line(line):
    lane = lax.broadcasted_iota(jnp.int32, (BLOCK, KEYS), 1)
    row = lax.broadcasted_iota(jnp.int32, (BLOCK, KEYS), 0)
    return (
        jnp.sum(jnp.where(lane == row, line, 0.0), axis=1, keepdims=True),
        jnp.sum(jnp.where(lane == row + BLOCK, line, 0.0), axis=1, keepdims=True))


def kernel(
    parents_hbm, lengths_hbm, lists_hbm, queries, prompt, pool, value_up,
    out,
    parents, lengths, page_lists,
    q_in, q_wide, q_mirror, q_own, q_buf, pool_in, pool_flat, keys, v_buf, lists, room, cap, scores, probs,
    part, stat, rs1, rs1_stat, zs, zs_stat_src, zs_stat, rs2_src, rs2_stat_src, rs2, rs2_stat, out_src,
    local_sem, key_send, key_recv, swap_send, swap_recv, q_send, q_recv, next_send, next_recv, v_send, v_recv,
    rs1_send, rs1_recv, zs_send, zs_recv, rs2_send, rs2_recv, out_send, out_recv,
):
    seq = lax.axis_index("seq")
    head = lax.axis_index("head")
    x = seq % 4
    y_lo = seq // 4
    c = head % 2
    y_hi = (head // 2) % 2
    z = head // 4
    y = y_hi * 2 + y_lo
    x_hi = x // 2
    x_lo = x % 2
    request = x_lo * 2 + y_lo
    mirror_request = x_lo * 2 + 1 - y_lo

    def shifted(dx, dy, core=1):
        return place((x + dx + 4) % 4, (y + dy + 4) % 4, z, core)

    def up(dz, core=1):
        return place(x, y, (z + dz + NZ) % NZ, core)

    worker = place(x, y, z, 1)
    key_moves = ((0, 0), (1, 0), (0, 1), (1, 1))
    scatter_moves = ((0, 2), (2, 0))
    out_moves = [(dx, dy) for dy in range(2) for dx in range(4)]

    def out_place(dx, dy, core):
        return place((x + dx) % 4, y_hi * 2 + (y_lo + dy) % 2, z, core)

    barrier = pltpu.get_barrier_semaphore()

    @pl.when(c == 1)
    def _():
        senders = [up(dz, core) for core in range(2) for dz in (2, 6, 1, 7)]
        senders += [
            shifted(-dx * (1 - 2 * core), -dy * (1 - 2 * core), core) for core in range(2) for dx, dy in key_moves[1:]]
        senders += [place(x, 3 - y, z, core) for core in range(2)]
        senders += [shifted(dx, dy) for dx, dy in scatter_moves]
        senders += [place(x, y, z, 0)]
        for sender in senders:
            pl.semaphore_signal(barrier, inc=1, device_id=sender, device_id_type=MESH)

    own_q = pltpu.make_async_copy(queries.at[pl.ds(request * BEAM, BEAM)], q_in.at[0], local_sem.at[0])
    mirror_q = pltpu.make_async_copy(queries.at[pl.ds(mirror_request * BEAM, BEAM)], q_in.at[1], local_sem.at[1])
    own_pool = pltpu.make_async_copy(pool, pool_in, local_sem.at[2])
    own_prompt = pltpu.make_async_copy(prompt.at[request], keys.at[1, 0, 0], local_sem.at[3])
    own_v = pltpu.make_async_copy(value_up, v_buf.at[1], local_sem.at[4])
    get_parents = pltpu.make_async_copy(parents_hbm, parents, local_sem.at[5])
    get_lengths = pltpu.make_async_copy(lengths_hbm, lengths, local_sem.at[6])
    get_lists = pltpu.make_async_copy(lists_hbm, page_lists, local_sem.at[7])
    own_q.start()
    mirror_q.start()
    own_pool.start()

    @pl.when(c == 1)
    def _():
        own_prompt.start()
        get_parents.start()
        get_lengths.start()
        get_lists.start()
        own_v.start()

    def packed(i):
        for b in range(BEAM):
            block = q_in[i, b].astype(F32)
            half, start = b // 4, b % 4 * 4
            q_wide[i, start : start + 4, half * LAT : (half + 1) * LAT] = block[:, :LAT]
            if half:
                rotary = jnp.concatenate([q_in[i, b - 4].astype(F32)[:, LAT:], block[:, LAT:]], axis=1)
                q_wide[i, start : start + 4, 2 * LAT :] = rotary
        return q_wide[i].astype(BF16)

    mirror_q.wait()
    q_mirror[...] = packed(1)
    own_q.wait()
    q_own[...] = packed(0)
    own_pool.wait()
    flat_pool = pool_in[...].reshape(KEYS, WIDTH)
    pool_flat[:LAT] = flat_pool[:, :LAT].T
    pool_flat[LAT:] = flat_pool[:, LAT:].T

    @pl.when(c == 1)
    def _():
        q_buf[y_hi, SLOT[0], 1] = q_own[...]
        keys[1, 0, 1] = pool_flat[...]
        pl.semaphore_wait(barrier, 10)

    @pl.when(c == 0)
    def _():
        pl.semaphore_wait(barrier, 9)

    copies = []

    def describe(src, dst, send_sem, recv_sem, target):
        return pltpu.make_async_remote_copy(
            src_ref=src, dst_ref=dst, send_sem=send_sem, recv_sem=recv_sem, device_id=target, device_id_type=MESH)

    def send(*what):
        copy = describe(*what)
        copy.start()
        copies.append(copy)
        return copy

    step = 1 - 2 * c
    send(q_mirror, q_buf.at[y_hi, SLOT[0], c], swap_send, swap_recv.at[c], place(x, 3 - y, z, 1))
    for i, dz in enumerate((2, 6, 1, 7)):
        slot = SLOT[NZ - dz]
        send(q_own, q_buf.at[y_hi, slot, c], q_send.at[i], q_recv.at[c, slot], up(dz))
    pieces = ((0, slice(0, WIDTH)), (1, slice(0, WIDTH // 2)), (1, slice(WIDTH // 2, WIDTH)))

    def key_piece(kind, piece, target):
        pooled, rows = pieces[piece]
        dx, dy = key_moves[kind]
        target_request = (x_lo + dx) % 2 * 2 + (y_lo + dy) % 2
        return describe(
            pool_flat.at[rows] if pooled else prompt.at[target_request], keys.at[c, kind, pooled, rows],
            key_send.at[kind, piece], key_recv.at[c, kind, piece], target)

    for piece in range(3):
        for kind in (3, 1, 2):
            dx, dy = key_moves[kind]
            copy = key_piece(kind, piece, shifted(dx * step, dy * step))
            copy.start()
            copies.append(copy)

    @pl.when(c == 0)
    def _():
        mine = [describe(q_own, q_buf.at[y_hi, SLOT[0], 0], q_send.at[4], q_recv.at[0, SLOT[0]], worker)]
        mine += [key_piece(0, piece, worker) for piece in range(3)]
        mine += [describe(value_up, v_buf.at[0], v_send, v_recv, worker)]
        for copy in mine:
            copy.start()
        for i in range(8):
            describe(out_src.at[0], out.at[0], v_send, out_recv.at[i], worker).wait_recv()
        for copy in mine:
            copy.wait_send()

    @pl.when(c == 1)
    def _():
        work = []

        def post(*what):
            copy = describe(*what)
            copy.start()
            work.append(copy)
            return copy

        def arrived(dst, recv_sem):
            describe(dst, dst, v_send, recv_sem, place(x, y, z, 0)).wait_recv()

        def along_z(group, source, dz, slot):
            side = (y_hi + group) % 2
            post(
                q_buf.at[side, source], q_buf.at[side, slot],
                next_send.at[group, slot], next_recv.at[group, slot], up(dz))

        def await_slot(group, slot):
            side = (y_hi + group) % 2
            if group == 0 and slot not in (SLOT[3], SLOT[4], SLOT[5]):
                for core in range(2):
                    if core == 0 or slot != SLOT[0]:
                        arrived(q_buf.at[side, slot, core], q_recv.at[core, slot])
            else:
                arrived(q_buf.at[side, slot], next_recv.at[group, slot])

        def second_step(group):
            await_slot(group, SLOT[6])
            await_slot(group, SLOT[2])
            if group == 0:
                along_z(group, SLOT[6], 2, SLOT[4])
            else:
                along_z(group, SLOT[2], -2, SLOT[4])
            along_z(group, SLOT[6], 1, SLOT[5])
            along_z(group, SLOT[2], -1, SLOT[3])

        def await_keys(piece, own):
            pooled, rows = pieces[piece]
            for core in range(2):
                for kind in range(4):
                    if (kind == 0) == own and (core == 0 or kind > 0):
                        arrived(keys.at[core, kind, pooled, rows], key_recv.at[core, kind, piece])

        for core in range(2):
            arrived(q_buf.at[1 - y_hi, SLOT[0], core], swap_recv.at[core])
        for dz in (2, 6, 1, 7):
            along_z(1, SLOT[0], dz, SLOT[NZ - dz])
        second_step(0)

        get_parents.wait()
        get_lengths.wait()
        get_lists.wait()
        slot_index = lax.broadcasted_iota(jnp.int32, (4, MAXP), 1)
        for b in range(BEAM):
            parent = parents[request * BEAM + b]
            lists[4 * b : 4 * b + 4, :] = jnp.broadcast_to(page_lists[pl.ds(parent, 1), :], (4, MAXP))
            room[4 * b : 4 * b + 4, :] = jnp.clip(lengths[parent] - slot_index * PAGE, 0, PAGE)
        chosen = lists[...]
        space = room[...]
        lane = lax.broadcasted_iota(jnp.int32, (4 * BEAM, KEYS), 1)
        for core in range(2):
            sign = 1 - 2 * core
            for kind, (dx, dy) in enumerate(key_moves):
                s_seq, s_head = place((x - sign * dx + 4) % 4, (y - sign * dy + 4) % 4, z, core)
                page = (s_seq * 32 + s_head) * 2
                live = [
                    jnp.sum(jnp.where(chosen == page + i, space, 0), axis=1, keepdims=True) for i in range(2)]
                seen = lane < jnp.where(lane < PAGE, live[0], live[1] + PAGE)
                cap[core, kind] = jnp.where(seen, jnp.inf, -jnp.inf)

        def attend(group, half, blocks):
            block = q_buf[(y_hi + group) % 2].reshape(ROWS, 2 * LAT + 128)
            rotary = block[:, 2 * LAT :]
            upper = jnp.where(lax.broadcasted_iota(jnp.int32, (ROWS, 128), 1) < ROPE, 0, 1)
            rows = jnp.concatenate([
                jnp.where(half == 0, block[:, :LAT], block[:, LAT : 2 * LAT]),
                jnp.where(upper == half, rotary, 0)], axis=1)
            many = len(blocks) * KEYS
            for i in range(0, len(blocks), 2):
                two = blocks[i : i + 2]
                columns = jnp.concatenate([keys[k] for k in two], axis=1)
                columns = jnp.concatenate([columns, columns[LAT:]], axis=0)
                raw = jnp.dot(rows, columns, preferred_element_type=F32)
                if two[0][2]:
                    limit = jnp.concatenate([cap[core, kind, pl.ds(16 * half, 16)] for core, kind, _ in two], axis=1)
                    raw = jnp.minimum(raw.reshape(2 * NZ, 16, 2 * KEYS), limit[None]).reshape(ROWS, 2 * KEYS)
                scores[:, i * KEYS : (i + 2) * KEYS] = raw
            peak = jnp.maximum(jnp.max(scores[:, :many], axis=1, keepdims=True), LOWEST)
            weights = jnp.exp2((scores[:, :many] - peak) * RATE)
            total = jnp.sum(weights, axis=1, keepdims=True)
            probs[:, :many] = weights.astype(BF16)
            values = jnp.concatenate([keys[core, kind, pooled, :LAT] for core, kind, pooled in blocks], axis=1)
            latent = lax.dot_general(
                probs[:, :many], values, (((1,), (1,)), ((), ())), preferred_element_type=F32)
            return peak, total, latent

        def store(group, half, result, in_lines):
            peak, total, latent = result
            side = (y_hi + group) % 2
            part[side, half] = latent.astype(BF16)
            if in_lines:
                zs_stat_src[...] = lines(peak, total)
            else:
                first = lax.broadcasted_iota(jnp.int32, (KEYS, KEYS), 1) == 0
                for i in range(2):
                    rows = slice(i * KEYS, (i + 1) * KEYS)
                    stat[side, half, i] = jnp.where(first, peak[rows], total[rows]).T[:8]

        def both(one, two):
            peak1, total1, latent1 = one
            peak2, total2, latent2 = two
            peak = jnp.maximum(peak1, peak2)
            keep1 = jnp.exp2((peak1 - peak) * RATE)
            keep2 = jnp.exp2((peak2 - peak) * RATE)
            return peak, total1 * keep1 + total2 * keep2, latent1 * keep1 + latent2 * keep2

        early = [(core, kind, 0) for core in range(2) for kind in range(4)] + [(0, 0, 1), (1, 0, 1)]
        late = [(core, kind, 1) for core in range(2) for kind in range(1, 4)]
        rs1_copies = {}

        def scatter(i, group, half):
            target = shifted(*scatter_moves[i])
            side = (y_hi + group) % 2
            rs1_copies[i, 2] = post(
                stat.at[side, half], rs1_stat.at[i], rs1_send.at[i, 2], rs1_recv.at[i, 2], target)
            for chunk in range(2):
                rows = pl.ds(KEYS * chunk, KEYS)
                rs1_copies[i, chunk] = post(
                    part.at[side, half, rows], rs1.at[i, rows], rs1_send.at[i, chunk], rs1_recv.at[i, chunk], target)

        second_step(1)
        for slot in (SLOT[0], SLOT[1], SLOT[7], SLOT[3], SLOT[5], SLOT[4]):
            await_slot(0, slot)
        own_prompt.wait()
        for piece in range(3):
            await_keys(piece, True)
        await_keys(0, False)
        early_z = attend(0, 1 - x_hi, early)
        early_y = attend(0, x_hi, early)
        for slot in (SLOT[1], SLOT[7], SLOT[3], SLOT[5], SLOT[4]):
            await_slot(1, slot)
        early_x = attend(1, 1 - x_hi, early)
        await_keys(1, False)
        await_keys(2, False)
        store(0, 1 - x_hi, both(early_z, attend(0, 1 - x_hi, late)), True)
        zs_copies = []
        for slot in range(NZ - 1):
            target = up(RELATIVE[slot])
            zs_copies.append(post(
                part.at[y_hi, 1 - x_hi, pl.ds(BLOCK * slot, BLOCK)], zs.at[slot],
                zs_send.at[slot, 0], zs_recv.at[slot, 0], target))
            zs_copies.append(post(
                zs_stat_src.at[slot], zs_stat.at[slot], zs_send.at[slot, 1], zs_recv.at[slot, 1], target))
        store(0, x_hi, both(early_y, attend(0, x_hi, late)), False)
        scatter(0, 0, x_hi)
        store(1, 1 - x_hi, both(early_x, attend(1, 1 - x_hi, late)), False)
        scatter(1, 1, 1 - x_hi)
        store(1, x_hi, attend(1, x_hi, early + late), False)

        rs2_copies = []

        def home(slot, target):
            rs2_copies.append(post(
                rs2_src.at[slot], rs2.at[slot], rs2_send.at[slot, 0], rs2_recv.at[slot, 0], target))
            rs2_copies.append(post(
                rs2_stat_src.at[slot], rs2_stat.at[slot], rs2_send.at[slot, 1], rs2_recv.at[slot, 1], target))

        for i in range(2):
            rs1_copies[i, 2].wait_recv()
        for chunk in range(2):
            rows = slice(chunk * KEYS, (chunk + 1) * KEYS)
            for i in range(2):
                rs1_copies[i, chunk].wait_recv()
            columns = jnp.concatenate([
                stat[1 - y_hi, x_hi, chunk], rs1_stat[0, chunk], rs1_stat[1, chunk], jnp.zeros((KEYS - 24, KEYS), F32),
            ], axis=0).T
            peak, total, latent = merge(
                [part[1 - y_hi, x_hi, rows], rs1[0, rows], rs1[1, rows]],
                [(columns[:, 8 * i : 8 * i + 1], columns[:, 8 * i + 1 : 8 * i + 2]) for i in range(3)])
            rs2_src[4 * chunk : 4 * chunk + 4] = latent.astype(BF16).reshape(4, BLOCK, LAT)
            rs2_stat_src[4 * chunk : 4 * chunk + 4] = lines(peak, total)
            for slot in range(4 * chunk, 4 * chunk + 4):
                home(slot, place(x, 3 - y, (z + RELATIVE[slot]) % NZ, 1))
        for copy in zs_copies:
            copy.wait_recv()
        peak, total, latent = merge(
            [part[y_hi, 1 - x_hi, BLOCK * SLOT[0] :]] + [zs[slot] for slot in range(NZ - 1)],
            [from_line(zs_stat_src[SLOT[0]])] + [from_line(zs_stat[slot]) for slot in range(NZ - 1)])
        rs2_src[NZ] = latent.astype(BF16)
        rs2_stat_src[NZ : NZ + 1] = lines(peak, total)
        home(NZ, out_place(2, 1, 1))
        own_v.wait()
        arrived(v_buf.at[0], v_recv)
        for copy in rs2_copies:
            copy.wait_recv()
        peak, total, latent = merge(
            [rs2[slot] for slot in range(NZ + 1)], [from_line(rs2_stat[slot]) for slot in range(NZ + 1)])
        latent = (latent / total).astype(BF16)
        row = lax.broadcasted_iota(jnp.int32, (16, VDIM), 0)
        place_out = mirror_request * 2 + x_hi
        out_copies = []
        for core in range(2):
            attended = jnp.zeros((16, VDIM), F32)
            for h in range(4):
                product = jnp.dot(latent[16 * core : 16 * core + 16], v_buf[core, h], preferred_element_type=F32)
                attended = jnp.where(row % 4 == h, product, attended)
            out_src[core] = attended.astype(BF16)
            for i, (dx, dy) in enumerate(out_moves):
                if core == 0 or i > 0:
                    copy = post(
                        out_src.at[core], out.at[place_out], out_send.at[core, i], out_recv.at[i],
                        out_place(dx, dy, core))
                    if core == 1:
                        out_copies.append(copy)
        out[place_out] = out_src[1]
        for copy in out_copies:
            copy.wait_recv()
        for copy in work:
            copy.wait_send()

    for copy in copies:
        copy.wait_send()


def body(queries, prompt_latent, pool_latent, value_up, parents, page_lists, lengths):
    vmem = pl.BlockSpec(memory_space=pltpu.VMEM)
    hbm = pl.BlockSpec(memory_space=pltpu.HBM)
    operands = (parents, lengths, page_lists, queries, prompt_latent.swapaxes(1, 2), pool_latent, value_up)
    dma = pltpu.SemaphoreType.DMA
    result = pl.pallas_call(
        kernel,
        out_shape=pltpu.VMEM((8, 16, VDIM), BF16),
        in_specs=[hbm] * 7,
        out_specs=vmem,
        scratch_shapes=[
            pltpu.SMEM((32,), jnp.int32),
            pltpu.SMEM((32,), jnp.int32),
            pltpu.VMEM((32, MAXP), jnp.int32),
            pltpu.VMEM((2, BEAM, 4, WIDTH), BF16),
            pltpu.VMEM((2, 16, 2 * LAT + 128), F32),
            pltpu.VMEM((16, 2 * LAT + 128), BF16),
            pltpu.VMEM((16, 2 * LAT + 128), BF16),
            pltpu.VMEM((2, NZ, 2, 16, 2 * LAT + 128), BF16),
            pltpu.VMEM((2, PAGE, WIDTH), BF16),
            pltpu.VMEM((WIDTH, KEYS), BF16),
            pltpu.VMEM((2, 4, 2, WIDTH, KEYS), BF16),
            pltpu.VMEM((2, 4, LAT, VDIM), BF16),
            pltpu.VMEM((4 * BEAM, MAXP), jnp.int32),
            pltpu.VMEM((4 * BEAM, MAXP), jnp.int32),
            pltpu.VMEM((2, 4, 4 * BEAM, KEYS), F32),
            pltpu.VMEM((ROWS, 16 * KEYS), F32),
            pltpu.VMEM((ROWS, 16 * KEYS), BF16),
            pltpu.VMEM((2, 2, ROWS, LAT), BF16),
            pltpu.VMEM((2, 2, 2, 8, KEYS), F32),
            pltpu.VMEM((2, ROWS, LAT), BF16),
            pltpu.VMEM((2, 2, 8, KEYS), F32),
            pltpu.VMEM((NZ - 1, BLOCK, LAT), BF16),
            pltpu.VMEM((NZ, 1, KEYS), F32),
            pltpu.VMEM((NZ - 1, 1, KEYS), F32),
            pltpu.VMEM((NZ + 1, BLOCK, LAT), BF16),
            pltpu.VMEM((NZ + 1, 1, KEYS), F32),
            pltpu.VMEM((NZ + 1, BLOCK, LAT), BF16),
            pltpu.VMEM((NZ + 1, 1, KEYS), F32),
            pltpu.VMEM((2, 16, VDIM), BF16),
            dma((8,)), dma((4, 3)), dma((2, 4, 3)), dma, dma((2,)), dma((5,)), dma((2, NZ)), dma((2, NZ)), dma((2, NZ)),
            dma, dma, dma((2, 3)), dma((2, 3)), dma((NZ - 1, 2)), dma((NZ - 1, 2)), dma((NZ + 1, 2)), dma((NZ + 1, 2)),
            dma((2, 8)), dma((8,)),
        ],
        compiler_params=pltpu.CompilerParams(
            collective_id=0, has_side_effects=True, vmem_limit_bytes=48 * 2**20
        ),
    )(
        *[pltpu.with_memory_space_constraint(operand, pltpu.HBM) for operand in operands]
    )
    return result.reshape(32, 4, VDIM)


def solution(mesh):
    return jax.shard_map(
        body,
        mesh=mesh,
        in_specs=(
            P(None, "head", None),
            P(None, ("seq", "head"), None),
            P(("seq", "head"), None, None),
            P("head", None, None),
            P(),
            P(),
            P(),
        ),
        out_specs=P(None, "head", None),
        check_vma=False,
    )
```

```python
import jax
import jax.numpy as jnp
from jax import lax
from jax.experimental import pallas as pl
from jax.experimental.pallas import tpu as pltpu
from jax.sharding import PartitionSpec as P

LAT = 512
ROPE = 64
WIDTH = LAT + ROPE
VDIM = 128
BEAM = 8
PAGE = 64
MAXP = 64
NZ = 8
RELATIVE = (4, 3, 5, 2, 6, 1, 7, 0)
CHUNKS = 2
CHUNK = 128 // CHUNKS
SLOT = {dz: k for k, dz in enumerate(RELATIVE)}
KEYS = 128
LOG2E = 1.4426950408889634
RATE = (VDIM + ROPE) ** -0.5 * LOG2E
LOWEST = -3.0e38
MESH = pl.DeviceIdType.MESH
F32 = jnp.float32
BF16 = jnp.bfloat16


def place(x, y, z, c):
    return ((y % 2) * 4 + x, z * 4 + (y // 2) * 2 + c)


def merge(parts, stats):
    peak = stats[0][0]
    for other, _ in stats[1:]:
        peak = jnp.maximum(peak, other)
    total = jnp.zeros_like(peak)
    latent = jnp.zeros((peak.shape[0], LAT), F32)
    for part, (part_peak, part_total) in zip(parts, stats):
        keep = jnp.exp2((part_peak - peak) * RATE)
        total = total + part_total * keep
        latent = latent + part[:, :LAT].astype(F32) * keep
    return peak, total, latent


def lines(peak, total, start=0):
    rows = peak.shape[0]
    lane = lax.broadcasted_iota(jnp.int32, (rows, KEYS), 1) - start
    row = lax.broadcasted_iota(jnp.int32, (rows, KEYS), 0) % 16
    spread = jnp.where(lane == row, peak, 0.0) + jnp.where(lane == row + 16, total, 0.0)
    return jnp.sum(spread.reshape(rows // 16, 16, KEYS), axis=1, keepdims=True)


def from_line(line, start=0):
    lane = lax.broadcasted_iota(jnp.int32, (16, KEYS), 1) - start
    row = lax.broadcasted_iota(jnp.int32, (16, KEYS), 0)
    return (
        jnp.sum(jnp.where(lane == row, line, 0.0), axis=1, keepdims=True),
        jnp.sum(jnp.where(lane == row + 16, line, 0.0), axis=1, keepdims=True))


def kernel(
    parents_hbm, lengths_hbm, lists_hbm, queries, prompt, pool, value_up,
    out,
    parents, lengths, page_lists,
    q_in, q_wide, q_mirror, q_buf, pool_in, keys, v_buf, lists, room, cap, scores, probs,
    part, stat, rs1, rs1_stat, zs, zs_stat_src, zs_stat, rs2_src, rs2_stat_src, rs2, rs2_stat, out_src,
    local_sem, key_send, key_recv, core_send, core_recv, swap_send, swap_recv, q_send, q_recv,
    v_send, v_recv, rs1_send, rs1_recv, zs_send, zs_recv, rs2_send, rs2_recv, out_send, out_recv,
):
    seq = lax.axis_index("seq")
    head = lax.axis_index("head")
    x = seq % 4
    y_lo = seq // 4
    c = head % 2
    y_hi = (head // 2) % 2
    z = head // 4
    y = y_hi * 2 + y_lo
    x_hi = x // 2
    x_lo = x % 2
    step = 1 - 2 * c
    request = x_lo * 2 + y_lo

    def shifted(dx, dy, sign=1, core=c):
        return place((x + sign * dx + 4) % 4, (y + sign * dy + 4) % 4, z, core)

    other_core = place(x, y, z, 1 - c)
    mirror = place(x, 3 - y, z, c)
    key_moves = ((1, 0), (0, 1), (1, 1))
    scatter_moves = ((0, 2), (2, 0))
    out_moves = [(dx, dy) for dy in range(2) for dx in range(4)]

    def out_place(dx, dy, core):
        return place((x + dx) % 4, y_hi * 2 + (y_lo + dy) % 2, z, core)

    barrier = pltpu.get_barrier_semaphore()
    senders = [place(x, y, (z + dz) % NZ, c) for dz in (2, 6, 1, 7)]
    senders += [shifted(dx * step, dy * step, -1) for dx, dy in key_moves]
    senders += [shifted(dx, dy) for dx, dy in scatter_moves]
    senders += [mirror, other_core]
    for sender in senders:
        pl.semaphore_signal(barrier, inc=1, device_id=sender, device_id_type=MESH)

    mirror_request = x_lo * 2 + 1 - y_lo
    own_q = pltpu.make_async_copy(queries.at[pl.ds(request * BEAM, BEAM)], q_in.at[0], local_sem.at[0])
    mirror_q = pltpu.make_async_copy(queries.at[pl.ds(mirror_request * BEAM, BEAM)], q_in.at[1], local_sem.at[1])
    own_pool = pltpu.make_async_copy(pool, pool_in, local_sem.at[2])
    own_prompt = pltpu.make_async_copy(prompt.at[request], keys.at[c, 0, 0], local_sem.at[3])
    own_v = pltpu.make_async_copy(value_up, v_buf.at[1], local_sem.at[4])
    get_parents = pltpu.make_async_copy(parents_hbm, parents, local_sem.at[5])
    get_lengths = pltpu.make_async_copy(lengths_hbm, lengths, local_sem.at[6])
    get_lists = pltpu.make_async_copy(lists_hbm, page_lists, local_sem.at[7])
    own_q.start()
    mirror_q.start()
    own_pool.start()
    own_prompt.start()
    get_parents.start()
    get_lengths.start()
    get_lists.start()
    own_v.start()

    def packed(i):
        for b in range(BEAM):
            block = q_in[i, b].astype(F32)
            half, start = b // 4, b % 4 * 4
            q_wide[i, start : start + 4, half * LAT : (half + 1) * LAT] = block[:, :LAT]
            if half:
                rotary = jnp.concatenate([q_in[i, b - 4].astype(F32)[:, LAT:], block[:, LAT:]], axis=1)
                q_wide[i, start : start + 4, 2 * LAT :] = rotary
        return q_wide[i].astype(BF16)

    mirror_q.wait()
    q_mirror[...] = packed(1)
    own_q.wait()
    q_buf[y_hi, SLOT[0]] = packed(0)
    own_pool.wait()
    flat_pool = pool_in[...].reshape(KEYS, WIDTH)
    keys[c, 0, 1, :LAT] = flat_pool[:, :LAT].T
    keys[c, 0, 1, LAT:] = flat_pool[:, LAT:].T

    pl.semaphore_wait(barrier, len(senders))

    copies = []

    def describe(src, dst, send_sem, recv_sem, target):
        return pltpu.make_async_remote_copy(
            src_ref=src, dst_ref=dst, send_sem=send_sem, recv_sem=recv_sem, device_id=target, device_id_type=MESH)

    def send(*what):
        copy = describe(*what)
        copy.start()
        copies.append(copy)
        return copy

    def arrived(dst, recv_sem):
        describe(dst, dst, v_send, recv_sem, other_core).wait_recv()

    swap = send(q_mirror, q_buf.at[y_hi, SLOT[0]], swap_send, swap_recv, mirror)
    q_copies = {}

    def along_z(group, source, dz, slot):
        side = (y_hi + group) % 2
        q_copies[group, slot] = send(
            q_buf.at[side, source], q_buf.at[side, slot],
            q_send.at[group, slot], q_recv.at[group, slot], place(x, y, (z + dz + NZ) % NZ, c))

    def first_step(group):
        for dz in (2, 6, 1, 7):
            along_z(group, SLOT[0], dz, SLOT[NZ - dz])

    def second_step(group):
        q_copies[group, SLOT[6]].wait_recv()
        q_copies[group, SLOT[2]].wait_recv()
        along_z(group, SLOT[6] + c * (SLOT[2] - SLOT[6]), 2 * step, SLOT[4])
        along_z(group, SLOT[6], 1, SLOT[5])
        along_z(group, SLOT[2], -1, SLOT[3])

    def wait_queries(group):
        for dz in (1, 7, 3, 5, 4):
            q_copies[group, SLOT[dz]].wait_recv()

    first_step(0)
    pieces = ((0, slice(0, WIDTH)), (1, slice(0, WIDTH // 2)), (1, slice(WIDTH // 2, WIDTH)))
    key_copies = {}

    def key_piece(kind, piece):
        pooled, rows = pieces[piece]
        dx, dy = key_moves[kind - 1]
        target_request = (x_lo + dx) % 2 * 2 + (y_lo + dy) % 2
        key_copies[kind, piece] = send(
            keys.at[c, 0, 1, rows] if pooled else prompt.at[target_request], keys.at[c, kind, pooled, rows],
            key_send.at[kind - 1, piece], key_recv.at[kind - 1, piece], shifted(dx * step, dy * step))

    core_copies = {}

    def to_core(kind, piece):
        pooled, rows = pieces[piece]
        core_copies[kind, piece] = send(
            keys.at[c, kind, pooled, rows], keys.at[c, kind, pooled, rows],
            core_send.at[kind, piece], core_recv.at[kind, piece], other_core)

    def wait_core(piece):
        for kind in range(4):
            core_copies[kind, piece].wait_recv()

    for kind in range(1, 4):
        key_piece(kind, 0)
    for piece in (1, 2):
        for kind in range(1, 4):
            key_piece(kind, piece)
    own_prompt.wait()
    for piece in range(3):
        to_core(0, piece)

    get_parents.wait()
    get_lengths.wait()
    get_lists.wait()
    slot = lax.broadcasted_iota(jnp.int32, (4, MAXP), 1)
    for b in range(BEAM):
        parent = parents[request * BEAM + b]
        lists[4 * b : 4 * b + 4, :] = jnp.broadcast_to(page_lists[pl.ds(parent, 1), :], (4, MAXP))
        room[4 * b : 4 * b + 4, :] = jnp.clip(lengths[parent] - slot * PAGE, 0, PAGE)
    chosen = lists[...]
    space = room[...]
    lane = lax.broadcasted_iota(jnp.int32, (4 * BEAM, KEYS), 1)
    for cc in range(2):
        sign = 1 - 2 * cc
        for kind, (dx, dy) in enumerate(((0, 0),) + key_moves):
            sy = (y - sign * dy + 4) % 4
            s_seq, s_head = place((x - sign * dx + 4) % 4, sy, z, cc)
            page = (s_seq * 32 + s_head) * 2
            live = [
                jnp.sum(jnp.where(chosen == page + i, space, 0), axis=1, keepdims=True) for i in range(2)
            ]
            seen = lane < jnp.where(lane < PAGE, live[0], live[1] + PAGE)
            cap[:, (cc * 4 + kind) * KEYS : (cc * 4 + kind + 1) * KEYS] = jnp.where(seen, jnp.inf, -jnp.inf)

    swap.wait_recv()
    first_step(1)
    second_step(0)
    for kind in range(1, 4):
        key_copies[kind, 0].wait_recv()
        to_core(kind, 0)
    second_step(1)
    for kind in range(1, 4):
        key_copies[kind, 1].wait_recv()
        to_core(kind, 1)

    def attend(group, pooled):
        block = q_buf[group].reshape(KEYS, 2 * LAT + 128)
        rotary = block[:, 2 * LAT :]
        lane = lax.broadcasted_iota(jnp.int32, (KEYS, 128), 1)
        rows = jnp.concatenate([
            jnp.concatenate([block[:, :LAT], jnp.where(lane < ROPE, rotary, 0)], axis=1),
            jnp.concatenate([block[:, LAT : 2 * LAT], jnp.where(lane < ROPE, 0, rotary)], axis=1),
        ], axis=0)
        for pair in range(4):
            cc, kind = pair // 2, pair % 2 * 2
            columns = jnp.concatenate([keys[cc, kind, pooled], keys[cc, kind + 1, pooled]], axis=1)
            columns = jnp.concatenate([columns, columns[LAT:]], axis=0)
            raw = jnp.dot(rows, columns, preferred_element_type=F32)
            if pooled:
                limit = cap[:, 2 * pair * KEYS : 2 * (pair + 1) * KEYS].reshape(2, 1, 16, 2 * KEYS)
                raw = jnp.minimum(raw.reshape(2, NZ, 16, 2 * KEYS), limit).reshape(2 * KEYS, 2 * KEYS)
            scores[:, 2 * pair * KEYS : 2 * (pair + 1) * KEYS] = raw
        peak = jnp.max(scores[...], axis=1, keepdims=True)
        if pooled:
            peak = jnp.maximum(peak, LOWEST)
        weights = jnp.exp2((scores[...] - peak) * RATE)
        total = jnp.sum(weights, axis=1, keepdims=True)
        probs[...] = weights.astype(BF16)
        values = jnp.concatenate([keys[cc, kind, pooled, :LAT] for cc in range(2) for kind in range(4)], axis=1)
        latent = lax.dot_general(
            probs[...], values, (((1,), (1,)), ((), ())), preferred_element_type=F32)
        return peak, total, latent

    def finish(group, first, z_first):
        peak1, total1, latent1 = first
        peak2, total2, latent2 = attend(group, 1)
        peak = jnp.maximum(peak1, peak2)
        keep1 = jnp.exp2((peak1 - peak) * RATE)
        keep2 = jnp.exp2((peak2 - peak) * RATE)
        total = total1 * keep1 + total2 * keep2
        part[group] = (latent1 * keep1 + latent2 * keep2).astype(BF16).reshape(2, KEYS, LAT)
        lane = lax.broadcasted_iota(jnp.int32, (KEYS, 128), 1)
        for half in range(2):
            half_rows = slice(half * KEYS, (half + 1) * KEYS)
            stat[group, half] = jnp.where(lane == 0, peak[half_rows], total[half_rows]).T[:8]
            if z_first:
                zs_stat_src[half] = lines(peak[half_rows], total[half_rows])

    def scatter(i, group, half):
        target = shifted(*scatter_moves[i], core=1)
        send(stat.at[group, half], rs1_stat.at[i, c], rs1_send.at[i, CHUNKS], rs1_recv.at[i, c, CHUNKS], target)
        for chunk in range(CHUNKS):
            rows = pl.ds(CHUNK * chunk, CHUNK)
            send(
                part.at[group, half, rows], rs1.at[i, c, rows],
                rs1_send.at[i, chunk], rs1_recv.at[i, c, chunk], target)

    wait_queries(0)
    wait_core(0)
    prompt_a = attend(y_hi, 0)
    for kind in range(1, 4):
        key_copies[kind, 2].wait_recv()
        to_core(kind, 2)
    wait_queries(1)
    prompt_b = attend(1 - y_hi, 0)
    wait_core(1)
    wait_core(2)
    finish(y_hi, prompt_a, True)
    for slot in range(NZ - 1):
        target = place(x, y, (z + RELATIVE[slot]) % NZ, 1)
        send(
            part.at[y_hi, 1 - x_hi, pl.ds(16 * slot, 16)], zs.at[slot, c],
            zs_send.at[slot, 0], zs_recv.at[c, slot, 0], target)
        send(
            zs_stat_src.at[1 - x_hi, slot], zs_stat.at[slot, c], zs_send.at[slot, 1], zs_recv.at[c, slot, 1], target)
    scatter(0, y_hi, x_hi)
    finish(1 - y_hi, prompt_b, False)
    scatter(1, 1 - y_hi, 1 - x_hi)
    own_v.wait()
    last = SLOT[0]

    @pl.when(c == 0)
    def _():
        mine = [
            describe(
                part.at[y_hi, 1 - x_hi, pl.ds(16 * last, 16)], zs.at[last, 0],
                zs_send.at[last, 0], zs_recv.at[0, last, 0], other_core),
            describe(
                zs_stat_src.at[1 - x_hi, last], zs_stat.at[last, 0],
                zs_send.at[last, 1], zs_recv.at[0, last, 1], other_core),
            describe(part.at[1 - y_hi, x_hi], rs1.at[2, 0], rs1_send.at[2, 0], rs1_recv.at[2, 0, 0], other_core),
            describe(stat.at[1 - y_hi, x_hi], rs1_stat.at[2, 0], rs1_send.at[2, 1], rs1_recv.at[2, 0, 1], other_core),
            describe(value_up, v_buf.at[0], v_send, v_recv, other_core),
        ]
        for copy in mine:
            copy.start()
        for i in range(8):
            arrived(out.at[0], out_recv.at[i])
        for copy in mine:
            copy.wait_send()

    @pl.when(c == 1)
    def _():
        work = []

        def post(*what):
            copy = describe(*what)
            copy.start()
            work.append(copy)
            return copy

        zs[last, 1] = part[y_hi, 1 - x_hi, 16 * last :]
        zs_stat[last, 1] = zs_stat_src[1 - x_hi, last]
        rs2_copies = []

        def home(slot, target):
            rs2_copies.append(post(
                rs2_src.at[slot], rs2.at[slot], rs2_send.at[slot, 0], rs2_recv.at[slot, 0], target))
            rs2_copies.append(post(
                rs2_stat_src.at[slot], rs2_stat.at[slot], rs2_send.at[slot, 1], rs2_recv.at[slot, 1], target))

        per = CHUNK // 16
        for chunk in range(CHUNKS):
            rows = slice(chunk * CHUNK, (chunk + 1) * CHUNK)
            here = slice(chunk * per, (chunk + 1) * per)
            both = []
            for core in range(2):
                if chunk == 0:
                    for i in range(2):
                        arrived(rs1_stat.at[i, core], rs1_recv.at[i, core, CHUNKS])
                    if core == 0:
                        arrived(rs1.at[2, 0], rs1_recv.at[2, 0, 0])
                        arrived(rs1_stat.at[2, 0], rs1_recv.at[2, 0, 1])
                for i in range(2):
                    arrived(rs1.at[i, core, pl.ds(CHUNK * chunk, CHUNK)], rs1_recv.at[i, core, chunk])
                kept = part[1 - y_hi, x_hi, rows] if core else rs1[2, 0, rows]
                kept_stat = stat[1 - y_hi, x_hi] if core else rs1_stat[2, 0]
                columns = jnp.concatenate([
                    kept_stat, rs1_stat[0, core], rs1_stat[1, core], jnp.zeros((KEYS - 24, KEYS), F32)], axis=0).T[rows]
                peak, total, latent = merge(
                    [kept, rs1[0, core, rows], rs1[1, core, rows]],
                    [(columns[:, 8 * i : 8 * i + 1], columns[:, 8 * i + 1 : 8 * i + 2]) for i in range(3)])
                rs2_src[here, core] = latent.astype(BF16).reshape(per, 16, LAT)
                both.append(lines(peak, total, 32 * core))
            rs2_stat_src[here] = both[0] + both[1]
            for slot in range(per * chunk, per * chunk + per):
                home(slot, place(x, 3 - y, (z + RELATIVE[slot]) % NZ, 1))
        both = []
        for core in range(2):
            for slot in range(NZ):
                if core == 0 or slot != last:
                    arrived(zs.at[slot, core], zs_recv.at[core, slot, 0])
                    arrived(zs_stat.at[slot, core], zs_recv.at[core, slot, 1])
            peak, total, latent = merge(
                [zs[slot, core] for slot in range(NZ)], [from_line(zs_stat[slot, core]) for slot in range(NZ)])
            rs2_src[NZ, core] = latent.astype(BF16)
            both.append(lines(peak, total, 32 * core))
        rs2_stat_src[NZ : NZ + 1] = both[0] + both[1]
        home(NZ, out_place(2, 1, 1))
        arrived(v_buf.at[0], v_recv)
        for copy in rs2_copies:
            copy.wait_recv()
        row = lax.broadcasted_iota(jnp.int32, (16, VDIM), 0)
        place_out = mirror_request * 2 + x_hi
        out_copies = []
        for core in range(2):
            peak, total, latent = merge(
                [rs2[slot, core] for slot in range(NZ + 1)],
                [from_line(rs2_stat[slot], 32 * core) for slot in range(NZ + 1)])
            latent = (latent / total).astype(BF16)
            attended = jnp.zeros((16, VDIM), F32)
            for h in range(4):
                product = jnp.dot(latent, v_buf[core, h], preferred_element_type=F32)
                attended = jnp.where(row % 4 == h, product, attended)
            out_src[core] = attended.astype(BF16)
            for i, (dx, dy) in enumerate(out_moves):
                if core == 0 or i > 0:
                    copy = post(
                        out_src.at[core], out.at[place_out], out_send.at[core, i], out_recv.at[i],
                        out_place(dx, dy, core))
                    if core == 1:
                        out_copies.append(copy)
        out[place_out] = out_src[1]
        for copy in out_copies:
            copy.wait_recv()
        for copy in work:
            copy.wait_send()

    for copy in copies:
        copy.wait_send()


def body(queries, prompt_latent, pool_latent, value_up, parents, page_lists, lengths):
    vmem = pl.BlockSpec(memory_space=pltpu.VMEM)
    hbm = pl.BlockSpec(memory_space=pltpu.HBM)
    operands = (parents, lengths, page_lists, queries, prompt_latent.swapaxes(1, 2), pool_latent, value_up)
    dma = pltpu.SemaphoreType.DMA
    result = pl.pallas_call(
        kernel,
        out_shape=pltpu.VMEM((8, 16, VDIM), BF16),
        in_specs=[hbm] * 7,
        out_specs=vmem,
        scratch_shapes=[
            pltpu.SMEM((32,), jnp.int32),
            pltpu.SMEM((32,), jnp.int32),
            pltpu.VMEM((32, MAXP), jnp.int32),
            pltpu.VMEM((2, BEAM, 4, WIDTH), BF16),
            pltpu.VMEM((2, 16, 2 * LAT + 128), F32),
            pltpu.VMEM((16, 2 * LAT + 128), BF16),
            pltpu.VMEM((2, NZ, 16, 2 * LAT + 128), BF16),
            pltpu.VMEM((2, PAGE, WIDTH), BF16),
            pltpu.VMEM((2, 4, 2, WIDTH, KEYS), BF16),
            pltpu.VMEM((2, 4, LAT, VDIM), BF16),
            pltpu.VMEM((4 * BEAM, MAXP), jnp.int32),
            pltpu.VMEM((4 * BEAM, MAXP), jnp.int32),
            pltpu.VMEM((4 * BEAM, 8 * KEYS), F32),
            pltpu.VMEM((2 * KEYS, 8 * KEYS), F32),
            pltpu.VMEM((2 * KEYS, 8 * KEYS), BF16),
            pltpu.VMEM((2, 2, KEYS, LAT), BF16),
            pltpu.VMEM((2, 2, 8, KEYS), F32),
            pltpu.VMEM((3, 2, KEYS, LAT), BF16),
            pltpu.VMEM((3, 2, 8, KEYS), F32),
            pltpu.VMEM((NZ, 2, 16, LAT), BF16),
            pltpu.VMEM((2, NZ, 1, KEYS), F32),
            pltpu.VMEM((NZ, 2, 1, KEYS), F32),
            pltpu.VMEM((NZ + 1, 2, 16, LAT), BF16),
            pltpu.VMEM((NZ + 1, 1, KEYS), F32),
            pltpu.VMEM((NZ + 1, 2, 16, LAT), BF16),
            pltpu.VMEM((NZ + 1, 1, KEYS), F32),
            pltpu.VMEM((2, 16, VDIM), BF16),
            dma((8,)), dma((3, 3)), dma((3, 3)), dma((4, 3)), dma((4, 3)), dma, dma, dma((2, NZ)), dma((2, NZ)),
            dma, dma,
            dma((3, CHUNKS + 1)), dma((3, 2, CHUNKS + 1)), dma((NZ, 2)), dma((2, NZ, 2)), dma((NZ + 1, 2)), dma((NZ + 1, 2)),
            dma((2, 8)), dma((8,)),
        ],
        compiler_params=pltpu.CompilerParams(
            collective_id=0, has_side_effects=True, vmem_limit_bytes=48 * 2**20
        ),
    )(
        *[pltpu.with_memory_space_constraint(operand, pltpu.HBM) for operand in operands]
    )
    return result.reshape(32, 4, VDIM)


def solution(mesh):
    return jax.shard_map(
        body,
        mesh=mesh,
        in_specs=(
            P(None, "head", None),
            P(None, ("seq", "head"), None),
            P(("seq", "head"), None, None),
            P("head", None, None),
            P(),
            P(),
            P(),
        ),
        out_specs=P(None, "head", None),
        check_vma=False,
    )
```

```python
import jax
import jax.numpy as jnp
from jax import lax
from jax.experimental import pallas as pl
from jax.experimental.pallas import tpu as pltpu
from jax.sharding import PartitionSpec as P

LAT = 512
ROPE = 64
WIDTH = LAT + ROPE
VDIM = 128
BEAM = 8
PAGE = 64
MAXP = 64
NZ = 8
RELATIVE = (4, 3, 5, 2, 6, 1, 7, 0)
CHUNKS = 2
CHUNK = 128 // CHUNKS
SLOT = {dz: k for k, dz in enumerate(RELATIVE)}
KEYS = 128
LOG2E = 1.4426950408889634
RATE = (VDIM + ROPE) ** -0.5 * LOG2E
LOWEST = -3.0e38
MESH = pl.DeviceIdType.MESH
F32 = jnp.float32
BF16 = jnp.bfloat16


def place(x, y, z, c):
    return ((y % 2) * 4 + x, z * 4 + (y // 2) * 2 + c)


def merge(parts, stats):
    peak = stats[0][0]
    for other, _ in stats[1:]:
        peak = jnp.maximum(peak, other)
    total = jnp.zeros_like(peak)
    latent = jnp.zeros((peak.shape[0], LAT), F32)
    for part, (part_peak, part_total) in zip(parts, stats):
        keep = jnp.exp2((part_peak - peak) * RATE)
        total = total + part_total * keep
        latent = latent + part[:, :LAT].astype(F32) * keep
    return peak, total, latent


def lines(peak, total):
    rows = peak.shape[0]
    lane = lax.broadcasted_iota(jnp.int32, (rows, KEYS), 1)
    row = lax.broadcasted_iota(jnp.int32, (rows, KEYS), 0) % 16
    spread = jnp.where(lane == row, peak, 0.0) + jnp.where(lane == row + 16, total, 0.0)
    return jnp.sum(spread.reshape(rows // 16, 16, KEYS), axis=1, keepdims=True)


def from_line(line):
    lane = lax.broadcasted_iota(jnp.int32, (16, KEYS), 1)
    row = lax.broadcasted_iota(jnp.int32, (16, KEYS), 0)
    return (
        jnp.sum(jnp.where(lane == row, line, 0.0), axis=1, keepdims=True),
        jnp.sum(jnp.where(lane == row + 16, line, 0.0), axis=1, keepdims=True))


def kernel(
    parents_hbm, lengths_hbm, lists_hbm, queries, prompt, pool, value_up,
    out,
    parents, lengths, page_lists,
    q_in, q_wide, q_mirror, q_buf, pool_in, keys, v_buf, lists, room, cap, scores, probs,
    part, stat, rs1, rs1_stat, zs, zs_stat_src, zs_stat, rs2_src, rs2_stat_src, rs2, rs2_stat, out_src,
    local_sem, key_send, key_recv, core_send, core_recv, swap_send, swap_recv, q_send, q_recv,
    rs1_send, rs1_recv, zs_send, zs_recv, rs2_send, rs2_recv, out_send, out_recv,
):
    seq = lax.axis_index("seq")
    head = lax.axis_index("head")
    x = seq % 4
    y_lo = seq // 4
    c = head % 2
    y_hi = (head // 2) % 2
    z = head // 4
    y = y_hi * 2 + y_lo
    x_hi = x // 2
    x_lo = x % 2
    step = 1 - 2 * c
    request = x_lo * 2 + y_lo

    def shifted(dx, dy, sign=1):
        return place((x + sign * dx + 4) % 4, (y + sign * dy + 4) % 4, z, c)

    other_core = place(x, y, z, 1 - c)
    mirror = place(x, 3 - y, z, c)
    key_moves = ((1, 0), (0, 1), (1, 1))
    scatter_moves = ((0, 2), (2, 0))
    out_moves = [(dx, dy) for dy in range(2) for dx in range(4) if (dx, dy) != (0, 0)]

    def out_place(dx, dy):
        return place((x + dx) % 4, y_hi * 2 + (y_lo + dy) % 2, z, c)

    barrier = pltpu.get_barrier_semaphore()
    senders = [place(x, y, (z + dz) % NZ, c) for dz in (2, 6, 1, 7)]
    senders += [shifted(dx * step, dy * step, -1) for dx, dy in key_moves]
    senders += [shifted(dx, dy) for dx, dy in scatter_moves]
    senders += [mirror, other_core]
    for sender in senders:
        pl.semaphore_signal(barrier, inc=1, device_id=sender, device_id_type=MESH)

    mirror_request = x_lo * 2 + 1 - y_lo
    own_q = pltpu.make_async_copy(queries.at[pl.ds(request * BEAM, BEAM)], q_in.at[0], local_sem.at[0])
    mirror_q = pltpu.make_async_copy(queries.at[pl.ds(mirror_request * BEAM, BEAM)], q_in.at[1], local_sem.at[1])
    own_pool = pltpu.make_async_copy(pool, pool_in, local_sem.at[2])
    own_prompt = pltpu.make_async_copy(prompt.at[request], keys.at[c, 0, 0], local_sem.at[3])
    own_v = pltpu.make_async_copy(value_up, v_buf, local_sem.at[4])
    get_parents = pltpu.make_async_copy(parents_hbm, parents, local_sem.at[5])
    get_lengths = pltpu.make_async_copy(lengths_hbm, lengths, local_sem.at[6])
    get_lists = pltpu.make_async_copy(lists_hbm, page_lists, local_sem.at[7])
    own_q.start()
    mirror_q.start()
    own_pool.start()
    own_prompt.start()
    get_parents.start()
    get_lengths.start()
    get_lists.start()
    own_v.start()

    def packed(i):
        for b in range(BEAM):
            block = q_in[i, b].astype(F32)
            half, start = b // 4, b % 4 * 4
            q_wide[i, start : start + 4, half * LAT : (half + 1) * LAT] = block[:, :LAT]
            if half:
                rotary = jnp.concatenate([q_in[i, b - 4].astype(F32)[:, LAT:], block[:, LAT:]], axis=1)
                q_wide[i, start : start + 4, 2 * LAT :] = rotary
        return q_wide[i].astype(BF16)

    mirror_q.wait()
    q_mirror[...] = packed(1)
    own_q.wait()
    q_buf[y_hi, SLOT[0]] = packed(0)
    own_pool.wait()
    flat_pool = pool_in[...].reshape(KEYS, WIDTH)
    keys[c, 0, 1, :LAT] = flat_pool[:, :LAT].T
    keys[c, 0, 1, LAT:] = flat_pool[:, LAT:].T

    pl.semaphore_wait(barrier, len(senders))

    copies = []

    def send(src, dst, send_sem, recv_sem, target):
        copy = pltpu.make_async_remote_copy(
            src_ref=src, dst_ref=dst, send_sem=send_sem, recv_sem=recv_sem, device_id=target, device_id_type=MESH
        )
        copy.start()
        copies.append(copy)
        return copy

    swap = send(q_mirror, q_buf.at[y_hi, SLOT[0]], swap_send, swap_recv, mirror)
    q_copies = {}

    def along_z(group, source, dz, slot):
        side = (y_hi + group) % 2
        q_copies[group, slot] = send(
            q_buf.at[side, source], q_buf.at[side, slot],
            q_send.at[group, slot], q_recv.at[group, slot], place(x, y, (z + dz + NZ) % NZ, c))

    def first_step(group):
        for dz in (2, 6, 1, 7):
            along_z(group, SLOT[0], dz, SLOT[NZ - dz])

    def second_step(group):
        q_copies[group, SLOT[6]].wait_recv()
        q_copies[group, SLOT[2]].wait_recv()
        along_z(group, SLOT[6] + c * (SLOT[2] - SLOT[6]), 2 * step, SLOT[4])
        along_z(group, SLOT[6], 1, SLOT[5])
        along_z(group, SLOT[2], -1, SLOT[3])

    def wait_queries(group):
        for dz in (1, 7, 3, 5, 4):
            q_copies[group, SLOT[dz]].wait_recv()

    first_step(0)
    pieces = ((0, slice(0, WIDTH)), (1, slice(0, WIDTH // 2)), (1, slice(WIDTH // 2, WIDTH)))
    key_copies = {}

    def key_piece(kind, piece):
        pooled, rows = pieces[piece]
        dx, dy = key_moves[kind - 1]
        target_request = (x_lo + dx) % 2 * 2 + (y_lo + dy) % 2
        key_copies[kind, piece] = send(
            keys.at[c, 0, 1, rows] if pooled else prompt.at[target_request], keys.at[c, kind, pooled, rows],
            key_send.at[kind - 1, piece], key_recv.at[kind - 1, piece], shifted(dx * step, dy * step))

    core_copies = {}

    def to_core(kind, piece):
        pooled, rows = pieces[piece]
        core_copies[kind, piece] = send(
            keys.at[c, kind, pooled, rows], keys.at[c, kind, pooled, rows],
            core_send.at[kind, piece], core_recv.at[kind, piece], other_core)

    def wait_core(piece):
        for kind in range(4):
            core_copies[kind, piece].wait_recv()

    for kind in range(1, 4):
        key_piece(kind, 0)
    for piece in (1, 2):
        for kind in range(1, 4):
            key_piece(kind, piece)
    own_prompt.wait()
    for piece in range(3):
        to_core(0, piece)

    get_parents.wait()
    get_lengths.wait()
    get_lists.wait()
    slot = lax.broadcasted_iota(jnp.int32, (4, MAXP), 1)
    for b in range(BEAM):
        parent = parents[request * BEAM + b]
        lists[4 * b : 4 * b + 4, :] = jnp.broadcast_to(page_lists[pl.ds(parent, 1), :], (4, MAXP))
        room[4 * b : 4 * b + 4, :] = jnp.clip(lengths[parent] - slot * PAGE, 0, PAGE)
    chosen = lists[...]
    space = room[...]
    lane = lax.broadcasted_iota(jnp.int32, (4 * BEAM, KEYS), 1)
    for cc in range(2):
        sign = 1 - 2 * cc
        for kind, (dx, dy) in enumerate(((0, 0),) + key_moves):
            sy = (y - sign * dy + 4) % 4
            s_seq, s_head = place((x - sign * dx + 4) % 4, sy, z, cc)
            page = (s_seq * 32 + s_head) * 2
            live = [
                jnp.sum(jnp.where(chosen == page + i, space, 0), axis=1, keepdims=True) for i in range(2)
            ]
            seen = lane < jnp.where(lane < PAGE, live[0], live[1] + PAGE)
            cap[:, (cc * 4 + kind) * KEYS : (cc * 4 + kind + 1) * KEYS] = jnp.where(seen, jnp.inf, -jnp.inf)

    swap.wait_recv()
    first_step(1)
    second_step(0)
    for kind in range(1, 4):
        key_copies[kind, 0].wait_recv()
        to_core(kind, 0)
    second_step(1)
    for kind in range(1, 4):
        key_copies[kind, 1].wait_recv()
        to_core(kind, 1)

    def attend(group, pooled):
        block = q_buf[group].reshape(KEYS, 2 * LAT + 128)
        rotary = block[:, 2 * LAT :]
        lane = lax.broadcasted_iota(jnp.int32, (KEYS, 128), 1)
        rows = jnp.concatenate([
            jnp.concatenate([block[:, :LAT], jnp.where(lane < ROPE, rotary, 0)], axis=1),
            jnp.concatenate([block[:, LAT : 2 * LAT], jnp.where(lane < ROPE, 0, rotary)], axis=1),
        ], axis=0)
        for pair in range(4):
            cc, kind = pair // 2, pair % 2 * 2
            columns = jnp.concatenate([keys[cc, kind, pooled], keys[cc, kind + 1, pooled]], axis=1)
            columns = jnp.concatenate([columns, columns[LAT:]], axis=0)
            raw = jnp.dot(rows, columns, preferred_element_type=F32)
            if pooled:
                limit = cap[:, 2 * pair * KEYS : 2 * (pair + 1) * KEYS].reshape(2, 1, 16, 2 * KEYS)
                raw = jnp.minimum(raw.reshape(2, NZ, 16, 2 * KEYS), limit).reshape(2 * KEYS, 2 * KEYS)
            scores[:, 2 * pair * KEYS : 2 * (pair + 1) * KEYS] = raw
        peak = jnp.max(scores[...], axis=1, keepdims=True)
        if pooled:
            peak = jnp.maximum(peak, LOWEST)
        weights = jnp.exp2((scores[...] - peak) * RATE)
        total = jnp.sum(weights, axis=1, keepdims=True)
        probs[...] = weights.astype(BF16)
        values = jnp.concatenate([keys[cc, kind, pooled, :LAT] for cc in range(2) for kind in range(4)], axis=1)
        latent = lax.dot_general(
            probs[...], values, (((1,), (1,)), ((), ())), preferred_element_type=F32)
        return peak, total, latent

    def finish(group, first, z_first):
        peak1, total1, latent1 = first
        peak2, total2, latent2 = attend(group, 1)
        peak = jnp.maximum(peak1, peak2)
        keep1 = jnp.exp2((peak1 - peak) * RATE)
        keep2 = jnp.exp2((peak2 - peak) * RATE)
        total = total1 * keep1 + total2 * keep2
        part[group] = (latent1 * keep1 + latent2 * keep2).astype(BF16).reshape(2, KEYS, LAT)
        lane = lax.broadcasted_iota(jnp.int32, (KEYS, 128), 1)
        for half in range(2):
            half_rows = slice(half * KEYS, (half + 1) * KEYS)
            stat[group, half] = jnp.where(lane == 0, peak[half_rows], total[half_rows]).T[:8]
            if z_first:
                zs_stat_src[half] = lines(peak[half_rows], total[half_rows])

    def scatter(i, group, half):
        target = shifted(*scatter_moves[i])
        rs1_copies[i, CHUNKS] = send(
            stat.at[group, half], rs1_stat.at[i], rs1_send.at[i, CHUNKS], rs1_recv.at[i, CHUNKS], target)
        for chunk in range(CHUNKS):
            rows = pl.ds(CHUNK * chunk, CHUNK)
            rs1_copies[i, chunk] = send(
                part.at[group, half, rows], rs1.at[i, rows], rs1_send.at[i, chunk], rs1_recv.at[i, chunk], target)

    rs1_copies = {}
    zs_copies = []
    wait_queries(0)
    wait_core(0)
    prompt_a = attend(y_hi, 0)
    for kind in range(1, 4):
        key_copies[kind, 2].wait_recv()
        to_core(kind, 2)
    wait_queries(1)
    prompt_b = attend(1 - y_hi, 0)
    wait_core(1)
    wait_core(2)
    finish(y_hi, prompt_a, True)
    scatter(0, y_hi, x_hi)
    for slot in range(NZ - 1):
        target = place(x, y, (z + RELATIVE[slot]) % NZ, c)
        zs_copies.append(send(
            part.at[y_hi, 1 - x_hi, pl.ds(16 * slot, 16)], zs.at[slot], zs_send.at[slot, 0], zs_recv.at[slot, 0], target))
        zs_copies.append(send(
            zs_stat_src.at[1 - x_hi, slot], zs_stat.at[slot], zs_send.at[slot, 1], zs_recv.at[slot, 1], target))
    finish(1 - y_hi, prompt_b, False)
    scatter(1, 1 - y_hi, 1 - x_hi)

    rs2_copies = []

    def home(slot, target):
        rs2_copies.append(send(
            rs2_src.at[slot], rs2.at[slot], rs2_send.at[slot, 0], rs2_recv.at[slot, 0], target))
        rs2_copies.append(send(
            rs2_stat_src.at[slot], rs2_stat.at[slot], rs2_send.at[slot, 1], rs2_recv.at[slot, 1], target))

    for i in range(2):
        rs1_copies[i, CHUNKS].wait_recv()
    columns = jnp.concatenate([
        stat[1 - y_hi, x_hi], rs1_stat[0], rs1_stat[1], jnp.zeros((KEYS - 24, KEYS), F32)], axis=0).T
    per = CHUNK // 16
    for chunk in range(CHUNKS):
        rows = slice(chunk * CHUNK, (chunk + 1) * CHUNK)
        for i in range(2):
            rs1_copies[i, chunk].wait_recv()
        peak, total, latent = merge(
            [part[1 - y_hi, x_hi, rows], rs1[0, rows], rs1[1, rows]],
            [(columns[rows, 8 * i : 8 * i + 1], columns[rows, 8 * i + 1 : 8 * i + 2]) for i in range(3)])
        rs2_src[per * chunk : per * chunk + per] = latent.astype(BF16).reshape(per, 16, LAT)
        rs2_stat_src[per * chunk : per * chunk + per] = lines(peak, total)
        for slot in range(per * chunk, per * chunk + per):
            home(slot, place(x, 3 - y, (z + RELATIVE[slot]) % NZ, c))
    for copy in zs_copies:
        copy.wait_recv()
    peak, total, latent = merge(
        [part[y_hi, 1 - x_hi, 16 * SLOT[0] :]] + [zs[slot] for slot in range(NZ - 1)],
        [from_line(zs_stat_src[1 - x_hi, SLOT[0]])] + [from_line(zs_stat[slot]) for slot in range(NZ - 1)])
    rs2_src[NZ] = latent.astype(BF16)
    rs2_stat_src[NZ : NZ + 1] = lines(peak, total)
    home(NZ, place((x + 2) % 4, y_hi * 2 + 1 - y_lo, z, c))
    own_v.wait()
    for copy in rs2_copies:
        copy.wait_recv()
    peak, total, latent = merge([rs2[slot] for slot in range(NZ + 1)], [from_line(rs2_stat[slot]) for slot in range(NZ + 1)])
    latent = (latent / total).astype(BF16)
    attended = jnp.zeros((16, VDIM), F32)
    row = lax.broadcasted_iota(jnp.int32, (16, VDIM), 0)
    for h in range(4):
        product = jnp.dot(latent, v_buf[h], preferred_element_type=F32)
        attended = jnp.where(row % 4 == h, product, attended)
    out_src[...] = attended.astype(BF16)
    place_out = mirror_request * 2 + x_hi
    out_copies = []
    for i, (dx, dy) in enumerate(out_moves):
        out_copies.append(send(
            out_src, out.at[place_out], out_send.at[i], out_recv.at[i], out_place(dx, dy)))
    out[place_out] = out_src[...]
    for copy in out_copies:
        copy.wait_recv()
    for copy in copies:
        copy.wait_send()


def body(queries, prompt_latent, pool_latent, value_up, parents, page_lists, lengths):
    vmem = pl.BlockSpec(memory_space=pltpu.VMEM)
    hbm = pl.BlockSpec(memory_space=pltpu.HBM)
    operands = (parents, lengths, page_lists, queries, prompt_latent.swapaxes(1, 2), pool_latent, value_up)
    dma = pltpu.SemaphoreType.DMA
    result = pl.pallas_call(
        kernel,
        out_shape=pltpu.VMEM((8, 16, VDIM), BF16),
        in_specs=[hbm] * 7,
        out_specs=vmem,
        scratch_shapes=[
            pltpu.SMEM((32,), jnp.int32),
            pltpu.SMEM((32,), jnp.int32),
            pltpu.VMEM((32, MAXP), jnp.int32),
            pltpu.VMEM((2, BEAM, 4, WIDTH), BF16),
            pltpu.VMEM((2, 16, 2 * LAT + 128), F32),
            pltpu.VMEM((16, 2 * LAT + 128), BF16),
            pltpu.VMEM((2, NZ, 16, 2 * LAT + 128), BF16),
            pltpu.VMEM((2, PAGE, WIDTH), BF16),
            pltpu.VMEM((2, 4, 2, WIDTH, KEYS), BF16),
            pltpu.VMEM((4, LAT, VDIM), BF16),
            pltpu.VMEM((4 * BEAM, MAXP), jnp.int32),
            pltpu.VMEM((4 * BEAM, MAXP), jnp.int32),
            pltpu.VMEM((4 * BEAM, 8 * KEYS), F32),
            pltpu.VMEM((2 * KEYS, 8 * KEYS), F32),
            pltpu.VMEM((2 * KEYS, 8 * KEYS), BF16),
            pltpu.VMEM((2, 2, KEYS, LAT), BF16),
            pltpu.VMEM((2, 2, 8, KEYS), F32),
            pltpu.VMEM((2, KEYS, LAT), BF16),
            pltpu.VMEM((2, 8, KEYS), F32),
            pltpu.VMEM((NZ - 1, 16, LAT), BF16),
            pltpu.VMEM((2, NZ, 1, KEYS), F32),
            pltpu.VMEM((NZ - 1, 1, KEYS), F32),
            pltpu.VMEM((NZ + 1, 16, LAT), BF16),
            pltpu.VMEM((NZ + 1, 1, KEYS), F32),
            pltpu.VMEM((NZ + 1, 16, LAT), BF16),
            pltpu.VMEM((NZ + 1, 1, KEYS), F32),
            pltpu.VMEM((16, VDIM), BF16),
            dma((8,)), dma((3, 3)), dma((3, 3)), dma((4, 3)), dma((4, 3)), dma, dma, dma((2, NZ)), dma((2, NZ)),
            dma((2, CHUNKS + 1)), dma((2, CHUNKS + 1)), dma((NZ - 1, 2)), dma((NZ - 1, 2)), dma((NZ + 1, 2)), dma((NZ + 1, 2)), dma((7,)), dma((7,)),
        ],
        compiler_params=pltpu.CompilerParams(
            collective_id=0, has_side_effects=True, vmem_limit_bytes=48 * 2**20
        ),
    )(
        *[pltpu.with_memory_space_constraint(operand, pltpu.HBM) for operand in operands]
    )
    return result.reshape(32, 4, VDIM)


def solution(mesh):
    return jax.shard_map(
        body,
        mesh=mesh,
        in_specs=(
            P(None, "head", None),
            P(None, ("seq", "head"), None),
            P(("seq", "head"), None, None),
            P("head", None, None),
            P(),
            P(),
            P(),
        ),
        out_specs=P(None, "head", None),
        check_vma=False,
    )
```

```python
import jax
import jax.numpy as jnp
from jax import lax
from jax.experimental import pallas as pl
from jax.experimental.pallas import tpu as pltpu
from jax.sharding import PartitionSpec as P

LAT = 512
ROPE = 64
WIDTH = LAT + ROPE
VDIM = 128
BEAM = 8
PAGE = 64
MAXP = 64
NZ = 8
RELATIVE = (4, 3, 5, 2, 6, 1, 7, 0)
CHUNKS = 2
CHUNK = 128 // CHUNKS
SLOT = {dz: k for k, dz in enumerate(RELATIVE)}
KEYS = 128
LOG2E = 1.4426950408889634
RATE = (VDIM + ROPE) ** -0.5 * LOG2E
LOWEST = -3.0e38
MESH = pl.DeviceIdType.MESH
F32 = jnp.float32
BF16 = jnp.bfloat16


def place(x, y, z, c):
    return ((y % 2) * 4 + x, z * 4 + (y // 2) * 2 + c)


def merge(parts, stats):
    peak = stats[0][0]
    for other, _ in stats[1:]:
        peak = jnp.maximum(peak, other)
    total = jnp.zeros_like(peak)
    latent = jnp.zeros((peak.shape[0], LAT), F32)
    for part, (part_peak, part_total) in zip(parts, stats):
        keep = jnp.exp2((part_peak - peak) * RATE)
        total = total + part_total * keep
        latent = latent + part[:, :LAT].astype(F32) * keep
    return peak, total, latent


def lines(peak, total):
    rows = peak.shape[0]
    lane = lax.broadcasted_iota(jnp.int32, (rows, KEYS), 1)
    row = lax.broadcasted_iota(jnp.int32, (rows, KEYS), 0) % 16
    spread = jnp.where(lane == row, peak, 0.0) + jnp.where(lane == row + 16, total, 0.0)
    return jnp.sum(spread.reshape(rows // 16, 16, KEYS), axis=1, keepdims=True)


def from_line(line):
    lane = lax.broadcasted_iota(jnp.int32, (16, KEYS), 1)
    row = lax.broadcasted_iota(jnp.int32, (16, KEYS), 0)
    return (
        jnp.sum(jnp.where(lane == row, line, 0.0), axis=1, keepdims=True),
        jnp.sum(jnp.where(lane == row + 16, line, 0.0), axis=1, keepdims=True))


def kernel(
    parents_hbm, lengths_hbm, lists_hbm, queries, prompt, pool, value_up,
    out,
    parents, lengths, page_lists,
    q_in, q_wide, q_mirror, q_buf, pool_in, keys, v_buf, lists, room, cap, scores, probs,
    part, stat, rs1, rs1_stat, zs, zs_stat_src, zs_stat, rs2_src, rs2_stat_src, rs2, rs2_stat, out_src,
    local_sem, key_send, key_recv, core_send, core_recv, swap_send, swap_recv, q_send, q_recv,
    rs1_send, rs1_recv, zs_send, zs_recv, rs2_send, rs2_recv, out_send, out_recv,
):
    seq = lax.axis_index("seq")
    head = lax.axis_index("head")
    x = seq % 4
    y_lo = seq // 4
    c = head % 2
    y_hi = (head // 2) % 2
    z = head // 4
    y = y_hi * 2 + y_lo
    x_hi = x // 2
    x_lo = x % 2
    step = 1 - 2 * c
    request = x_lo * 2 + y_lo

    def shifted(dx, dy, sign=1):
        return place((x + sign * dx + 4) % 4, (y + sign * dy + 4) % 4, z, c)

    other_core = place(x, y, z, 1 - c)
    mirror = place(x, 3 - y, z, c)
    key_moves = ((1, 0), (0, 1), (1, 1))
    scatter_moves = ((0, 2), (2, 0))
    out_moves = [(dx, dy) for dy in range(2) for dx in range(4) if (dx, dy) != (0, 0)]

    def out_place(dx, dy):
        return place((x + dx) % 4, y_hi * 2 + (y_lo + dy) % 2, z, c)

    barrier = pltpu.get_barrier_semaphore()
    senders = [place(x, y, (z + dz) % NZ, c) for dz in (2, 6, 1, 7)]
    senders += [shifted(dx * step, dy * step, -1) for dx, dy in key_moves]
    senders += [shifted(dx, dy) for dx, dy in scatter_moves]
    senders += [place(x, 3 - y, (z + dz) % NZ, c) for dz in (2, 6)]
    senders += [mirror, other_core]
    for sender in senders:
        pl.semaphore_signal(barrier, inc=1, device_id=sender, device_id_type=MESH)

    mirror_request = x_lo * 2 + 1 - y_lo
    own_q = pltpu.make_async_copy(queries.at[pl.ds(request * BEAM, BEAM)], q_in.at[0], local_sem.at[0])
    mirror_q = pltpu.make_async_copy(queries.at[pl.ds(mirror_request * BEAM, BEAM)], q_in.at[1], local_sem.at[1])
    own_pool = pltpu.make_async_copy(pool, pool_in, local_sem.at[2])
    own_prompt = pltpu.make_async_copy(prompt.at[request], keys.at[c, 0, 0], local_sem.at[3])
    own_v = pltpu.make_async_copy(value_up, v_buf, local_sem.at[4])
    get_parents = pltpu.make_async_copy(parents_hbm, parents, local_sem.at[5])
    get_lengths = pltpu.make_async_copy(lengths_hbm, lengths, local_sem.at[6])
    get_lists = pltpu.make_async_copy(lists_hbm, page_lists, local_sem.at[7])
    own_q.start()
    mirror_q.start()
    own_pool.start()
    own_prompt.start()
    get_parents.start()
    get_lengths.start()
    get_lists.start()
    own_v.start()

    def packed(i):
        for b in range(BEAM):
            block = q_in[i, b].astype(F32)
            half, start = b // 4, b % 4 * 4
            q_wide[i, start : start + 4, half * LAT : (half + 1) * LAT] = block[:, :LAT]
            if half:
                rotary = jnp.concatenate([q_in[i, b - 4].astype(F32)[:, LAT:], block[:, LAT:]], axis=1)
                q_wide[i, start : start + 4, 2 * LAT :] = rotary
        return q_wide[i].astype(BF16)

    mirror_q.wait()
    q_mirror[...] = packed(1)
    own_q.wait()
    q_buf[y_hi, SLOT[0]] = packed(0)
    own_pool.wait()
    flat_pool = pool_in[...].reshape(KEYS, WIDTH)
    keys[c, 0, 1, :LAT] = flat_pool[:, :LAT].T
    keys[c, 0, 1, LAT:] = flat_pool[:, LAT:].T

    pl.semaphore_wait(barrier, len(senders))

    copies = []

    def send(src, dst, send_sem, recv_sem, target):
        copy = pltpu.make_async_remote_copy(
            src_ref=src, dst_ref=dst, send_sem=send_sem, recv_sem=recv_sem, device_id=target, device_id_type=MESH
        )
        copy.start()
        copies.append(copy)
        return copy

    swap = send(q_mirror, q_buf.at[y_hi, SLOT[0]], swap_send, swap_recv, mirror)
    q_copies = {}

    def along_z(group, source, dz, slot):
        side = (y_hi + group) % 2
        q_copies[group, slot] = send(
            q_buf.at[side, source], q_buf.at[side, slot],
            q_send.at[group, slot], q_recv.at[group, slot], place(x, y, (z + dz + NZ) % NZ, c))

    def first_step(group, steps):
        for dz in steps:
            along_z(group, SLOT[0], dz, SLOT[NZ - dz])

    def second_step(group):
        q_copies[group, SLOT[6]].wait_recv()
        q_copies[group, SLOT[2]].wait_recv()
        along_z(group, SLOT[6] + c * (SLOT[2] - SLOT[6]), 2 * step, SLOT[4])
        along_z(group, SLOT[6], 1, SLOT[5])
        along_z(group, SLOT[2], -1, SLOT[3])

    def wait_queries(group):
        for dz in (1, 7, 3, 5, 4):
            q_copies[group, SLOT[dz]].wait_recv()

    first_step(0, (2, 6))
    for dz in (2, 6):
        slot = SLOT[NZ - dz]
        q_copies[1, slot] = send(
            q_mirror, q_buf.at[y_hi, slot], q_send.at[1, slot], q_recv.at[1, slot], place(x, 3 - y, (z + dz) % NZ, c))
    first_step(0, (1, 7))
    pieces = ((0, slice(0, WIDTH)), (1, slice(0, WIDTH // 2)), (1, slice(WIDTH // 2, WIDTH)))
    key_copies = {}

    def key_piece(kind, piece):
        pooled, rows = pieces[piece]
        dx, dy = key_moves[kind - 1]
        target_request = (x_lo + dx) % 2 * 2 + (y_lo + dy) % 2
        key_copies[kind, piece] = send(
            keys.at[c, 0, 1, rows] if pooled else prompt.at[target_request], keys.at[c, kind, pooled, rows],
            key_send.at[kind - 1, piece], key_recv.at[kind - 1, piece], shifted(dx * step, dy * step))

    core_copies = {}

    def to_core(kind, piece):
        pooled, rows = pieces[piece]
        core_copies[kind, piece] = send(
            keys.at[c, kind, pooled, rows], keys.at[c, kind, pooled, rows],
            core_send.at[kind, piece], core_recv.at[kind, piece], other_core)

    def wait_core(piece):
        for kind in range(4):
            core_copies[kind, piece].wait_recv()

    for kind in range(1, 4):
        key_piece(kind, 0)
    for piece in (1, 2):
        for kind in range(1, 4):
            key_piece(kind, piece)
    own_prompt.wait()
    for piece in range(3):
        to_core(0, piece)

    get_parents.wait()
    get_lengths.wait()
    get_lists.wait()
    slot = lax.broadcasted_iota(jnp.int32, (4, MAXP), 1)
    for b in range(BEAM):
        parent = parents[request * BEAM + b]
        lists[4 * b : 4 * b + 4, :] = jnp.broadcast_to(page_lists[pl.ds(parent, 1), :], (4, MAXP))
        room[4 * b : 4 * b + 4, :] = jnp.clip(lengths[parent] - slot * PAGE, 0, PAGE)
    chosen = lists[...]
    space = room[...]
    lane = lax.broadcasted_iota(jnp.int32, (4 * BEAM, KEYS), 1)
    for cc in range(2):
        sign = 1 - 2 * cc
        for kind, (dx, dy) in enumerate(((0, 0),) + key_moves):
            sy = (y - sign * dy + 4) % 4
            s_seq, s_head = place((x - sign * dx + 4) % 4, sy, z, cc)
            page = (s_seq * 32 + s_head) * 2
            live = [
                jnp.sum(jnp.where(chosen == page + i, space, 0), axis=1, keepdims=True) for i in range(2)
            ]
            seen = lane < jnp.where(lane < PAGE, live[0], live[1] + PAGE)
            cap[:, (cc * 4 + kind) * KEYS : (cc * 4 + kind + 1) * KEYS] = jnp.where(seen, jnp.inf, -jnp.inf)

    second_step(0)
    second_step(1)
    swap.wait_recv()
    first_step(1, (1, 7))
    for kind in range(1, 4):
        key_copies[kind, 0].wait_recv()
        to_core(kind, 0)
    for kind in range(1, 4):
        key_copies[kind, 1].wait_recv()
        to_core(kind, 1)

    def attend(group, pooled):
        block = q_buf[group].reshape(KEYS, 2 * LAT + 128)
        rotary = block[:, 2 * LAT :]
        lane = lax.broadcasted_iota(jnp.int32, (KEYS, 128), 1)
        rows = jnp.concatenate([
            jnp.concatenate([block[:, :LAT], jnp.where(lane < ROPE, rotary, 0)], axis=1),
            jnp.concatenate([block[:, LAT : 2 * LAT], jnp.where(lane < ROPE, 0, rotary)], axis=1),
        ], axis=0)
        for pair in range(4):
            cc, kind = pair // 2, pair % 2 * 2
            columns = jnp.concatenate([keys[cc, kind, pooled], keys[cc, kind + 1, pooled]], axis=1)
            columns = jnp.concatenate([columns, columns[LAT:]], axis=0)
            raw = jnp.dot(rows, columns, preferred_element_type=F32)
            if pooled:
                limit = cap[:, 2 * pair * KEYS : 2 * (pair + 1) * KEYS].reshape(2, 1, 16, 2 * KEYS)
                raw = jnp.minimum(raw.reshape(2, NZ, 16, 2 * KEYS), limit).reshape(2 * KEYS, 2 * KEYS)
            scores[:, 2 * pair * KEYS : 2 * (pair + 1) * KEYS] = raw
        peak = jnp.max(scores[...], axis=1, keepdims=True)
        if pooled:
            peak = jnp.maximum(peak, LOWEST)
        weights = jnp.exp2((scores[...] - peak) * RATE)
        total = jnp.sum(weights, axis=1, keepdims=True)
        probs[...] = weights.astype(BF16)
        values = jnp.concatenate([keys[cc, kind, pooled, :LAT] for cc in range(2) for kind in range(4)], axis=1)
        latent = lax.dot_general(
            probs[...], values, (((1,), (1,)), ((), ())), preferred_element_type=F32)
        return peak, total, latent

    def finish(group, first, z_first):
        peak1, total1, latent1 = first
        peak2, total2, latent2 = attend(group, 1)
        peak = jnp.maximum(peak1, peak2)
        keep1 = jnp.exp2((peak1 - peak) * RATE)
        keep2 = jnp.exp2((peak2 - peak) * RATE)
        total = total1 * keep1 + total2 * keep2
        part[group] = (latent1 * keep1 + latent2 * keep2).astype(BF16).reshape(2, KEYS, LAT)
        lane = lax.broadcasted_iota(jnp.int32, (KEYS, 128), 1)
        for half in range(2):
            half_rows = slice(half * KEYS, (half + 1) * KEYS)
            stat[group, half] = jnp.where(lane == 0, peak[half_rows], total[half_rows]).T[:8]
            if z_first:
                zs_stat_src[half] = lines(peak[half_rows], total[half_rows])

    def scatter(i, group, half):
        target = shifted(*scatter_moves[i])
        rs1_copies[i, CHUNKS] = send(
            stat.at[group, half], rs1_stat.at[i], rs1_send.at[i, CHUNKS], rs1_recv.at[i, CHUNKS], target)
        for chunk in range(CHUNKS):
            rows = pl.ds(CHUNK * chunk, CHUNK)
            rs1_copies[i, chunk] = send(
                part.at[group, half, rows], rs1.at[i, rows], rs1_send.at[i, chunk], rs1_recv.at[i, chunk], target)

    rs1_copies = {}
    zs_copies = []
    wait_queries(0)
    wait_core(0)
    prompt_a = attend(y_hi, 0)
    for kind in range(1, 4):
        key_copies[kind, 2].wait_recv()
        to_core(kind, 2)
    wait_queries(1)
    prompt_b = attend(1 - y_hi, 0)
    wait_core(1)
    wait_core(2)
    finish(y_hi, prompt_a, True)
    scatter(0, y_hi, x_hi)
    for slot in range(NZ - 1):
        target = place(x, y, (z + RELATIVE[slot]) % NZ, c)
        zs_copies.append(send(
            part.at[y_hi, 1 - x_hi, pl.ds(16 * slot, 16)], zs.at[slot], zs_send.at[slot, 0], zs_recv.at[slot, 0], target))
        zs_copies.append(send(
            zs_stat_src.at[1 - x_hi, slot], zs_stat.at[slot], zs_send.at[slot, 1], zs_recv.at[slot, 1], target))
    finish(1 - y_hi, prompt_b, False)
    scatter(1, 1 - y_hi, 1 - x_hi)

    rs2_copies = []

    def home(slot, target):
        rs2_copies.append(send(
            rs2_src.at[slot], rs2.at[slot], rs2_send.at[slot, 0], rs2_recv.at[slot, 0], target))
        rs2_copies.append(send(
            rs2_stat_src.at[slot], rs2_stat.at[slot], rs2_send.at[slot, 1], rs2_recv.at[slot, 1], target))

    for i in range(2):
        rs1_copies[i, CHUNKS].wait_recv()
    columns = jnp.concatenate([
        stat[1 - y_hi, x_hi], rs1_stat[0], rs1_stat[1], jnp.zeros((KEYS - 24, KEYS), F32)], axis=0).T
    per = CHUNK // 16
    for chunk in range(CHUNKS):
        rows = slice(chunk * CHUNK, (chunk + 1) * CHUNK)
        for i in range(2):
            rs1_copies[i, chunk].wait_recv()
        peak, total, latent = merge(
            [part[1 - y_hi, x_hi, rows], rs1[0, rows], rs1[1, rows]],
            [(columns[rows, 8 * i : 8 * i + 1], columns[rows, 8 * i + 1 : 8 * i + 2]) for i in range(3)])
        rs2_src[per * chunk : per * chunk + per] = latent.astype(BF16).reshape(per, 16, LAT)
        rs2_stat_src[per * chunk : per * chunk + per] = lines(peak, total)
        for slot in range(per * chunk, per * chunk + per):
            home(slot, place(x, 3 - y, (z + RELATIVE[slot]) % NZ, c))
    for copy in zs_copies:
        copy.wait_recv()
    peak, total, latent = merge(
        [part[y_hi, 1 - x_hi, 16 * SLOT[0] :]] + [zs[slot] for slot in range(NZ - 1)],
        [from_line(zs_stat_src[1 - x_hi, SLOT[0]])] + [from_line(zs_stat[slot]) for slot in range(NZ - 1)])
    rs2_src[NZ] = latent.astype(BF16)
    rs2_stat_src[NZ : NZ + 1] = lines(peak, total)
    home(NZ, place((x + 2) % 4, y_hi * 2 + 1 - y_lo, z, c))
    own_v.wait()
    for copy in rs2_copies:
        copy.wait_recv()
    peak, total, latent = merge([rs2[slot] for slot in range(NZ + 1)], [from_line(rs2_stat[slot]) for slot in range(NZ + 1)])
    latent = (latent / total).astype(BF16)
    attended = jnp.zeros((16, VDIM), F32)
    row = lax.broadcasted_iota(jnp.int32, (16, VDIM), 0)
    for h in range(4):
        product = jnp.dot(latent, v_buf[h], preferred_element_type=F32)
        attended = jnp.where(row % 4 == h, product, attended)
    out_src[...] = attended.astype(BF16)
    place_out = mirror_request * 2 + x_hi
    out_copies = []
    for i, (dx, dy) in enumerate(out_moves):
        out_copies.append(send(
            out_src, out.at[place_out], out_send.at[i], out_recv.at[i], out_place(dx, dy)))
    out[place_out] = out_src[...]
    for copy in out_copies:
        copy.wait_recv()
    for copy in copies:
        copy.wait_send()


def body(queries, prompt_latent, pool_latent, value_up, parents, page_lists, lengths):
    vmem = pl.BlockSpec(memory_space=pltpu.VMEM)
    hbm = pl.BlockSpec(memory_space=pltpu.HBM)
    operands = (parents, lengths, page_lists, queries, prompt_latent.swapaxes(1, 2), pool_latent, value_up)
    dma = pltpu.SemaphoreType.DMA
    result = pl.pallas_call(
        kernel,
        out_shape=pltpu.VMEM((8, 16, VDIM), BF16),
        in_specs=[hbm] * 7,
        out_specs=vmem,
        scratch_shapes=[
            pltpu.SMEM((32,), jnp.int32),
            pltpu.SMEM((32,), jnp.int32),
            pltpu.VMEM((32, MAXP), jnp.int32),
            pltpu.VMEM((2, BEAM, 4, WIDTH), BF16),
            pltpu.VMEM((2, 16, 2 * LAT + 128), F32),
            pltpu.VMEM((16, 2 * LAT + 128), BF16),
            pltpu.VMEM((2, NZ, 16, 2 * LAT + 128), BF16),
            pltpu.VMEM((2, PAGE, WIDTH), BF16),
            pltpu.VMEM((2, 4, 2, WIDTH, KEYS), BF16),
            pltpu.VMEM((4, LAT, VDIM), BF16),
            pltpu.VMEM((4 * BEAM, MAXP), jnp.int32),
            pltpu.VMEM((4 * BEAM, MAXP), jnp.int32),
            pltpu.VMEM((4 * BEAM, 8 * KEYS), F32),
            pltpu.VMEM((2 * KEYS, 8 * KEYS), F32),
            pltpu.VMEM((2 * KEYS, 8 * KEYS), BF16),
            pltpu.VMEM((2, 2, KEYS, LAT), BF16),
            pltpu.VMEM((2, 2, 8, KEYS), F32),
            pltpu.VMEM((2, KEYS, LAT), BF16),
            pltpu.VMEM((2, 8, KEYS), F32),
            pltpu.VMEM((NZ - 1, 16, LAT), BF16),
            pltpu.VMEM((2, NZ, 1, KEYS), F32),
            pltpu.VMEM((NZ - 1, 1, KEYS), F32),
            pltpu.VMEM((NZ + 1, 16, LAT), BF16),
            pltpu.VMEM((NZ + 1, 1, KEYS), F32),
            pltpu.VMEM((NZ + 1, 16, LAT), BF16),
            pltpu.VMEM((NZ + 1, 1, KEYS), F32),
            pltpu.VMEM((16, VDIM), BF16),
            dma((8,)), dma((3, 3)), dma((3, 3)), dma((4, 3)), dma((4, 3)), dma, dma, dma((2, NZ)), dma((2, NZ)),
            dma((2, CHUNKS + 1)), dma((2, CHUNKS + 1)), dma((NZ - 1, 2)), dma((NZ - 1, 2)), dma((NZ + 1, 2)), dma((NZ + 1, 2)), dma((7,)), dma((7,)),
        ],
        compiler_params=pltpu.CompilerParams(
            collective_id=0, has_side_effects=True, vmem_limit_bytes=48 * 2**20
        ),
    )(
        *[pltpu.with_memory_space_constraint(operand, pltpu.HBM) for operand in operands]
    )
    return result.reshape(32, 4, VDIM)


def solution(mesh):
    return jax.shard_map(
        body,
        mesh=mesh,
        in_specs=(
            P(None, "head", None),
            P(None, ("seq", "head"), None),
            P(("seq", "head"), None, None),
            P("head", None, None),
            P(),
            P(),
            P(),
        ),
        out_specs=P(None, "head", None),
        check_vma=False,
    )
```

```python
import jax
import jax.numpy as jnp
from jax import lax
from jax.experimental import pallas as pl
from jax.experimental.pallas import tpu as pltpu
from jax.sharding import PartitionSpec as P

LAT = 512
ROPE = 64
WIDTH = LAT + ROPE
VDIM = 128
BEAM = 8
PAGE = 64
MAXP = 64
NZ = 8
RELATIVE = (4, 3, 5, 2, 6, 1, 7, 0)
CHUNKS = 2
CHUNK = 128 // CHUNKS
SLOT = {dz: k for k, dz in enumerate(RELATIVE)}
KEYS = 128
LOG2E = 1.4426950408889634
RATE = (VDIM + ROPE) ** -0.5 * LOG2E
LOWEST = -3.0e38
MESH = pl.DeviceIdType.MESH
F32 = jnp.float32
BF16 = jnp.bfloat16


def place(x, y, z, c):
    return ((y % 2) * 4 + x, z * 4 + (y // 2) * 2 + c)


def merge(parts, stats):
    peak = stats[0][0]
    for other, _ in stats[1:]:
        peak = jnp.maximum(peak, other)
    total = jnp.zeros_like(peak)
    latent = jnp.zeros((peak.shape[0], LAT), F32)
    for part, (part_peak, part_total) in zip(parts, stats):
        keep = jnp.exp2((part_peak - peak) * RATE)
        total = total + part_total * keep
        latent = latent + part[:, :LAT].astype(F32) * keep
    return peak, total, latent


def lines(peak, total):
    rows = peak.shape[0]
    lane = lax.broadcasted_iota(jnp.int32, (rows, KEYS), 1)
    row = lax.broadcasted_iota(jnp.int32, (rows, KEYS), 0) % 16
    spread = jnp.where(lane == row, peak, 0.0) + jnp.where(lane == row + 16, total, 0.0)
    return jnp.sum(spread.reshape(rows // 16, 16, KEYS), axis=1, keepdims=True)


def from_line(line):
    lane = lax.broadcasted_iota(jnp.int32, (16, KEYS), 1)
    row = lax.broadcasted_iota(jnp.int32, (16, KEYS), 0)
    return (
        jnp.sum(jnp.where(lane == row, line, 0.0), axis=1, keepdims=True),
        jnp.sum(jnp.where(lane == row + 16, line, 0.0), axis=1, keepdims=True))


def kernel(
    parents_hbm, lengths_hbm, lists_hbm, queries, prompt, pool, value_up,
    out,
    parents, lengths, page_lists,
    q_in, q_wide, q_mirror, q_buf, pool_in, keys, v_buf, lists, room, cap, scores, probs,
    part, stat, rs1, rs1_stat, zs, zs_stat_src, zs_stat, rs2_src, rs2_stat_src, rs2, rs2_stat, out_src,
    local_sem, key_send, key_recv, core_send, core_recv, swap_send, swap_recv, q_send, q_recv,
    rs1_send, rs1_recv, zs_send, zs_recv, rs2_send, rs2_recv, out_send, out_recv,
):
    seq = lax.axis_index("seq")
    head = lax.axis_index("head")
    x = seq % 4
    y_lo = seq // 4
    c = head % 2
    y_hi = (head // 2) % 2
    z = head // 4
    y = y_hi * 2 + y_lo
    x_hi = x // 2
    x_lo = x % 2
    step = 1 - 2 * c
    request = x_lo * 2 + y_lo

    def shifted(dx, dy, sign=1):
        return place((x + sign * dx + 4) % 4, (y + sign * dy + 4) % 4, z, c)

    other_core = place(x, y, z, 1 - c)
    mirror = place(x, 3 - y, z, c)
    key_moves = ((1, 0), (0, 1), (1, 1))
    scatter_moves = ((0, 2), (2, 0))
    out_moves = [(dx, dy) for dy in range(2) for dx in range(4) if (dx, dy) != (0, 0)]

    def out_place(dx, dy):
        return place((x + dx) % 4, y_hi * 2 + (y_lo + dy) % 2, z, c)

    barrier = pltpu.get_barrier_semaphore()
    senders = [place(x, y, (z + dz) % NZ, c) for dz in (2, 6, 1, 7)]
    senders += [shifted(dx * step, dy * step, -1) for dx, dy in key_moves]
    senders += [shifted(dx, dy) for dx, dy in scatter_moves]
    senders += [place(x, 3 - y, (z + dz) % NZ, c) for dz in (2, 6)]
    senders += [mirror, other_core]
    for sender in senders:
        pl.semaphore_signal(barrier, inc=1, device_id=sender, device_id_type=MESH)

    mirror_request = x_lo * 2 + 1 - y_lo
    own_q = pltpu.make_async_copy(queries.at[pl.ds(request * BEAM, BEAM)], q_in.at[0], local_sem.at[0])
    mirror_q = pltpu.make_async_copy(queries.at[pl.ds(mirror_request * BEAM, BEAM)], q_in.at[1], local_sem.at[1])
    own_pool = pltpu.make_async_copy(pool, pool_in, local_sem.at[2])
    own_prompt = pltpu.make_async_copy(prompt.at[request], keys.at[c, 0, 0], local_sem.at[3])
    own_v = pltpu.make_async_copy(value_up, v_buf, local_sem.at[4])
    get_parents = pltpu.make_async_copy(parents_hbm, parents, local_sem.at[5])
    get_lengths = pltpu.make_async_copy(lengths_hbm, lengths, local_sem.at[6])
    get_lists = pltpu.make_async_copy(lists_hbm, page_lists, local_sem.at[7])
    own_q.start()
    mirror_q.start()
    own_pool.start()
    own_prompt.start()
    get_parents.start()
    get_lengths.start()
    get_lists.start()
    own_v.start()

    def packed(i):
        for b in range(BEAM):
            block = q_in[i, b].astype(F32)
            half, start = b // 4, b % 4 * 4
            q_wide[i, start : start + 4, half * LAT : (half + 1) * LAT] = block[:, :LAT]
            if half:
                rotary = jnp.concatenate([q_in[i, b - 4].astype(F32)[:, LAT:], block[:, LAT:]], axis=1)
                q_wide[i, start : start + 4, 2 * LAT :] = rotary
        return q_wide[i].astype(BF16)

    mirror_q.wait()
    q_mirror[...] = packed(1)
    own_q.wait()
    q_buf[y_hi, SLOT[0]] = packed(0)
    own_pool.wait()
    flat_pool = pool_in[...].reshape(KEYS, WIDTH)
    keys[c, 0, 1, :LAT] = flat_pool[:, :LAT].T
    keys[c, 0, 1, LAT:] = flat_pool[:, LAT:].T

    pl.semaphore_wait(barrier, len(senders))

    copies = []

    def send(src, dst, send_sem, recv_sem, target):
        copy = pltpu.make_async_remote_copy(
            src_ref=src, dst_ref=dst, send_sem=send_sem, recv_sem=recv_sem, device_id=target, device_id_type=MESH
        )
        copy.start()
        copies.append(copy)
        return copy

    swap = send(q_mirror, q_buf.at[y_hi, SLOT[0]], swap_send, swap_recv, mirror)
    q_copies = {}

    def along_z(group, source, dz, slot):
        side = (y_hi + group) % 2
        q_copies[group, slot] = send(
            q_buf.at[side, source], q_buf.at[side, slot],
            q_send.at[group, slot], q_recv.at[group, slot], place(x, y, (z + dz + NZ) % NZ, c))

    def first_step(group, steps):
        for dz in steps:
            along_z(group, SLOT[0], dz, SLOT[NZ - dz])

    def second_step(group):
        q_copies[group, SLOT[6]].wait_recv()
        q_copies[group, SLOT[2]].wait_recv()
        along_z(group, SLOT[6] + c * (SLOT[2] - SLOT[6]), 2 * step, SLOT[4])
        along_z(group, SLOT[6], 1, SLOT[5])
        along_z(group, SLOT[2], -1, SLOT[3])

    def wait_queries(group):
        for dz in (1, 7, 3, 5, 4):
            q_copies[group, SLOT[dz]].wait_recv()

    first_step(0, (2, 6))
    for dz in (2, 6):
        slot = SLOT[NZ - dz]
        q_copies[1, slot] = send(
            q_mirror, q_buf.at[y_hi, slot], q_send.at[1, slot], q_recv.at[1, slot], place(x, 3 - y, (z + dz) % NZ, c))
    first_step(0, (1, 7))
    pieces = ((0, slice(0, WIDTH)), (1, slice(0, WIDTH // 2)), (1, slice(WIDTH // 2, WIDTH)))
    key_copies = {}

    def key_piece(kind, piece):
        pooled, rows = pieces[piece]
        dx, dy = key_moves[kind - 1]
        target_request = (x_lo + dx) % 2 * 2 + (y_lo + dy) % 2
        key_copies[kind, piece] = send(
            keys.at[c, 0, 1, rows] if pooled else prompt.at[target_request], keys.at[c, kind, pooled, rows],
            key_send.at[kind - 1, piece], key_recv.at[kind - 1, piece], shifted(dx * step, dy * step))

    core_copies = {}

    def to_core(kind, piece):
        pooled, rows = pieces[piece]
        core_copies[kind, piece] = send(
            keys.at[c, kind, pooled, rows], keys.at[c, kind, pooled, rows],
            core_send.at[kind, piece], core_recv.at[kind, piece], other_core)

    def wait_core(piece):
        for kind in range(4):
            core_copies[kind, piece].wait_recv()

    for kind in range(1, 4):
        key_piece(kind, 0)
    for piece in (1, 2):
        for kind in range(1, 4):
            key_piece(kind, piece)
    own_prompt.wait()
    for piece in range(3):
        to_core(0, piece)

    get_parents.wait()
    get_lengths.wait()
    get_lists.wait()
    slot = lax.broadcasted_iota(jnp.int32, (4, MAXP), 1)
    for b in range(BEAM):
        parent = parents[request * BEAM + b]
        lists[4 * b : 4 * b + 4, :] = jnp.broadcast_to(page_lists[pl.ds(parent, 1), :], (4, MAXP))
        room[4 * b : 4 * b + 4, :] = jnp.clip(lengths[parent] - slot * PAGE, 0, PAGE)
    chosen = lists[...]
    space = room[...]
    lane = lax.broadcasted_iota(jnp.int32, (4 * BEAM, KEYS), 1)
    for cc in range(2):
        sign = 1 - 2 * cc
        for kind, (dx, dy) in enumerate(((0, 0),) + key_moves):
            sy = (y - sign * dy + 4) % 4
            s_seq, s_head = place((x - sign * dx + 4) % 4, sy, z, cc)
            page = (s_seq * 32 + s_head) * 2
            live = [
                jnp.sum(jnp.where(chosen == page + i, space, 0), axis=1, keepdims=True) for i in range(2)
            ]
            seen = lane < jnp.where(lane < PAGE, live[0], live[1] + PAGE)
            cap[:, (cc * 4 + kind) * KEYS : (cc * 4 + kind + 1) * KEYS] = jnp.where(seen, jnp.inf, -jnp.inf)

    second_step(0)
    second_step(1)
    for kind in range(1, 4):
        key_copies[kind, 0].wait_recv()
        to_core(kind, 0)
    swap.wait_recv()
    first_step(1, (1, 7))
    for kind in range(1, 4):
        key_copies[kind, 1].wait_recv()
        to_core(kind, 1)

    def attend(group, pooled):
        block = q_buf[group].reshape(KEYS, 2 * LAT + 128)
        rotary = block[:, 2 * LAT :]
        lane = lax.broadcasted_iota(jnp.int32, (KEYS, 128), 1)
        rows = jnp.concatenate([
            jnp.concatenate([block[:, :LAT], jnp.where(lane < ROPE, rotary, 0)], axis=1),
            jnp.concatenate([block[:, LAT : 2 * LAT], jnp.where(lane < ROPE, 0, rotary)], axis=1),
        ], axis=0)
        for pair in range(4):
            cc, kind = pair // 2, pair % 2 * 2
            columns = jnp.concatenate([keys[cc, kind, pooled], keys[cc, kind + 1, pooled]], axis=1)
            columns = jnp.concatenate([columns, columns[LAT:]], axis=0)
            raw = jnp.dot(rows, columns, preferred_element_type=F32)
            if pooled:
                limit = cap[:, 2 * pair * KEYS : 2 * (pair + 1) * KEYS].reshape(2, 1, 16, 2 * KEYS)
                raw = jnp.minimum(raw.reshape(2, NZ, 16, 2 * KEYS), limit).reshape(2 * KEYS, 2 * KEYS)
            scores[:, 2 * pair * KEYS : 2 * (pair + 1) * KEYS] = raw
        peak = jnp.max(scores[...], axis=1, keepdims=True)
        if pooled:
            peak = jnp.maximum(peak, LOWEST)
        weights = jnp.exp2((scores[...] - peak) * RATE)
        total = jnp.sum(weights, axis=1, keepdims=True)
        probs[...] = weights.astype(BF16)
        values = jnp.concatenate([keys[cc, kind, pooled, :LAT] for cc in range(2) for kind in range(4)], axis=1)
        latent = lax.dot_general(
            probs[...], values, (((1,), (1,)), ((), ())), preferred_element_type=F32)
        return peak, total, latent

    def finish(group, first, z_first):
        peak1, total1, latent1 = first
        peak2, total2, latent2 = attend(group, 1)
        peak = jnp.maximum(peak1, peak2)
        keep1 = jnp.exp2((peak1 - peak) * RATE)
        keep2 = jnp.exp2((peak2 - peak) * RATE)
        total = total1 * keep1 + total2 * keep2
        part[group] = (latent1 * keep1 + latent2 * keep2).astype(BF16).reshape(2, KEYS, LAT)
        lane = lax.broadcasted_iota(jnp.int32, (KEYS, 128), 1)
        for half in range(2):
            half_rows = slice(half * KEYS, (half + 1) * KEYS)
            stat[group, half] = jnp.where(lane == 0, peak[half_rows], total[half_rows]).T[:8]
            if z_first:
                zs_stat_src[half] = lines(peak[half_rows], total[half_rows])

    def scatter(i, group, half):
        target = shifted(*scatter_moves[i])
        rs1_copies[i, CHUNKS] = send(
            stat.at[group, half], rs1_stat.at[i], rs1_send.at[i, CHUNKS], rs1_recv.at[i, CHUNKS], target)
        for chunk in range(CHUNKS):
            rows = pl.ds(CHUNK * chunk, CHUNK)
            rs1_copies[i, chunk] = send(
                part.at[group, half, rows], rs1.at[i, rows], rs1_send.at[i, chunk], rs1_recv.at[i, chunk], target)

    rs1_copies = {}
    zs_copies = []
    wait_queries(0)
    wait_core(0)
    prompt_a = attend(y_hi, 0)
    for kind in range(1, 4):
        key_copies[kind, 2].wait_recv()
        to_core(kind, 2)
    wait_queries(1)
    prompt_b = attend(1 - y_hi, 0)
    wait_core(1)
    wait_core(2)
    finish(y_hi, prompt_a, True)
    scatter(0, y_hi, x_hi)
    finish(1 - y_hi, prompt_b, False)
    scatter(1, 1 - y_hi, 1 - x_hi)
    for slot in range(NZ - 1):
        target = place(x, y, (z + RELATIVE[slot]) % NZ, c)
        zs_copies.append(send(
            part.at[y_hi, 1 - x_hi, pl.ds(16 * slot, 16)], zs.at[slot], zs_send.at[slot, 0], zs_recv.at[slot, 0], target))
        zs_copies.append(send(
            zs_stat_src.at[1 - x_hi, slot], zs_stat.at[slot], zs_send.at[slot, 1], zs_recv.at[slot, 1], target))

    rs2_copies = []

    def home(slot, target):
        rs2_copies.append(send(
            rs2_src.at[slot], rs2.at[slot], rs2_send.at[slot, 0], rs2_recv.at[slot, 0], target))
        rs2_copies.append(send(
            rs2_stat_src.at[slot], rs2_stat.at[slot], rs2_send.at[slot, 1], rs2_recv.at[slot, 1], target))

    for i in range(2):
        rs1_copies[i, CHUNKS].wait_recv()
    columns = jnp.concatenate([
        stat[1 - y_hi, x_hi], rs1_stat[0], rs1_stat[1], jnp.zeros((KEYS - 24, KEYS), F32)], axis=0).T
    per = CHUNK // 16
    for chunk in range(CHUNKS):
        rows = slice(chunk * CHUNK, (chunk + 1) * CHUNK)
        for i in range(2):
            rs1_copies[i, chunk].wait_recv()
        peak, total, latent = merge(
            [part[1 - y_hi, x_hi, rows], rs1[0, rows], rs1[1, rows]],
            [(columns[rows, 8 * i : 8 * i + 1], columns[rows, 8 * i + 1 : 8 * i + 2]) for i in range(3)])
        rs2_src[per * chunk : per * chunk + per] = latent.astype(BF16).reshape(per, 16, LAT)
        rs2_stat_src[per * chunk : per * chunk + per] = lines(peak, total)
        for slot in range(per * chunk, per * chunk + per):
            home(slot, place(x, 3 - y, (z + RELATIVE[slot]) % NZ, c))
    for copy in zs_copies:
        copy.wait_recv()
    peak, total, latent = merge(
        [part[y_hi, 1 - x_hi, 16 * SLOT[0] :]] + [zs[slot] for slot in range(NZ - 1)],
        [from_line(zs_stat_src[1 - x_hi, SLOT[0]])] + [from_line(zs_stat[slot]) for slot in range(NZ - 1)])
    rs2_src[NZ] = latent.astype(BF16)
    rs2_stat_src[NZ : NZ + 1] = lines(peak, total)
    home(NZ, place((x + 2) % 4, y_hi * 2 + 1 - y_lo, z, c))
    own_v.wait()
    for copy in rs2_copies:
        copy.wait_recv()
    peak, total, latent = merge([rs2[slot] for slot in range(NZ + 1)], [from_line(rs2_stat[slot]) for slot in range(NZ + 1)])
    latent = (latent / total).astype(BF16)
    attended = jnp.zeros((16, VDIM), F32)
    row = lax.broadcasted_iota(jnp.int32, (16, VDIM), 0)
    for h in range(4):
        product = jnp.dot(latent, v_buf[h], preferred_element_type=F32)
        attended = jnp.where(row % 4 == h, product, attended)
    out_src[...] = attended.astype(BF16)
    place_out = mirror_request * 2 + x_hi
    out_copies = []
    for i, (dx, dy) in enumerate(out_moves):
        out_copies.append(send(
            out_src, out.at[place_out], out_send.at[i], out_recv.at[i], out_place(dx, dy)))
    out[place_out] = out_src[...]
    for copy in out_copies:
        copy.wait_recv()
    for copy in copies:
        copy.wait_send()


def body(queries, prompt_latent, pool_latent, value_up, parents, page_lists, lengths):
    vmem = pl.BlockSpec(memory_space=pltpu.VMEM)
    hbm = pl.BlockSpec(memory_space=pltpu.HBM)
    operands = (parents, lengths, page_lists, queries, prompt_latent.swapaxes(1, 2), pool_latent, value_up)
    dma = pltpu.SemaphoreType.DMA
    result = pl.pallas_call(
        kernel,
        out_shape=pltpu.VMEM((8, 16, VDIM), BF16),
        in_specs=[hbm] * 7,
        out_specs=vmem,
        scratch_shapes=[
            pltpu.SMEM((32,), jnp.int32),
            pltpu.SMEM((32,), jnp.int32),
            pltpu.VMEM((32, MAXP), jnp.int32),
            pltpu.VMEM((2, BEAM, 4, WIDTH), BF16),
            pltpu.VMEM((2, 16, 2 * LAT + 128), F32),
            pltpu.VMEM((16, 2 * LAT + 128), BF16),
            pltpu.VMEM((2, NZ, 16, 2 * LAT + 128), BF16),
            pltpu.VMEM((2, PAGE, WIDTH), BF16),
            pltpu.VMEM((2, 4, 2, WIDTH, KEYS), BF16),
            pltpu.VMEM((4, LAT, VDIM), BF16),
            pltpu.VMEM((4 * BEAM, MAXP), jnp.int32),
            pltpu.VMEM((4 * BEAM, MAXP), jnp.int32),
            pltpu.VMEM((4 * BEAM, 8 * KEYS), F32),
            pltpu.VMEM((2 * KEYS, 8 * KEYS), F32),
            pltpu.VMEM((2 * KEYS, 8 * KEYS), BF16),
            pltpu.VMEM((2, 2, KEYS, LAT), BF16),
            pltpu.VMEM((2, 2, 8, KEYS), F32),
            pltpu.VMEM((2, KEYS, LAT), BF16),
            pltpu.VMEM((2, 8, KEYS), F32),
            pltpu.VMEM((NZ - 1, 16, LAT), BF16),
            pltpu.VMEM((2, NZ, 1, KEYS), F32),
            pltpu.VMEM((NZ - 1, 1, KEYS), F32),
            pltpu.VMEM((NZ + 1, 16, LAT), BF16),
            pltpu.VMEM((NZ + 1, 1, KEYS), F32),
            pltpu.VMEM((NZ + 1, 16, LAT), BF16),
            pltpu.VMEM((NZ + 1, 1, KEYS), F32),
            pltpu.VMEM((16, VDIM), BF16),
            dma((8,)), dma((3, 3)), dma((3, 3)), dma((4, 3)), dma((4, 3)), dma, dma, dma((2, NZ)), dma((2, NZ)),
            dma((2, CHUNKS + 1)), dma((2, CHUNKS + 1)), dma((NZ - 1, 2)), dma((NZ - 1, 2)), dma((NZ + 1, 2)), dma((NZ + 1, 2)), dma((7,)), dma((7,)),
        ],
        compiler_params=pltpu.CompilerParams(
            collective_id=0, has_side_effects=True, vmem_limit_bytes=48 * 2**20
        ),
    )(
        *[pltpu.with_memory_space_constraint(operand, pltpu.HBM) for operand in operands]
    )
    return result.reshape(32, 4, VDIM)


def solution(mesh):
    return jax.shard_map(
        body,
        mesh=mesh,
        in_specs=(
            P(None, "head", None),
            P(None, ("seq", "head"), None),
            P(("seq", "head"), None, None),
            P("head", None, None),
            P(),
            P(),
            P(),
        ),
        out_specs=P(None, "head", None),
        check_vma=False,
    )
```

```python
import jax
import jax.numpy as jnp
from jax import lax
from jax.experimental import pallas as pl
from jax.experimental.pallas import tpu as pltpu
from jax.sharding import PartitionSpec as P

LAT = 512
ROPE = 64
WIDTH = LAT + ROPE
VDIM = 128
BEAM = 8
PAGE = 64
MAXP = 64
NZ = 8
RELATIVE = (4, 3, 5, 2, 6, 1, 7, 0)
CHUNKS = 2
CHUNK = 128 // CHUNKS
SLOT = {dz: k for k, dz in enumerate(RELATIVE)}
KEYS = 128
LOG2E = 1.4426950408889634
RATE = (VDIM + ROPE) ** -0.5 * LOG2E
LOWEST = -3.0e38
MESH = pl.DeviceIdType.MESH
F32 = jnp.float32
BF16 = jnp.bfloat16


def place(x, y, z, c):
    return ((y % 2) * 4 + x, z * 4 + (y // 2) * 2 + c)


def merge(parts, stats):
    peak = stats[0][0]
    for other, _ in stats[1:]:
        peak = jnp.maximum(peak, other)
    total = jnp.zeros_like(peak)
    latent = jnp.zeros((peak.shape[0], LAT), F32)
    for part, (part_peak, part_total) in zip(parts, stats):
        keep = jnp.exp2((part_peak - peak) * RATE)
        total = total + part_total * keep
        latent = latent + part[:, :LAT].astype(F32) * keep
    return peak, total, latent


def lines(peak, total):
    rows = peak.shape[0]
    lane = lax.broadcasted_iota(jnp.int32, (rows, KEYS), 1)
    row = lax.broadcasted_iota(jnp.int32, (rows, KEYS), 0) % 16
    spread = jnp.where(lane == row, peak, 0.0) + jnp.where(lane == row + 16, total, 0.0)
    return jnp.sum(spread.reshape(rows // 16, 16, KEYS), axis=1, keepdims=True)


def from_line(line):
    lane = lax.broadcasted_iota(jnp.int32, (16, KEYS), 1)
    row = lax.broadcasted_iota(jnp.int32, (16, KEYS), 0)
    return (
        jnp.sum(jnp.where(lane == row, line, 0.0), axis=1, keepdims=True),
        jnp.sum(jnp.where(lane == row + 16, line, 0.0), axis=1, keepdims=True))


def kernel(
    parents_hbm, lengths_hbm, lists_hbm, queries, prompt, pool, value_up,
    out,
    parents, lengths, page_lists,
    q_in, q_wide, q_mirror, q_buf, pool_in, keys, v_buf, lists, room, cap, scores, probs,
    part, stat, rs1, rs1_stat, zs, zs_stat_src, zs_stat, rs2_src, rs2_stat_src, rs2, rs2_stat, out_src,
    local_sem, key_send, key_recv, core_send, core_recv, swap_send, swap_recv, q_send, q_recv,
    rs1_send, rs1_recv, zs_send, zs_recv, rs2_send, rs2_recv, out_send, out_recv,
):
    seq = lax.axis_index("seq")
    head = lax.axis_index("head")
    x = seq % 4
    y_lo = seq // 4
    c = head % 2
    y_hi = (head // 2) % 2
    z = head // 4
    y = y_hi * 2 + y_lo
    x_hi = x // 2
    x_lo = x % 2
    step = 1 - 2 * c
    request = x_lo * 2 + y_lo

    def shifted(dx, dy, sign=1):
        return place((x + sign * dx + 4) % 4, (y + sign * dy + 4) % 4, z, c)

    other_core = place(x, y, z, 1 - c)
    mirror = place(x, 3 - y, z, c)
    key_moves = ((1, 0), (0, 1), (1, 1))
    scatter_moves = ((0, 2), (2, 0))
    out_moves = [(dx, dy) for dy in range(2) for dx in range(4) if (dx, dy) != (0, 0)]

    def out_place(dx, dy):
        return place((x + dx) % 4, y_hi * 2 + (y_lo + dy) % 2, z, c)

    barrier = pltpu.get_barrier_semaphore()
    senders = [place(x, y, (z + dz) % NZ, c) for dz in (2, 6, 1, 7)]
    senders += [shifted(dx * step, dy * step, -1) for dx, dy in key_moves]
    senders += [shifted(dx, dy) for dx, dy in scatter_moves]
    senders += [place(x, 3 - y, (z + dz) % NZ, c) for dz in (2, 6)]
    senders += [mirror, other_core]
    for sender in senders:
        pl.semaphore_signal(barrier, inc=1, device_id=sender, device_id_type=MESH)

    mirror_request = x_lo * 2 + 1 - y_lo
    own_q = pltpu.make_async_copy(queries.at[pl.ds(request * BEAM, BEAM)], q_in.at[0], local_sem.at[0])
    mirror_q = pltpu.make_async_copy(queries.at[pl.ds(mirror_request * BEAM, BEAM)], q_in.at[1], local_sem.at[1])
    own_pool = pltpu.make_async_copy(pool, pool_in, local_sem.at[2])
    own_prompt = pltpu.make_async_copy(prompt.at[request], keys.at[c, 0, 0], local_sem.at[3])
    own_v = pltpu.make_async_copy(value_up, v_buf, local_sem.at[4])
    get_parents = pltpu.make_async_copy(parents_hbm, parents, local_sem.at[5])
    get_lengths = pltpu.make_async_copy(lengths_hbm, lengths, local_sem.at[6])
    get_lists = pltpu.make_async_copy(lists_hbm, page_lists, local_sem.at[7])
    own_q.start()
    mirror_q.start()
    own_pool.start()
    own_prompt.start()
    get_parents.start()
    get_lengths.start()
    get_lists.start()
    own_v.start()

    def packed(i):
        for b in range(BEAM):
            block = q_in[i, b].astype(F32)
            half, start = b // 4, b % 4 * 4
            q_wide[i, start : start + 4, half * LAT : (half + 1) * LAT] = block[:, :LAT]
            if half:
                rotary = jnp.concatenate([q_in[i, b - 4].astype(F32)[:, LAT:], block[:, LAT:]], axis=1)
                q_wide[i, start : start + 4, 2 * LAT :] = rotary
        return q_wide[i].astype(BF16)

    mirror_q.wait()
    q_mirror[...] = packed(1)
    own_q.wait()
    q_buf[y_hi, SLOT[0]] = packed(0)
    own_pool.wait()
    flat_pool = pool_in[...].reshape(KEYS, WIDTH)
    keys[c, 0, 1, :LAT] = flat_pool[:, :LAT].T
    keys[c, 0, 1, LAT:] = flat_pool[:, LAT:].T

    pl.semaphore_wait(barrier, len(senders))

    copies = []

    def send(src, dst, send_sem, recv_sem, target):
        copy = pltpu.make_async_remote_copy(
            src_ref=src, dst_ref=dst, send_sem=send_sem, recv_sem=recv_sem, device_id=target, device_id_type=MESH
        )
        copy.start()
        copies.append(copy)
        return copy

    swap = send(q_mirror, q_buf.at[y_hi, SLOT[0]], swap_send, swap_recv, mirror)
    q_copies = {}

    def along_z(group, source, dz, slot):
        side = (y_hi + group) % 2
        q_copies[group, slot] = send(
            q_buf.at[side, source], q_buf.at[side, slot],
            q_send.at[group, slot], q_recv.at[group, slot], place(x, y, (z + dz + NZ) % NZ, c))

    def first_step(group, steps):
        for dz in steps:
            along_z(group, SLOT[0], dz, SLOT[NZ - dz])

    def second_step(group):
        q_copies[group, SLOT[6]].wait_recv()
        q_copies[group, SLOT[2]].wait_recv()
        along_z(group, SLOT[6] + c * (SLOT[2] - SLOT[6]), 2 * step, SLOT[4])
        along_z(group, SLOT[6], 1, SLOT[5])
        along_z(group, SLOT[2], -1, SLOT[3])

    def wait_queries(group):
        for dz in (1, 7, 3, 5, 4):
            q_copies[group, SLOT[dz]].wait_recv()

    first_step(0, (2, 6))
    for dz in (2, 6):
        slot = SLOT[NZ - dz]
        q_copies[1, slot] = send(
            q_mirror, q_buf.at[y_hi, slot], q_send.at[1, slot], q_recv.at[1, slot], place(x, 3 - y, (z + dz) % NZ, c))
    first_step(0, (1, 7))
    pieces = ((0, slice(0, WIDTH)), (1, slice(0, WIDTH // 2)), (1, slice(WIDTH // 2, WIDTH)))
    key_copies = {}

    def key_piece(kind, piece):
        pooled, rows = pieces[piece]
        dx, dy = key_moves[kind - 1]
        target_request = (x_lo + dx) % 2 * 2 + (y_lo + dy) % 2
        key_copies[kind, piece] = send(
            keys.at[c, 0, 1, rows] if pooled else prompt.at[target_request], keys.at[c, kind, pooled, rows],
            key_send.at[kind - 1, piece], key_recv.at[kind - 1, piece], shifted(dx * step, dy * step))

    core_copies = {}

    def to_core(kind, piece):
        pooled, rows = pieces[piece]
        core_copies[kind, piece] = send(
            keys.at[c, kind, pooled, rows], keys.at[c, kind, pooled, rows],
            core_send.at[kind, piece], core_recv.at[kind, piece], other_core)

    def wait_core(piece):
        for kind in range(4):
            core_copies[kind, piece].wait_recv()

    for kind in range(1, 4):
        key_piece(kind, 0)
    for piece in (1, 2):
        for kind in range(1, 4):
            key_piece(kind, piece)
    own_prompt.wait()
    for piece in range(3):
        to_core(0, piece)

    get_parents.wait()
    get_lengths.wait()
    get_lists.wait()
    slot = lax.broadcasted_iota(jnp.int32, (4, MAXP), 1)
    for b in range(BEAM):
        parent = parents[request * BEAM + b]
        lists[4 * b : 4 * b + 4, :] = jnp.broadcast_to(page_lists[pl.ds(parent, 1), :], (4, MAXP))
        room[4 * b : 4 * b + 4, :] = jnp.clip(lengths[parent] - slot * PAGE, 0, PAGE)
    chosen = lists[...]
    space = room[...]
    lane = lax.broadcasted_iota(jnp.int32, (4 * BEAM, KEYS), 1)
    for cc in range(2):
        sign = 1 - 2 * cc
        for kind, (dx, dy) in enumerate(((0, 0),) + key_moves):
            sy = (y - sign * dy + 4) % 4
            s_seq, s_head = place((x - sign * dx + 4) % 4, sy, z, cc)
            page = (s_seq * 32 + s_head) * 2
            live = [
                jnp.sum(jnp.where(chosen == page + i, space, 0), axis=1, keepdims=True) for i in range(2)
            ]
            seen = lane < jnp.where(lane < PAGE, live[0], live[1] + PAGE)
            cap[:, (cc * 4 + kind) * KEYS : (cc * 4 + kind + 1) * KEYS] = jnp.where(seen, jnp.inf, -jnp.inf)

    second_step(0)
    second_step(1)
    for kind in range(1, 4):
        key_copies[kind, 0].wait_recv()
        to_core(kind, 0)
    swap.wait_recv()
    first_step(1, (1, 7))
    for kind in range(1, 4):
        key_copies[kind, 1].wait_recv()
        to_core(kind, 1)

    def attend(group, pooled):
        block = q_buf[group].reshape(KEYS, 2 * LAT + 128)
        rotary = block[:, 2 * LAT :]
        lane = lax.broadcasted_iota(jnp.int32, (KEYS, 128), 1)
        rows = jnp.concatenate([
            jnp.concatenate([block[:, :LAT], jnp.where(lane < ROPE, rotary, 0)], axis=1),
            jnp.concatenate([block[:, LAT : 2 * LAT], jnp.where(lane < ROPE, 0, rotary)], axis=1),
        ], axis=0)
        for pair in range(4):
            cc, kind = pair // 2, pair % 2 * 2
            columns = jnp.concatenate([keys[cc, kind, pooled], keys[cc, kind + 1, pooled]], axis=1)
            columns = jnp.concatenate([columns, columns[LAT:]], axis=0)
            raw = jnp.dot(rows, columns, preferred_element_type=F32)
            if pooled:
                limit = cap[:, 2 * pair * KEYS : 2 * (pair + 1) * KEYS].reshape(2, 1, 16, 2 * KEYS)
                raw = jnp.minimum(raw.reshape(2, NZ, 16, 2 * KEYS), limit).reshape(2 * KEYS, 2 * KEYS)
            scores[:, 2 * pair * KEYS : 2 * (pair + 1) * KEYS] = raw
        peak = jnp.max(scores[...], axis=1, keepdims=True)
        if pooled:
            peak = jnp.maximum(peak, LOWEST)
        weights = jnp.exp2((scores[...] - peak) * RATE)
        total = jnp.sum(weights, axis=1, keepdims=True)
        probs[...] = weights.astype(BF16)
        values = jnp.concatenate([keys[cc, kind, pooled, :LAT] for cc in range(2) for kind in range(4)], axis=1)
        latent = lax.dot_general(
            probs[...], values, (((1,), (1,)), ((), ())), preferred_element_type=F32)
        return peak, total, latent

    def finish(group, first, z_first):
        peak1, total1, latent1 = first
        peak2, total2, latent2 = attend(group, 1)
        peak = jnp.maximum(peak1, peak2)
        keep1 = jnp.exp2((peak1 - peak) * RATE)
        keep2 = jnp.exp2((peak2 - peak) * RATE)
        total = total1 * keep1 + total2 * keep2
        part[group] = (latent1 * keep1 + latent2 * keep2).astype(BF16).reshape(2, KEYS, LAT)
        lane = lax.broadcasted_iota(jnp.int32, (KEYS, 128), 1)
        for half in range(2):
            half_rows = slice(half * KEYS, (half + 1) * KEYS)
            stat[group, half] = jnp.where(lane == 0, peak[half_rows], total[half_rows]).T[:8]
            if z_first:
                zs_stat_src[half] = lines(peak[half_rows], total[half_rows])

    def scatter(i, group, half):
        target = shifted(*scatter_moves[i])
        rs1_copies[i, CHUNKS] = send(
            stat.at[group, half], rs1_stat.at[i], rs1_send.at[i, CHUNKS], rs1_recv.at[i, CHUNKS], target)
        for chunk in range(CHUNKS):
            rows = pl.ds(CHUNK * chunk, CHUNK)
            rs1_copies[i, chunk] = send(
                part.at[group, half, rows], rs1.at[i, rows], rs1_send.at[i, chunk], rs1_recv.at[i, chunk], target)

    rs1_copies = {}
    zs_copies = []
    wait_queries(0)
    wait_core(0)
    prompt_a = attend(y_hi, 0)
    for kind in range(1, 4):
        key_copies[kind, 2].wait_recv()
        to_core(kind, 2)
    wait_queries(1)
    prompt_b = attend(1 - y_hi, 0)
    wait_core(1)
    wait_core(2)
    finish(y_hi, prompt_a, True)
    scatter(0, y_hi, x_hi)
    for slot in range(NZ - 1):
        target = place(x, y, (z + RELATIVE[slot]) % NZ, c)
        zs_copies.append(send(
            part.at[y_hi, 1 - x_hi, pl.ds(16 * slot, 16)], zs.at[slot], zs_send.at[slot, 0], zs_recv.at[slot, 0], target))
        zs_copies.append(send(
            zs_stat_src.at[1 - x_hi, slot], zs_stat.at[slot], zs_send.at[slot, 1], zs_recv.at[slot, 1], target))
    finish(1 - y_hi, prompt_b, False)
    scatter(1, 1 - y_hi, 1 - x_hi)

    rs2_copies = []

    def home(slot, target):
        rs2_copies.append(send(
            rs2_src.at[slot], rs2.at[slot], rs2_send.at[slot, 0], rs2_recv.at[slot, 0], target))
        rs2_copies.append(send(
            rs2_stat_src.at[slot], rs2_stat.at[slot], rs2_send.at[slot, 1], rs2_recv.at[slot, 1], target))

    for i in range(2):
        rs1_copies[i, CHUNKS].wait_recv()
    columns = jnp.concatenate([
        stat[1 - y_hi, x_hi], rs1_stat[0], rs1_stat[1], jnp.zeros((KEYS - 24, KEYS), F32)], axis=0).T
    per = CHUNK // 16
    for chunk in range(CHUNKS):
        rows = slice(chunk * CHUNK, (chunk + 1) * CHUNK)
        for i in range(2):
            rs1_copies[i, chunk].wait_recv()
        peak, total, latent = merge(
            [part[1 - y_hi, x_hi, rows], rs1[0, rows], rs1[1, rows]],
            [(columns[rows, 8 * i : 8 * i + 1], columns[rows, 8 * i + 1 : 8 * i + 2]) for i in range(3)])
        rs2_src[per * chunk : per * chunk + per] = latent.astype(BF16).reshape(per, 16, LAT)
        rs2_stat_src[per * chunk : per * chunk + per] = lines(peak, total)
        for slot in range(per * chunk, per * chunk + per):
            home(slot, place(x, 3 - y, (z + RELATIVE[slot]) % NZ, c))
    for copy in zs_copies:
        copy.wait_recv()
    peak, total, latent = merge(
        [part[y_hi, 1 - x_hi, 16 * SLOT[0] :]] + [zs[slot] for slot in range(NZ - 1)],
        [from_line(zs_stat_src[1 - x_hi, SLOT[0]])] + [from_line(zs_stat[slot]) for slot in range(NZ - 1)])
    rs2_src[NZ] = latent.astype(BF16)
    rs2_stat_src[NZ : NZ + 1] = lines(peak, total)
    home(NZ, place((x + 2) % 4, y_hi * 2 + 1 - y_lo, z, c))
    own_v.wait()
    for copy in rs2_copies:
        copy.wait_recv()
    peak, total, latent = merge([rs2[slot] for slot in range(NZ + 1)], [from_line(rs2_stat[slot]) for slot in range(NZ + 1)])
    latent = (latent / total).astype(BF16)
    attended = jnp.zeros((16, VDIM), F32)
    row = lax.broadcasted_iota(jnp.int32, (16, VDIM), 0)
    for h in range(4):
        product = jnp.dot(latent, v_buf[h], preferred_element_type=F32)
        attended = jnp.where(row % 4 == h, product, attended)
    out_src[...] = attended.astype(BF16)
    place_out = mirror_request * 2 + x_hi
    out_copies = []
    for i, (dx, dy) in enumerate(out_moves):
        out_copies.append(send(
            out_src, out.at[place_out], out_send.at[i], out_recv.at[i], out_place(dx, dy)))
    out[place_out] = out_src[...]
    for copy in out_copies:
        copy.wait_recv()
    for copy in copies:
        copy.wait_send()


def body(queries, prompt_latent, pool_latent, value_up, parents, page_lists, lengths):
    vmem = pl.BlockSpec(memory_space=pltpu.VMEM)
    hbm = pl.BlockSpec(memory_space=pltpu.HBM)
    operands = (parents, lengths, page_lists, queries, prompt_latent.swapaxes(1, 2), pool_latent, value_up)
    dma = pltpu.SemaphoreType.DMA
    result = pl.pallas_call(
        kernel,
        out_shape=pltpu.VMEM((8, 16, VDIM), BF16),
        in_specs=[hbm] * 7,
        out_specs=vmem,
        scratch_shapes=[
            pltpu.SMEM((32,), jnp.int32),
            pltpu.SMEM((32,), jnp.int32),
            pltpu.VMEM((32, MAXP), jnp.int32),
            pltpu.VMEM((2, BEAM, 4, WIDTH), BF16),
            pltpu.VMEM((2, 16, 2 * LAT + 128), F32),
            pltpu.VMEM((16, 2 * LAT + 128), BF16),
            pltpu.VMEM((2, NZ, 16, 2 * LAT + 128), BF16),
            pltpu.VMEM((2, PAGE, WIDTH), BF16),
            pltpu.VMEM((2, 4, 2, WIDTH, KEYS), BF16),
            pltpu.VMEM((4, LAT, VDIM), BF16),
            pltpu.VMEM((4 * BEAM, MAXP), jnp.int32),
            pltpu.VMEM((4 * BEAM, MAXP), jnp.int32),
            pltpu.VMEM((4 * BEAM, 8 * KEYS), F32),
            pltpu.VMEM((2 * KEYS, 8 * KEYS), F32),
            pltpu.VMEM((2 * KEYS, 8 * KEYS), BF16),
            pltpu.VMEM((2, 2, KEYS, LAT), BF16),
            pltpu.VMEM((2, 2, 8, KEYS), F32),
            pltpu.VMEM((2, KEYS, LAT), BF16),
            pltpu.VMEM((2, 8, KEYS), F32),
            pltpu.VMEM((NZ - 1, 16, LAT), BF16),
            pltpu.VMEM((2, NZ, 1, KEYS), F32),
            pltpu.VMEM((NZ - 1, 1, KEYS), F32),
            pltpu.VMEM((NZ + 1, 16, LAT), BF16),
            pltpu.VMEM((NZ + 1, 1, KEYS), F32),
            pltpu.VMEM((NZ + 1, 16, LAT), BF16),
            pltpu.VMEM((NZ + 1, 1, KEYS), F32),
            pltpu.VMEM((16, VDIM), BF16),
            dma((8,)), dma((3, 3)), dma((3, 3)), dma((4, 3)), dma((4, 3)), dma, dma, dma((2, NZ)), dma((2, NZ)),
            dma((2, CHUNKS + 1)), dma((2, CHUNKS + 1)), dma((NZ - 1, 2)), dma((NZ - 1, 2)), dma((NZ + 1, 2)), dma((NZ + 1, 2)), dma((7,)), dma((7,)),
        ],
        compiler_params=pltpu.CompilerParams(
            collective_id=0, has_side_effects=True, vmem_limit_bytes=48 * 2**20
        ),
    )(
        *[pltpu.with_memory_space_constraint(operand, pltpu.HBM) for operand in operands]
    )
    return result.reshape(32, 4, VDIM)


def solution(mesh):
    return jax.shard_map(
        body,
        mesh=mesh,
        in_specs=(
            P(None, "head", None),
            P(None, ("seq", "head"), None),
            P(("seq", "head"), None, None),
            P("head", None, None),
            P(),
            P(),
            P(),
        ),
        out_specs=P(None, "head", None),
        check_vma=False,
    )
```
